32 devices in a mesh: batch: 8 (over z, y), heads: 4 (over x, core).
Axes of the slice: x: 2, y: 2, z: 4, core: 2. Of those that a mesh axis runs over, the one named last changes fastest.
Arguments:
- frames_in: bfloat16 [16384, 512], P(('batch', 'heads')), may hold values from -6 to 6
- cotangent: bfloat16 [16384, 512], P(('batch', 'heads')), may hold values from -6 to 6
- lengths: int32 [8], replicated, may hold values from 1568 to 2048, as said below
- sample_weight: int32 [8], replicated, may hold values from 1 to 4
- ffn1_in: bfloat16 [512, 2048], P(('batch', 'heads')), may hold values from -0.25 to 0.25
- ffn1_out: bfloat16 [2048, 512], P(('batch', 'heads')), may hold values from -0.125 to 0.125
- att_proj: bfloat16 [8, 512, 256], P('heads', 'batch'), may hold values from -0.375 to 0.375
- att_out: bfloat16 [8, 64, 512], P('heads', None, 'batch'), may hold values from -1 to 1
- pos_bias: bfloat16 [8, 128], P('heads', 'batch'), may hold values from -3 to 3
- conv_in: bfloat16 [512, 1024], P(('batch', 'heads')), may hold values from -0.25 to 0.25
- dw_kernel: bfloat16 [32, 512], P(None, ('batch', 'heads')), may hold values from -1 to 1
- conv_out: bfloat16 [512, 512], P(('batch', 'heads')), may hold values from -0.25 to 0.25
- ffn2_in: bfloat16 [512, 2048], P(('batch', 'heads')), may hold values from -0.25 to 0.25
- ffn2_out: bfloat16 [2048, 512], P(('batch', 'heads')), may hold values from -0.125 to 0.125
- norm_gain: bfloat16 [6, 512], P(None, ('batch', 'heads')), may hold values from 0.5 to 1.5
- norm_bias: bfloat16 [6, 512], P(None, ('batch', 'heads')), may hold values from -1.25 to 1.25
Outputs:
- layer_out: bfloat16 [16384, 512], P(('batch', 'heads'))
- frames_grad: bfloat16 [16384, 512], P(('batch', 'heads'))
- ffn1_in_grad: float32 [512, 2048], P(('batch', 'heads'))
- ffn1_out_grad: float32 [2048, 512], P(('batch', 'heads'))
- att_proj_grad: float32 [8, 512, 256], P('heads', 'batch')
- att_out_grad: float32 [8, 64, 512], P('heads', None, 'batch')
- pos_bias_grad: float32 [8, 128], P('heads', 'batch')
- conv_in_grad: float32 [512, 1024], P(('batch', 'heads'))
- dw_kernel_grad: float32 [32, 512], P(None, ('batch', 'heads'))
- conv_out_grad: float32 [512, 512], P(('batch', 'heads'))
- ffn2_in_grad: float32 [512, 2048], P(('batch', 'heads'))
- ffn2_out_grad: float32 [2048, 512], P(('batch', 'heads'))
- norm_gain_grad: float32 [6, 512], P(None, ('batch', 'heads'))
- norm_bias_grad: float32 [6, 512], P(None, ('batch', 'heads'))
The draws below stay inside these ranges and needn't reach their ends.
Inputs may be any that keep to these rules, and one draw needn't show every extreme that they name: `lengths`: utterance u fills frame slots u * 2048 onward up to its length; one utterance fills all its slots.
All inputs are finite; a program needn't handle non-finite values.
Results may differ from the reference program's by a relative error of at most 0.025.
Values may be sent and summed in bfloat16 or wider, within the bound.
No kernel may reach another device: no remote copies, remote signals or barrier semaphores. Data moves between devices by JAX's collectives and lax.ppermute only.
A program may use at most 192 MiB of HBM per device.

```python
import math
from functools import partial
import jax
import jax.numpy as jnp
from jax import lax

D = 512
FF = 2048
H = 8
DH = 64
K = 32
TOK_DEV = 512
LEN = 2048
UTTS = 8
FRAMES = 16384


def draw_lengths(key, part):
    first_key = jax.random.fold_in(key, 11)
    second_key = jax.random.fold_in(key, 12)
    least = LEN - TOK_DEV + K
    values = jax.random.randint(first_key, (UTTS,), least, LEN + 1)
    chosen = jax.random.randint(second_key, (), 0, UTTS)
    return jnp.where(jnp.arange(UTTS, dtype=jnp.int32) == chosen, LEN, values).astype(jnp.int32)


def with_ends(entries, own_key, low, largest):
    longest = entries.shape.index(max(entries.shape))
    spots = []
    for shift in (0, 1):
        where = [jax.random.randint(jax.random.fold_in(own_key, axis), (), 0, length) for axis, length in enumerate(entries.shape)]
        where[longest] = (where[longest] + shift) % entries.shape[longest]
        spots.append(tuple(where))
    return entries.at[spots[0]].set(low).at[spots[1]].set(largest)


def block_scale(own_key, dims, pieces, smallest, high):
    level = 1.0
    for axis_at, parts in pieces:
        heights = jax.random.uniform(jax.random.fold_in(jax.random.fold_in(own_key, 6), axis_at), (parts,), jnp.float32, smallest / len(pieces), high / len(pieces))
        level = level * jnp.repeat(jnp.exp(heights), dims[axis_at] // parts).reshape((-1,) + (1,) * (len(dims) - 1 - axis_at))
    return level


def bell_draw(own_key, extent, width, bound, shards=(), kind=jnp.bfloat16):
    entries = jax.random.normal(own_key, extent, jnp.float32) * width
    if len(shards) > 0:
        entries = block_scale(own_key, extent, shards, -0.22, 0.18) * entries
    return jnp.clip(entries, min=-bound, max=bound).astype(kind)


def setup_inputs(seed: int = 0) -> dict:
    splits = jax.random.split(jax.random.key(seed), 17)
    frames_in = bell_draw(splits[0], (FRAMES, D), 1.0, 6.0, ((0, 32),))
    cotangent = bell_draw(splits[1], (FRAMES, D), 1.0, 6.0, ((0, 32),))
    lengths = draw_lengths(jax.random.fold_in(splits[16], 71), 0)
    sample_weight = with_ends(jax.random.randint(splits[3], (UTTS,), 1, 5), jax.random.fold_in(splits[3], 1), 1, 4).astype(jnp.int32)
    ffn1_in = bell_draw(splits[4], (D, FF), D ** -0.5, 0.25, ((0, 32),))
    ffn1_out = bell_draw(splits[5], (FF, D), FF ** -0.5, 0.125, ((0, 32),))
    att_proj = bell_draw(splits[6], (H, D, 4 * DH), (D // 2) ** -0.5, 0.375, ((0, 4), (1, 8)))
    att_out = bell_draw(splits[7], (H, DH, D), (D // 16) ** -0.5, 1.0, ((0, 4), (2, 8)))
    pos_bias = bell_draw(splits[8], (H, 2 * DH), 0.5, 3.0, ((0, 4), (1, 8)))
    conv_in = bell_draw(splits[9], (D, 2 * D), D ** -0.5, 0.25, ((0, 32),))
    dw_kernel = bell_draw(splits[10], (K, D), K ** -0.5, 1.0, ((1, 32),))
    conv_out = bell_draw(splits[11], (D, D), D ** -0.5, 0.25, ((0, 32),))
    ffn2_in = bell_draw(splits[12], (D, FF), D ** -0.5, 0.25, ((0, 32),))
    ffn2_out = bell_draw(splits[13], (FF, D), FF ** -0.5, 0.125, ((0, 32),))
    norm_gain = jnp.clip(1.0 + 0.1 * jax.random.normal(splits[14], (6, D), jnp.float32), 0.5, 1.5).astype(jnp.bfloat16)
    norm_bias = bell_draw(splits[15], (6, D), 0.2, 1.25, ((1, 32),))
    return dict(frames_in=frames_in, cotangent=cotangent, lengths=lengths, sample_weight=sample_weight, ffn1_in=ffn1_in, ffn1_out=ffn1_out, att_proj=att_proj, att_out=att_out, pos_bias=pos_bias, conv_in=conv_in, dw_kernel=dw_kernel, conv_out=conv_out, ffn2_in=ffn2_in, ffn2_out=ffn2_out, norm_gain=norm_gain, norm_bias=norm_bias)


@jax.custom_vjp
def low(v):
    return lax.optimization_barrier(v.astype(jnp.bfloat16)).astype(jnp.float32)

@jax.custom_vjp
def low_back(v):
    return v

def low_keep(v):
    return (low(v), None)

def low_pass(kept, grad):
    return (grad,)

def back_keep(v):
    return (v, None)

def back_low(kept, grad):
    return (low(grad),)
low.defvjp(low_keep, low_pass)
low_back.defvjp(back_keep, back_low)
epsilon = 1e-05
highest = lax.Precision.HIGHEST

def product(left_op, right_op):
    return jnp.dot(left_op, right_op, precision=highest)

def layer_norm(source, gain_row, bias_row):
    center = source - lax.optimization_barrier(jnp.mean(source, axis=-1, keepdims=True))
    spread = lax.optimization_barrier(jnp.mean(center * center, axis=-1, keepdims=True))
    return center * lax.rsqrt(spread + epsilon) * gain_row + bias_row

def sinusoid(row_total, col_total):
    distance = (jnp.arange(row_total, dtype=jnp.int32) - row_total // 2).astype(jnp.float32)
    half_index = jnp.arange(col_total // 2, dtype=jnp.int32).astype(jnp.float32)
    frequency = jnp.exp(half_index * (-2.0 * math.log(10000.0) / col_total))
    phase = distance[:, None] * frequency[None, :]
    return jnp.stack([jnp.sin(phase), jnp.cos(phase)], axis=-1).reshape(row_total, col_total)

def feed_forward(source, w_in, w_out, gain_row, bias_row):
    normed = low(layer_norm(source, gain_row, bias_row))
    hidden = low_back(product(normed, w_in))
    active = low(jax.nn.silu(hidden))
    return source + 0.5 * low_back(product(active, w_out))

def utterance_attention(pos_table, operands):
    q_content, q_position, key_low, value_low, valid_keys = operands
    content = jnp.einsum('hie,hje->hij', q_content, key_low, precision=highest)
    shifted = low_back(jnp.einsum('hie,hre->hir', q_position, pos_table, precision=highest))
    step_ids = jnp.arange(LEN, dtype=jnp.int32)
    rel_index = step_ids[None, :] - step_ids[:, None] + (LEN - 1)
    rel_index = jnp.broadcast_to(rel_index[None], (H, LEN, LEN))
    raw_scores = low_back(content + jnp.take_along_axis(shifted, rel_index, axis=2))
    scores = jnp.where(valid_keys[None, None, :] > 0, raw_scores * DH ** (-0.5), -1e+30)
    weights = jax.nn.softmax(scores, axis=-1)
    mixed_out = jnp.einsum('hij,hje->hie', low(weights), value_low, precision=highest)
    return low(low_back(mixed_out))

def attention(source, proj_w, out_w, pos_w, gain_row, bias_row, valid_mask):
    normed = low(layer_norm(source, gain_row, bias_row))
    projected = jnp.einsum('fd,hde->hfe', normed, proj_w[:, :, :3 * DH], precision=highest)
    query_full = low_back(projected[:, :, :DH])
    key_low = low(low_back(projected[:, :, DH:2 * DH]))
    value_low = low(low_back(projected[:, :, 2 * DH:]))
    q_content = low(query_full + pos_w[:, None, :DH])
    q_position = low(query_full + pos_w[:, None, DH:])
    pos_source = low(sinusoid(2 * LEN - 1, D))
    pos_table = low(jnp.einsum('rd,hde->hre', pos_source, proj_w[:, :, 3 * DH:], precision=highest))

    def per_utter(array):
        return array.reshape(H, UTTS, LEN, DH).transpose(1, 0, 2, 3)
    mixed_out = lax.map(jax.checkpoint(partial(utterance_attention, pos_table)), (per_utter(q_content), per_utter(q_position), per_utter(key_low), per_utter(value_low), valid_mask))
    mixed_out = mixed_out.transpose(1, 0, 2, 3).reshape(H, FRAMES, DH)
    return low_back(jnp.einsum('hfe,hed->fd', mixed_out, out_w, precision=highest))

def convolve(source, conv_a, kernel_w, conv_b, gain_row, bias_row, bn_gain, bn_bias, row_valid, valid_total):
    normed = low(layer_norm(source, gain_row, bias_row))
    gated_pair = low_back(product(normed, conv_a))
    glu_low = low(gated_pair[:, :D] * jax.nn.sigmoid(gated_pair[:, D:]) * row_valid)
    padded = jnp.pad(glu_low.reshape(UTTS, LEN, D), ((0, 0), (K // 2 - 1, K // 2), (0, 0)))
    depth_out = jnp.zeros((UTTS, LEN, D), jnp.float32)
    for tap_index in range(K):
        depth_out = depth_out + padded[:, tap_index:tap_index + LEN, :] * kernel_w[tap_index]
    depth_out = low_back(depth_out.reshape(FRAMES, D))
    first_moment = lax.optimization_barrier(jnp.sum(depth_out * row_valid, axis=0))
    squares = lax.optimization_barrier(jnp.sum(depth_out * depth_out * row_valid, axis=0))
    mean_bn = first_moment / valid_total
    var_bn = squares / valid_total - mean_bn * mean_bn
    normed_bn = (depth_out - mean_bn) * lax.rsqrt(var_bn + epsilon) * bn_gain + bn_bias
    active = low(jax.nn.silu(normed_bn))
    return low_back(product(active, conv_b))

def reference(frames_in, cotangent, lengths, sample_weight, ffn1_in, ffn1_out, att_proj, att_out, pos_bias, conv_in, dw_kernel, conv_out, ffn2_in, ffn2_out, norm_gain, norm_bias):
    step_ids = jnp.arange(LEN, dtype=jnp.int32)
    valid_mask = (step_ids[None, :] < lengths[:, None]).astype(jnp.float32)
    row_valid = valid_mask.reshape(FRAMES, 1)
    valid_total = jnp.sum(lengths).astype(jnp.float32)
    seed_scale = (sample_weight.astype(jnp.float32) * 0.25)[:, None] * valid_mask

    def forward(frames, ffn1_a, ffn1_b, proj_w, out_w, pos_w, conv_a, kernel_w, conv_b, ffn2_a, ffn2_b, gain_rows, biases):
        after_ffn1 = feed_forward(frames, ffn1_a, ffn1_b, gain_rows[0], biases[0])
        after_att = after_ffn1 + attention(after_ffn1, proj_w, out_w, pos_w, gain_rows[1], biases[1], valid_mask)
        after_conv = after_att + convolve(after_att, conv_a, kernel_w, conv_b, gain_rows[2], biases[2], gain_rows[5], biases[5], row_valid, valid_total)
        after_ffn2 = feed_forward(after_conv, ffn2_a, ffn2_b, gain_rows[3], biases[3])
        return layer_norm(after_ffn2, gain_rows[4], biases[4])
    inputs = tuple((array.astype(jnp.float32) for array in (frames_in, ffn1_in, ffn1_out, att_proj, att_out, pos_bias, conv_in, dw_kernel, conv_out, ffn2_in, ffn2_out, norm_gain, norm_bias)))
    layer_out, pull = jax.vjp(forward, *inputs)
    seed_rows = cotangent.astype(jnp.float32) * seed_scale.reshape(FRAMES, 1)
    gradients = pull(seed_rows)
    return (layer_out.astype(jnp.bfloat16), gradients[0].astype(jnp.bfloat16), gradients[1], gradients[2], gradients[3], gradients[4], gradients[5], gradients[6], gradients[7], gradients[8], gradients[9], gradients[10], gradients[11], gradients[12])
```

```python
import math

import jax
import jax.numpy as jnp
from jax import lax
from jax.experimental import pallas as pl
from jax.experimental.pallas import tpu as pltpu
from jax.sharding import PartitionSpec as P

epsilon = 1e-05
BF = jnp.bfloat16
F32 = jnp.float32
BOTH = ("batch", "heads")
CHUNK = 128


def swap(source, axis, mask):
    count = lax.axis_size(axis)
    return lax.ppermute(source, axis, [(i, i ^ mask) for i in range(count)])


def at_index(source, index, axis=0):
    return lax.dynamic_index_in_dim(source, index, axis, keepdims=False)


def all_sum(source):
    for axis in ("heads", "batch"):
        count = lax.axis_size(axis)
        low = 1
        while low < count:
            high = min(count, low * 8)
            heard = [swap(source, axis, m) for m in range(low, high, low)]
            for piece in heard:
                source = source + piece
            low = high
    return source


def halo(cells, width):
    count = lax.axis_size("heads")
    ends = count - 1
    rows = cells.shape[0]
    before = lax.ppermute(cells[rows - width :], "heads", [(i, i + 1) for i in range(ends)])
    after = lax.ppermute(cells[:width], "heads", [(i + 1, i) for i in range(ends)])
    return jnp.concatenate([before, cells, after], axis=0)


DIMS = {"y": ("batch", 1), "x": ("heads", 2), "c": ("heads", 1)}
PLACE = {"y": 0, "x": 1, "c": 2}


def gather_pieces(shard, order):
    depth = lax.axis_size("batch") // 2
    z_at = lax.axis_index("batch") // 2
    held = [shard] + [swap(shard, "batch", 2 * k) for k in range(1, depth)]
    bit = 1
    while bit < depth:
        flip = (z_at & bit) != 0
        held = [jnp.where(flip, held[j ^ bit], held[j]) for j in range(depth)]
        bit *= 2
    pieces = {(0, 0, 0): jnp.stack(held)}
    for dim in order:
        axis, mask = DIMS[dim]
        for key in list(pieces):
            new_key = list(key)
            new_key[PLACE[dim]] ^= 1
            pieces[tuple(new_key)] = swap(pieces[key], axis, mask)
    return pieces


def assemble(piece_sets, outs, plan):
    keys = [sorted(s) for s in piece_sets]
    arrays = [s[k] for s, ks in zip(piece_sets, keys) for k in ks]
    total = [0]

    def kernel(*refs):
        sources = refs[: len(arrays)]
        targets = refs[len(arrays) : len(arrays) + len(outs)]
        sems = refs[-1]
        batch_at = lax.axis_index("batch")
        heads_at = lax.axis_index("heads")
        at = (lax.rem(batch_at, 2), lax.div(heads_at, 2), lax.rem(heads_at, 2))
        copies = []
        position = 0
        for set_at, ks in enumerate(keys):
            for key in ks:
                y, x, c = (1 - a if flip else a for a, flip in zip(at, key))
                for source, target in plan(set_at, sources[position], targets, y, x, c):
                    copy = pltpu.make_async_copy(source, target, sems.at[len(copies)])
                    copy.start()
                    copies.append(copy)
                position += 1
        for copy in copies:
            copy.wait()

    anywhere = pl.BlockSpec(memory_space=pl.ANY)
    return pl.pallas_call(
        kernel,
        in_specs=[anywhere] * len(arrays),
        out_specs=[anywhere] * len(outs),
        out_shape=[jax.ShapeDtypeStruct(shape, BF) for shape in outs],
        scratch_shapes=[pltpu.SemaphoreType.DMA((64,))],
        name="assemble",
    )(*arrays)


def scatter_sum(blocks, order):
    batch_at = lax.axis_index("batch")
    heads_at = lax.axis_index("heads")
    kind = blocks.dtype
    at = {"y": lax.rem(batch_at, 2), "x": lax.div(heads_at, 2), "c": lax.rem(heads_at, 2)}
    dims = ["c", "z", "y", "x"]
    for dim in order:
        axis, mask = DIMS[dim]
        where = dims.index(dim)
        heard = swap(at_index(blocks, 1 - at[dim], where), axis, mask)
        kept = at_index(blocks, at[dim], where)
        blocks = (kept.astype(F32) + heard.astype(F32)).astype(kind)
        dims.pop(where)
    depth = blocks.shape[0]
    z_at = lax.div(batch_at, 2)
    total = at_index(blocks, z_at).astype(F32)
    for k in range(1, depth):
        total = total + swap(at_index(blocks, z_at ^ k), "batch", 2 * k).astype(F32)
    return total


def layer_norm(source, gain_row, bias_row):
    center = source - jnp.mean(source, axis=-1, keepdims=True)
    spread = jnp.mean(center * center, axis=-1, keepdims=True)
    return center * lax.rsqrt(spread + epsilon) * gain_row + bias_row


def matmul(left_op, right_op):
    return jnp.dot(left_op, right_op, preferred_element_type=F32)


def inner_rows(left_op, right_op):
    return lax.dot_general(
        left_op, right_op, (((0,), (0,)), ((), ())), preferred_element_type=F32
    )


def outer_cols(left_op, right_op):
    return lax.dot_general(
        left_op, right_op, (((1,), (1,)), ((), ())), preferred_element_type=F32
    )


def ffn_forward(source, w_in, w_out, gain_row, bias_row):
    normed = layer_norm(source, gain_row, bias_row).astype(BF)
    hidden = matmul(normed, w_in)
    active = jax.nn.silu(hidden).astype(BF)
    return (source + 0.5 * matmul(active, w_out), (normed, hidden, active))


def ffn_backward(upstream, saved, source, w_in, w_out, gain_row, bias_row):
    normed, hidden, active = saved
    branch = (0.5 * upstream).astype(BF)
    grad_out = inner_rows(active, branch).astype(BF)
    _, silu_pull = jax.vjp(jax.nn.silu, hidden)
    grad_hidden = silu_pull(outer_cols(branch, w_out))[0].astype(BF)
    grad_in = inner_rows(normed, grad_hidden).astype(BF)
    _, norm_pull = jax.vjp(layer_norm, source, gain_row, bias_row)
    grad_source, grad_gain, grad_bias = norm_pull(outer_cols(grad_hidden, w_in))
    return (upstream + grad_source, grad_in, grad_out, grad_gain, grad_bias)


def batch_norm_act(depth_in, mean_in, var_in, gain_in, bias_in):
    return jax.nn.silu((depth_in - mean_in) * lax.rsqrt(var_in + epsilon) * gain_in + bias_in)


def att_fwd_kernel(
    mask_ref, keys_ref, own_ref, tw_ref, pos_ref, pb_ref, cs_ref, et_ref, w_ref, o_ref, kv_ref, q_ref
):
    rows = own_ref.shape[0]
    half = cs_ref.shape[2]
    tw = tw_ref[0]
    kv = matmul(keys_ref[...], tw[:, 128:384]).astype(BF)
    kv_ref[0] = kv
    query = matmul(own_ref[...], tw[:, :128])
    qc = (query + pb_ref[0, 0:1, :]).astype(BF)
    qp = (query + pb_ref[0, 1:2, :]).astype(BF)
    q_ref[0, 0] = qc
    q_ref[0, 1] = qp
    key, value = kv[:, :128], kv[:, 128:]
    first = lax.broadcasted_iota(jnp.int32, (rows, 128), 1) < 64
    zero = jnp.zeros((rows, 128), BF)
    mask = mask_ref[...]
    cos, sin = cs_ref[0], cs_ref[1]
    outs = []
    for head in range(2):
        qc_h = (jnp.where(first, qc, zero) if head == 0 else jnp.where(first, zero, qc)) * BF(0.125)
        qp_h = jnp.where(first, qp, zero) if head == 0 else jnp.where(first, zero, qp)
        turned = outer_cols(qp_h, pos_ref[0]) * 0.125
        us, uc = turned[:, :half], turned[:, half:]
        qr = jnp.concatenate(
            [(us * cos + uc * sin).astype(BF), (uc * cos - us * sin).astype(BF)], axis=1
        )
        parts = []
        for r in range(0, rows, CHUNK):
            scores = matmul(qr[r : r + CHUNK], et_ref[...])
            scores = scores + outer_cols(qc_h[r : r + CHUNK], key) + mask
            top = jnp.max(scores, axis=1, keepdims=True)
            grown = jnp.exp(scores - top)
            total = jnp.sum(grown, axis=1, keepdims=True)
            weights = (grown * (1.0 / total)).astype(BF)
            w_ref[0, head, r : r + CHUNK, :] = weights
            parts.append(matmul(weights, value))
        outs.append(jnp.concatenate(parts, axis=0))
    o_ref[0] = jnp.where(first, outs[0], outs[1])


def whole_block(array):
    return pl.BlockSpec(array.shape, lambda h: (0,) * array.ndim)


def pair_block(array):
    return pl.BlockSpec((1,) + array.shape[1:], lambda h: (h,) + (0,) * (array.ndim - 1))


def att_forward(mask, keys, own, tw, pos, pb, cs, et):
    pairs, rows, count = tw.shape[0], own.shape[0], keys.shape[0]
    outs = [
        jax.ShapeDtypeStruct((pairs, 2, rows, count), BF),
        jax.ShapeDtypeStruct((pairs, rows, 128), F32),
        jax.ShapeDtypeStruct((pairs, count, 256), BF),
        jax.ShapeDtypeStruct((pairs, 2, rows, 128), BF),
    ]
    return pl.pallas_call(
        att_fwd_kernel,
        grid=(pairs,),
        in_specs=[
            whole_block(mask),
            whole_block(keys),
            whole_block(own),
            pair_block(tw),
            pair_block(pos),
            pair_block(pb),
            whole_block(cs),
            whole_block(et),
        ],
        out_specs=[pair_block(a) for a in outs],
        out_shape=outs,
        compiler_params=pltpu.CompilerParams(vmem_limit_bytes=56 * 2**20),
        cost_estimate=pl.CostEstimate(flops=40 * 10**9, bytes_accessed=30 * 2**20, transcendentals=0),
        name="att_fwd",
    )(mask, keys, own, tw, pos, pb, cs, et)


def att_bwd_kernel(
    do_ref, o_ref, w_ref, kv_ref, q_ref, pos_ref, cs_ref, e_ref, dq_ref, dkv_ref, dpos_ref, db_ref, dr_ref
):
    rows = do_ref.shape[1]
    half = cs_ref.shape[2]
    do = do_ref[0]
    key, value = kv_ref[0, :, :128], kv_ref[0, :, 128:]
    first = lax.broadcasted_iota(jnp.int32, (rows, 128), 1) < 64
    zero = jnp.zeros((rows, 128), BF)
    zero_f = jnp.zeros((rows, 128), F32)
    inner = do.astype(F32) * o_ref[0]
    do_t = do.astype(F32).T.astype(BF)
    qc_t = (q_ref[0, 0].astype(F32) * 0.125).T.astype(BF)
    qp_t = q_ref[0, 1].astype(F32).T.astype(BF)
    cos, sin = cs_ref[0], cs_ref[1]
    dqcs, dqps = [], []
    for head in range(2):
        mine = slice(head * 64, head * 64 + 64)
        do_h = jnp.where(first, do, zero) if head == 0 else jnp.where(first, zero, do)
        inner_h = jnp.where(first, inner, zero_f) if head == 0 else jnp.where(first, zero_f, inner)
        inner_sum = jnp.sum(inner_h, axis=1, keepdims=True)
        for r in range(0, rows, CHUNK):
            dw = outer_cols(do_h[r : r + CHUNK], value)
            weights = w_ref[0, head, r : r + CHUNK, :].astype(F32)
            dr_ref[r : r + CHUNK, :] = (weights * (dw - inner_sum[r : r + CHUNK])).astype(BF)
        dr = dr_ref[...]
        turned = matmul(dr, e_ref[...]) * 0.125
        dqcs.append(matmul(dr, key) * 0.125)
        dkv_ref[0, 0, mine, :] = matmul(qc_t[mine], dr).astype(BF)
        dkv_ref[0, 1, mine, :] = matmul(do_t[mine], w_ref[0, head]).astype(BF)
        gs, gc = turned[:, :half], turned[:, half:]
        du = jnp.concatenate(
            [(gs * cos - gc * sin).astype(BF), (gs * sin + gc * cos).astype(BF)], axis=1
        )
        dqps.append(matmul(du, pos_ref[0]))
        dpos_ref[0, mine, :] = matmul(qp_t[mine], du)
    dqc = jnp.where(first, dqcs[0], dqcs[1])
    dqp = jnp.where(first, dqps[0], dqps[1])
    dq_ref[0] = (dqc + dqp).astype(BF)
    db_ref[0, 0:1, :] = jnp.sum(dqc, axis=0, keepdims=True)
    db_ref[0, 1:2, :] = jnp.sum(dqp, axis=0, keepdims=True)


def att_backward(do, o, weights, kv, q, pos, cs, e):
    pairs, rows, count, width = do.shape[0], do.shape[1], kv.shape[1], e.shape[1]
    outs = [
        jax.ShapeDtypeStruct((pairs, rows, 128), BF),
        jax.ShapeDtypeStruct((pairs, 2, 128, count), BF),
        jax.ShapeDtypeStruct((pairs, 128, width), F32),
        jax.ShapeDtypeStruct((pairs, 2, 128), F32),
    ]
    return pl.pallas_call(
        att_bwd_kernel,
        grid=(pairs,),
        in_specs=[
            pair_block(do),
            pair_block(o),
            pair_block(weights),
            pair_block(kv),
            pair_block(q),
            pair_block(pos),
            whole_block(cs),
            whole_block(e),
        ],
        out_specs=[pair_block(a) for a in outs],
        out_shape=outs,
        scratch_shapes=[pltpu.VMEM((rows, count), BF)],
        compiler_params=pltpu.CompilerParams(vmem_limit_bytes=56 * 2**20),
        cost_estimate=pl.CostEstimate(flops=30 * 10**9, bytes_accessed=30 * 2**20, transcendentals=0),
        name="att_bwd",
    )(do, o, weights, kv, q, pos, cs, e)


def small_shard(dw_kernel, norm_gain, norm_bias, pos_bias):
    stacked = jnp.concatenate([dw_kernel, norm_gain, norm_bias, pos_bias], axis=0)
    return jnp.pad(stacked.T, ((0, 0), (0, 128 - stacked.shape[0])))


def att_shard(att_proj, att_out):
    two, rows, four = att_proj.shape
    head_dim = four // 4
    parts = att_proj.transpose(1, 2, 0).reshape(rows, 4, head_dim, two).transpose(0, 1, 3, 2)
    parts = parts.reshape(rows, 4, two * head_dim)
    out_t = att_out.transpose(2, 0, 1).reshape(rows, two * head_dim)
    turned = parts[:, 3].reshape(rows // 2, 2, two * head_dim).transpose(1, 0, 2)
    turned = turned.reshape(rows, two * head_dim)
    return jnp.concatenate([parts[:, 0], parts[:, 1], parts[:, 2], out_t, turned], axis=1)


def by_columns(shard):
    rows, columns = shard.shape
    return shard.reshape(rows, columns // 512, 512).transpose(1, 0, 2).reshape(-1, 512)


def gather_fast(ffn1_in, ffn1_out, att_proj, att_out, small, conv_in, conv_out, ffn2_in, ffn2_out):
    depth = lax.axis_size("batch") // 2
    width = 16 * 8 * depth
    hidden = 64 * 8 * depth
    small_rows = jnp.pad(small, ((0, 0), (0, 512 - 128)))
    first_a = gather_pieces(jnp.concatenate([by_columns(ffn1_in), small_rows]), "yxc")
    first_b = gather_pieces(ffn1_out, "xyc")
    second = gather_pieces(att_shard(att_proj, att_out), "yxc")
    third_a = gather_pieces(jnp.concatenate([by_columns(ffn2_in), by_columns(conv_in)]), "yxc")
    third_b = gather_pieces(jnp.concatenate([ffn2_out, conv_out]), "xyc")

    def first_plan(which, source, outs, y, x, c):
        block = y * 4 + x * 2 + c
        if which == 0:
            for column in range(4):
                yield (
                    source.at[:, pl.ds(16 * column, 16), :],
                    outs[0].at[:, block, :, pl.ds(512 * column, 512)],
                )
            yield source.at[:, pl.ds(64, 16), pl.ds(0, 128)], outs[2].at[:, block]
        else:
            yield source, outs[1].at[:, block]

    def second_plan(which, source, outs, y, x, c):
        pair = x * 2 + c
        yield source.at[:, :, pl.ds(0, 512)], outs[0].at[pair, :, y]
        for part in range(2):
            yield (
                source.at[:, pl.ds(32 * part, 32), pl.ds(512, 128)],
                outs[1].at[pair, part, :, y],
            )

    def third_plan(which, source, outs, y, x, c):
        block = y * 4 + x * 2 + c
        if which == 0:
            for column in range(4):
                yield (
                    source.at[:, pl.ds(16 * column, 16), :],
                    outs[0].at[:, block, :, pl.ds(512 * column, 512)],
                )
            for column in range(2):
                yield (
                    source.at[:, pl.ds(64 + 16 * column, 16), :],
                    outs[2].at[:, block, :, pl.ds(512 * column, 512)],
                )
        else:
            yield source.at[:, pl.ds(0, 64), :], outs[1].at[:, block]
            yield source.at[:, pl.ds(64, 16), :], outs[3].at[:, block]

    ffn1_a, ffn1_b, small_all = assemble(
        [first_a, first_b],
        [(depth, 8, 16, 2048), (depth, 8, 64, 512), (depth, 8, 16, 128)],
        first_plan,
    )
    tw, pos = assemble(
        [second], [(4, depth, 2, 64, 512), (4, 2, depth, 2, 32, 128)], second_plan
    )
    ffn2_a, ffn2_b, conv_a, conv_b = assemble(
        [third_a, third_b],
        [(depth, 8, 16, 2048), (depth, 8, 64, 512), (depth, 8, 16, 1024), (depth, 8, 16, 512)],
        third_plan,
    )
    return (
        ffn1_a.reshape(width, 2048),
        ffn1_b.reshape(hidden, 512),
        small_all.reshape(width, 128),
        tw.reshape(4, width, 512),
        pos.reshape(4, width, 128),
        ffn2_a.reshape(width, 2048),
        ffn2_b.reshape(hidden, 512),
        conv_a.reshape(width, 1024),
        conv_b.reshape(width, 512),
    )


def gather_plain(ffn1_in, ffn1_out, att_proj, att_out, small, conv_in, conv_out, ffn2_in, ffn2_out):
    def rows_of(shard):
        return lax.all_gather(shard, BOTH, axis=0, tiled=True)

    pairs = lax.axis_size("heads")
    shard = att_shard(att_proj, att_out)
    rows = shard.shape[0]
    att_all = lax.all_gather(lax.all_gather(shard, "batch", axis=0), "heads", axis=0)
    tw = att_all[..., :512].reshape(pairs, -1, 512)
    pos = att_all[..., 512:].reshape(pairs, -1, 2, rows // 2, 128).transpose(0, 2, 1, 3, 4)
    return (
        rows_of(ffn1_in),
        rows_of(ffn1_out),
        rows_of(small),
        tw,
        pos.reshape(pairs, -1, 128),
        rows_of(ffn2_in),
        rows_of(ffn2_out),
        rows_of(conv_in),
        rows_of(conv_out),
    )


def rows_to_blocks(grad, depth):
    total, columns = grad.shape
    rows = total // (8 * depth)
    parts = columns // 512
    split = grad.reshape(depth, 2, 2, 2, rows, parts, 512)
    return split.transpose(3, 0, 1, 2, 5, 4, 6).reshape(2, depth, 2, 2, parts * rows, 512)


def blocks_to_rows(block, parts):
    rows = block.shape[0] // parts
    return block.reshape(parts, rows, 512).transpose(1, 0, 2).reshape(rows, parts * 512)


def att_blocks(grad, count):
    pairs, width, columns = grad.shape
    split = grad.reshape(2, 2, count // 2, 2, width // count, columns)
    return split.transpose(1, 2, 3, 0, 4, 5)


def local(
    frames_in,
    cotangent,
    lengths,
    sample_weight,
    ffn1_in,
    ffn1_out,
    att_proj,
    att_out,
    pos_bias,
    conv_in,
    dw_kernel,
    conv_out,
    ffn2_in,
    ffn2_out,
    norm_gain,
    norm_bias,
):
    row_count, model_width = frames_in.shape
    pairs = lax.axis_size("heads")
    batches = lax.axis_size("batch")
    head_index = lax.axis_index("heads")
    batch_index = lax.axis_index("batch")
    fast = ffn1_in.shape[0] == 16 and batches in (2, 4, 8) and pairs == 4
    kernel_len = dw_kernel.shape[0]
    half_kernel = kernel_len // 2
    head_dim = att_out.shape[1]
    channels = ffn1_in.shape[0]

    utter_ids = jnp.arange(lengths.shape[0], dtype=jnp.int32)
    own_length = jnp.sum(jnp.where(utter_ids == batch_index, lengths, 0))
    own_weight = jnp.sum(jnp.where(utter_ids == batch_index, sample_weight, 0)).astype(F32) * 0.25
    positions = head_index * row_count + jnp.arange(row_count, dtype=jnp.int32)
    row_valid = (positions < own_length).astype(F32)[:, None]
    total_valid = jnp.sum(lengths).astype(F32)

    small = small_shard(dw_kernel, norm_gain, norm_bias, pos_bias)
    gather = gather_fast if fast else gather_plain
    ffn1_a, ffn1_b, small_all, tw, pos_w, ffn2_a, ffn2_b, conv_a, conv_b = gather(
        ffn1_in, ffn1_out, att_proj, att_out, small, conv_in, conv_out, ffn2_in, ffn2_out
    )
    small_cols = small_all.T.astype(F32)
    depth_f = small_cols[:kernel_len]
    gains = small_cols[kernel_len : kernel_len + 6]
    biases = small_cols[kernel_len + 6 : kernel_len + 12]
    pos_b = small_cols[kernel_len + 12 : kernel_len + 14]
    pos_b = pos_b.reshape(2, batches, pairs, channels).transpose(2, 0, 1, 3)
    pos_b = pos_b.reshape(pairs, 2, 2, head_dim).transpose(0, 2, 1, 3).reshape(pairs, 2, 2 * head_dim)

    freq = jnp.exp(
        jnp.arange(model_width // 2, dtype=jnp.int32).astype(F32)
        * (-2.0 * math.log(10000.0) / model_width)
    )
    steps = row_count // 64
    blocks = jnp.arange(pairs, dtype=jnp.int32) ^ head_index
    coarse = (blocks[:, None] * steps + jnp.arange(steps, dtype=jnp.int32)[None, :]).reshape(-1)
    coarse_phase = (coarse * 64).astype(F32)[:, None] * freq[None, :]
    fine_phase = jnp.arange(64, dtype=jnp.int32).astype(F32)[:, None] * freq[None, :]
    sin_a, cos_a = jnp.sin(coarse_phase)[:, None, :], jnp.cos(coarse_phase)[:, None, :]
    sin_b, cos_b = jnp.sin(fine_phase)[None, :, :], jnp.cos(fine_phase)[None, :, :]
    sin_all = (sin_a * cos_b + cos_a * sin_b).reshape(pairs * row_count, -1)
    cos_all = (cos_a * cos_b - sin_a * sin_b).reshape(pairs * row_count, -1)
    table = jnp.concatenate([sin_all, cos_all], axis=1).astype(BF)
    table_t = table.T
    own_turn = jnp.stack([cos_all[:row_count], sin_all[:row_count]])
    key_positions = (
        blocks[:, None] * row_count + jnp.arange(row_count, dtype=jnp.int32)[None, :]
    ).reshape(1, -1)
    key_mask = jnp.where(key_positions < own_length, 0.0, -1e30).astype(F32)

    source = frames_in.astype(F32)
    after_ffn1, ffn1_saved = ffn_forward(source, ffn1_a, ffn1_b, gains[0], biases[0])
    normed_att = layer_norm(after_ffn1, gains[1], biases[1]).astype(BF)
    across = swap(normed_att, "heads", 2)
    keys_in = jnp.concatenate(
        [normed_att, swap(normed_att, "heads", 1), across, swap(across, "heads", 1)]
    )
    weights, mixed, kv, queries = att_forward(
        key_mask, keys_in, normed_att, tw, pos_w, pos_b, own_turn, table_t
    )
    w_out_t = tw[:, :, 3 * 128 :]
    mixed_low = mixed.astype(BF)
    after_att = after_ffn1 + jnp.einsum(
        "hfe,hde->fd", mixed_low, w_out_t, preferred_element_type=F32
    )
    normed_conv = layer_norm(after_att, gains[2], biases[2]).astype(BF)
    gated_pair = matmul(normed_conv, conv_a)

    def gate_unit(gated_in):
        return gated_in[:, :model_width] * jax.nn.sigmoid(gated_in[:, model_width:]) * row_valid

    glu_low = gate_unit(gated_pair).astype(BF)
    rimmed = halo(glu_low, half_kernel)
    depth_out = jnp.zeros((row_count, model_width), F32)
    for tap_index in range(kernel_len):
        depth_out = (
            depth_out
            + rimmed[tap_index + 1 : tap_index + 1 + row_count].astype(F32) * depth_f[tap_index]
        )
    moments = all_sum(
        jnp.stack(
            [
                jnp.sum(depth_out * row_valid, axis=0),
                jnp.sum(depth_out * depth_out * row_valid, axis=0),
            ]
        )
    )
    mean_bn = moments[0] / total_valid
    var_bn = moments[1] / total_valid - mean_bn * mean_bn
    swish_low = batch_norm_act(depth_out, mean_bn, var_bn, gains[5], biases[5]).astype(BF)
    after_conv = after_att + matmul(swish_low, conv_b)
    after_ffn2, ffn2_saved = ffn_forward(after_conv, ffn2_a, ffn2_b, gains[3], biases[3])
    layer_out = layer_norm(after_ffn2, gains[4], biases[4])
    seed_rows = cotangent.astype(F32) * (own_weight * row_valid)
    _, final_pull = jax.vjp(layer_norm, after_ffn2, gains[4], biases[4])
    upstream, gain_final, bias_final = final_pull(seed_rows)
    upstream, grad_ffn2_a, grad_ffn2_b, gain_ffn2, bias_ffn2 = ffn_backward(
        upstream, ffn2_saved, after_conv, ffn2_a, ffn2_b, gains[3], biases[3]
    )
    branch_low = upstream.astype(BF)
    grad_conv_b = inner_rows(swish_low, branch_low).astype(BF)
    _, norm_act_pull = jax.vjp(batch_norm_act, depth_out, mean_bn, var_bn, gains[5], biases[5])
    grad_depth, grad_mean, grad_var, gain_batch, bias_batch = norm_act_pull(
        outer_cols(branch_low, conv_b)
    )
    grad_mean, grad_var = all_sum(jnp.stack([grad_mean, grad_var]))
    grad_first = (grad_mean - 2.0 * mean_bn * grad_var) / total_valid
    grad_second = grad_var / total_valid
    grad_depth = grad_depth + row_valid * (grad_first + 2.0 * depth_out * grad_second)
    depth_low = grad_depth.astype(BF)
    depth_rim = halo(depth_low, half_kernel)
    depth_grad_f = depth_low.astype(F32)
    grad_glu = jnp.zeros((row_count, model_width), F32)
    kernel_rows = []
    for tap_index in range(kernel_len):
        back_start = kernel_len - 1 - tap_index
        grad_glu = (
            grad_glu
            + depth_rim[back_start : back_start + row_count].astype(F32) * depth_f[tap_index]
        )
        kernel_rows.append(
            jnp.sum(
                rimmed[tap_index + 1 : tap_index + 1 + row_count].astype(F32) * depth_grad_f,
                axis=0,
            )
        )
    grad_kernel = jnp.stack(kernel_rows)
    _, gate_pull = jax.vjp(gate_unit, gated_pair)
    grad_gated = gate_pull(grad_glu)[0].astype(BF)
    grad_conv_a = inner_rows(normed_conv, grad_gated).astype(BF)
    _, conv_norm_pull = jax.vjp(layer_norm, after_att, gains[2], biases[2])
    grad_source, gain_conv, bias_conv = conv_norm_pull(outer_cols(grad_gated, conv_a))
    upstream = upstream + grad_source

    out_grad = upstream.astype(BF)
    grad_mixed = jnp.einsum("fd,hde->hfe", out_grad, w_out_t, preferred_element_type=F32)
    grad_out_t = jnp.einsum("fd,hfe->hde", out_grad, mixed_low, preferred_element_type=F32)
    grad_q, grad_kv, grad_pos, grad_bias = att_backward(
        grad_mixed.astype(BF), mixed, weights, kv, queries, pos_w, own_turn, table
    )
    w_kv = tw[:, :, 128:384].reshape(pairs, model_width, 2, 128)
    grad_keys_in = jnp.einsum("htek,hdte->kd", grad_kv, w_kv, preferred_element_type=F32)
    pieces = [
        grad_keys_in[k * row_count : (k + 1) * row_count].astype(BF) for k in range(pairs)
    ]
    near = swap(jnp.stack([pieces[1], pieces[3]]), "heads", 1).astype(F32)
    far = swap((pieces[2].astype(F32) + near[1]).astype(BF), "heads", 2).astype(F32)
    grad_normed = jnp.einsum("hfe,hde->fd", grad_q, tw[:, :, :128], preferred_element_type=F32)
    grad_normed = grad_normed + grad_keys_in[:row_count] + near[0] + far
    grad_tw = jnp.concatenate(
        [
            jnp.einsum("fd,hfe->hde", normed_att, grad_q, preferred_element_type=F32),
            jnp.einsum("kd,htek->hdte", keys_in, grad_kv, preferred_element_type=F32).reshape(
                pairs, model_width, 256
            ),
            grad_out_t,
        ],
        axis=2,
    ).astype(BF)
    _, att_norm_pull = jax.vjp(layer_norm, after_ffn1, gains[1], biases[1])
    grad_source, gain_att, bias_att = att_norm_pull(grad_normed)
    upstream = upstream + grad_source
    upstream, grad_ffn1_a, grad_ffn1_b, gain_ffn1, bias_ffn1 = ffn_backward(
        upstream, ffn1_saved, source, ffn1_a, ffn1_b, gains[0], biases[0]
    )
    bias_part = grad_bias.reshape(pairs, 2, 2, head_dim).transpose(0, 2, 1, 3)
    bias_part = bias_part.reshape(pairs, 2, batches, channels).transpose(1, 2, 0, 3)
    small_grads = jnp.concatenate(
        [
            grad_kernel,
            jnp.stack([gain_ffn1, gain_att, gain_conv, gain_ffn2, gain_final, gain_batch]),
            jnp.stack([bias_ffn1, bias_att, bias_conv, bias_ffn2, bias_final, bias_batch]),
            bias_part.reshape(2, model_width),
        ]
    )
    small_rows = small_grads.shape[0]
    small_grads = jnp.pad(small_grads, ((0, 128 - small_rows), (0, 0))).T
    grad_pos = grad_pos.transpose(0, 2, 1)
    width = model_width // batches
    grad_pos = grad_pos.reshape(pairs, 2, batches, width // 2, 128).transpose(0, 2, 1, 3, 4)
    grad_pos = grad_pos.reshape(pairs, model_width, 128).astype(BF)
    grad_att = jnp.concatenate([grad_tw, grad_pos], axis=2)
    if fast:
        depth = batches // 2
        sum_a = scatter_sum(
            jnp.concatenate(
                [rows_to_blocks(grad_ffn2_a, depth), rows_to_blocks(grad_conv_a, depth)], axis=4
            ),
            "cxy",
        )
        sum_b = scatter_sum(
            jnp.concatenate(
                [rows_to_blocks(grad_ffn2_b, depth), rows_to_blocks(grad_conv_b, depth)], axis=4
            ),
            "cyx",
        )
        own_ffn2_a, own_conv_a = blocks_to_rows(sum_a[:64], 4), blocks_to_rows(sum_a[64:], 2)
        own_ffn2_b, own_conv_b = sum_b[:64], sum_b[64:]
        own_att = scatter_sum(att_blocks(grad_att, batches), "cxy")
        own_ffn1_a = blocks_to_rows(scatter_sum(rows_to_blocks(grad_ffn1_a, depth), "cxy"), 4)
        own_ffn1_b = scatter_sum(rows_to_blocks(grad_ffn1_b, depth), "cyx")
        small_blocks = small_grads.reshape(depth, 2, 2, 2, channels, 128).transpose(3, 0, 1, 2, 4, 5)
        own_small = scatter_sum(small_blocks, "cyx")
    else:

        def to_rows(grad):
            return lax.psum_scatter(grad.astype(F32), BOTH, scatter_dimension=0, tiled=True)

        own_ffn1_a, own_ffn1_b = to_rows(grad_ffn1_a), to_rows(grad_ffn1_b)
        own_ffn2_a, own_ffn2_b = to_rows(grad_ffn2_a), to_rows(grad_ffn2_b)
        own_conv_a, own_conv_b = to_rows(grad_conv_a), to_rows(grad_conv_b)
        own_small = to_rows(small_grads)
        own_att = lax.psum_scatter(
            lax.psum_scatter(grad_att.astype(F32), "batch", scatter_dimension=1, tiled=True),
            "heads",
            scatter_dimension=0,
            tiled=True,
        )[0]
    own_small = own_small.T
    tokens = kernel_len + 12
    turned = own_att[:, 512:].reshape(2, width // 2, 2 * head_dim).transpose(1, 0, 2)
    parts = jnp.stack(
        [own_att[:, :128], own_att[:, 128:256], own_att[:, 256:384], turned.reshape(width, 128)],
        axis=1,
    )
    own_proj = parts.reshape(width, 4, 2, head_dim).transpose(2, 0, 1, 3)
    own_out = own_att[:, 384:512].T.reshape(2, head_dim, width)
    return (
        layer_out.astype(BF),
        upstream.astype(BF),
        own_ffn1_a,
        own_ffn1_b,
        own_proj.reshape(2, width, 4 * head_dim),
        own_out,
        own_small[tokens : tokens + 2],
        own_conv_a,
        own_small[:kernel_len],
        own_conv_b,
        own_ffn2_a,
        own_ffn2_b,
        own_small[kernel_len : kernel_len + 6],
        own_small[kernel_len + 6 : kernel_len + 12],
    )


def solution(mesh):
    placed = (
        P(("batch", "heads"), None),
        P(("batch", "heads"), None),
        P(),
        P(),
        P(("batch", "heads"), None),
        P(("batch", "heads"), None),
        P("heads", "batch", None),
        P("heads", None, "batch"),
        P("heads", "batch"),
        P(("batch", "heads"), None),
        P(None, ("batch", "heads")),
        P(("batch", "heads"), None),
        P(("batch", "heads"), None),
        P(("batch", "heads"), None),
        P(None, ("batch", "heads")),
        P(None, ("batch", "heads")),
    )
    return jax.shard_map(
        local,
        mesh=mesh,
        in_specs=placed,
        out_specs=(
            P(("batch", "heads"), None),
            P(("batch", "heads"), None),
            P(("batch", "heads"), None),
            P(("batch", "heads"), None),
            P("heads", "batch", None),
            P("heads", None, "batch"),
            P("heads", "batch"),
            P(("batch", "heads"), None),
            P(None, ("batch", "heads")),
            P(("batch", "heads"), None),
            P(("batch", "heads"), None),
            P(("batch", "heads"), None),
            P(None, ("batch", "heads")),
            P(None, ("batch", "heads")),
        ),
        check_vma=False,
    )
```

```python
import math

import jax
import jax.numpy as jnp
from jax import lax
from jax.experimental import pallas as pl
from jax.experimental.pallas import tpu as pltpu
from jax.sharding import PartitionSpec as P

epsilon = 1e-05
BF = jnp.bfloat16
F32 = jnp.float32
BOTH = ("batch", "heads")
CHUNK = 256
HALO = 16
SCALE = 0.125
LOG2E = 1.4426950408889634
GAIN, BIAS, POS_BIAS = 32, 38, 44
KZ = (0, 2, 1, 3)
DIMS = {"y": ("batch", 1), "x": ("heads", 2)}
VMEM_BYTES = 40 * 2**20


def swap(source, axis, mask):
    count = lax.axis_size(axis)
    return lax.ppermute(source, axis, [(i, i ^ mask) for i in range(count)])


def sum_over(source, axis):
    mask = 1
    while mask < lax.axis_size(axis):
        source = source + swap(source, axis, mask)
        mask *= 2
    return source


def halo(cells):
    ends = lax.axis_size("heads") - 1
    rows = cells.shape[0]
    before = lax.ppermute(cells[rows - HALO :], "heads", [(i, i + 1) for i in range(ends)])
    after = lax.ppermute(cells[:HALO], "heads", [(i + 1, i) for i in range(ends)])
    return before, after


def behind(source, *others):
    return lax.optimization_barrier((source,) + others)[0]


def gather_depth(shard):
    held = shard[None]
    for mask in (4, 2):
        held = jnp.concatenate([held, swap(held, "batch", mask)])
    return held


def total(*terms):
    value = terms[0].astype(F32)
    for term in terms[1:]:
        value = value + term.astype(F32)
    return value


class Exchange:
    def __init__(self, own, heard, steps):
        self.terms, self.steps = [own, heard], list(steps)

    def send(self):
        parts, axis, mask = self.steps.pop(0)
        moving = total(*[term[part] for term, part in zip(self.terms, parts, strict=True)])
        self.terms.append(swap(moving.astype(BF), axis, mask))


def steps_first(order):
    one, two = DIMS[order[0]], DIMS[order[1]]
    return [
        ([(1,), (1,)],) + one,
        ([(0, 1), (0, 1), (1,)],) + two,
        ([(0, 0, slice(2, 4)), (0, 0, slice(2, 4)), (0, slice(2, 4)), (slice(2, 4),)],) + ("batch", 2),
        ([(0, 0, 1), (0, 0, 1), (0, 1), (1,), (1,)],) + ("batch", 4),
    ]


def steps_attention():
    high = slice(2, 4)
    return [
        ([(1,), (1,)], "batch", 1),
        ([(0, high), (0, high), (high,)], "batch", 2),
        ([(0, 1), (0, 1), (1,), (1,)], "batch", 4),
        ([(0, 0, 1), (0, 0, 1), (0, 1), (0, 1), (1,)], "heads", 2),
    ]


def dot(left, right):
    return jnp.dot(left, right, preferred_element_type=F32)


def dot_nt(left, right):
    return lax.dot_general(left, right, (((1,), (1,)), ((), ())), preferred_element_type=F32)


def dot_tn(left, right):
    return lax.dot_general(left, right, (((0,), (0,)), ((), ())), preferred_element_type=F32)


def norm(source):
    center = source - jnp.mean(source, axis=-1, keepdims=True)
    scale = lax.rsqrt(jnp.mean(center * center, axis=-1, keepdims=True) + epsilon)
    return center * scale, scale


def norm_back(upstream, normed, scale, gain_row):
    inner = upstream * gain_row
    mean = jnp.mean(inner, axis=-1, keepdims=True)
    along = jnp.mean(inner * normed, axis=-1, keepdims=True)
    gain_grad = jnp.sum(upstream * normed, axis=0, keepdims=True)
    return scale * (inner - mean - normed * along), gain_grad, jnp.sum(upstream, axis=0, keepdims=True)


def row(small_ref, index):
    return small_ref[index : index + 1, :]


def place():
    batch_at = lax.axis_index("batch")
    heads_at = lax.axis_index("heads")
    return batch_at // 2, batch_at % 2, heads_at // 2, heads_at % 2


def block_index(kz, ky, kx, kc):
    z, y, x, c = place()
    return ((z ^ kz) * 2 + (y ^ ky)) * 4 + (x ^ kx) * 2 + (c ^ kc)


def part(index, size):
    return pl.ds(pl.multiple_of(index * size, size), size)


def valid_rows(ints_ref, rows):
    steps = lax.broadcasted_iota(jnp.int32, (rows, 1), 0) + ints_ref[1]
    return (steps < ints_ref[0]).astype(F32)


def whole(array):
    return pl.BlockSpec(array.shape, lambda *_: (0,) * len(array.shape), pipeline_mode=pl.Buffered(1))


def per_pair(array):
    return pl.BlockSpec((1,) + array.shape[1:], lambda h: (h,) + (0,) * (len(array.shape) - 1))


def shaped(shape, kind):
    return jax.ShapeDtypeStruct(shape, kind)


SMEM = pl.BlockSpec(memory_space=pltpu.SMEM)


VMEM = pl.BlockSpec(memory_space=pltpu.VMEM)


def cost(time):
    return pl.CostEstimate(flops=int(time * 10**9), bytes_accessed=2**12, transcendentals=0)


def run(kernel, inputs, outs, name, specs=None, grid=(), scratch=(), limit=24, time=0.01):
    return pl.pallas_call(
        kernel,
        grid=grid,
        in_specs=specs or [VMEM] * len(inputs),
        out_specs=[whole(o) for o in outs] if grid else [VMEM] * len(outs),
        out_shape=outs,
        scratch_shapes=list(scratch),
        compiler_params=pltpu.CompilerParams(vmem_limit_bytes=limit * 2**20),
        cost_estimate=cost(time),
        name=name,
    )(*inputs)


def fetch(*arrays):
    def kernel(*refs):
        count = len(arrays)
        copies = [pltpu.make_async_copy(refs[i], refs[count + i], refs[-1].at[i]) for i in range(count)]
        for copy in copies:
            copy.start()
        for copy in copies:
            copy.wait()

    return run(
        kernel,
        list(arrays),
        [shaped(a.shape, a.dtype) for a in arrays],
        "fetch",
        specs=[pl.BlockSpec(memory_space=pltpu.HBM)] * len(arrays),
        scratch=[pltpu.SemaphoreType.DMA((len(arrays),))],
    )


def place_first(sets_a, sets_b):
    def kernel(*refs):
        a_refs, b_refs = refs[:4], refs[4:8]
        win_ref, wout_ref, small_ref, pb_ref, chan_ref, stage_ref = refs[8:]
        for k in range(4):
            for i in range(8):
                at = block_index(KZ[i % 4], i // 4, k & 1, k >> 1)
                for column in range(4):
                    win_ref[column, part(at, 16), :] = a_refs[k][i, :, 512 * column : 512 * column + 512]
                at = block_index(KZ[i % 4], k & 1, i // 4, k >> 1)
                wout_ref[part(at, 64), :] = b_refs[k][i, 0:64, :]
                chan_ref[part(at, 16), :] = b_refs[k][i, 64:80, 0:128].astype(F32)
        small_ref[...] = chan_ref[...].T
        for mask in range(4):
            pair = lax.axis_index("heads") ^ mask
            for b in range(8):
                stage_ref[16 * b : 16 * b + 16, :] = chan_ref[part(4 * b + pair, 16), :]
            one, two = (stage_ref[...].T[at : at + 1] for at in (POS_BIAS, POS_BIAS + 1))
            pb_ref[mask, 0:1, :] = jnp.concatenate([one[:, :64], two[:, :64]], axis=1)
            pb_ref[mask, 1:2, :] = jnp.concatenate([one[:, 64:], two[:, 64:]], axis=1)

    return run(
        kernel,
        list(sets_a) + list(sets_b),
        [shaped((4, 512, 512), BF), shaped((2048, 512), BF), shaped((128, 512), F32), shaped((4, 2, 128), F32)],
        "place_first",
        scratch=[pltpu.VMEM((512, 128), F32), pltpu.VMEM((128, 128), F32)],
    )


def place_attention(sets):
    def kernel(*refs):
        tw_ref, pos_ref = refs[4:]
        z, y, _, _ = place()
        for k in range(4):
            for i in range(8):
                pair = (i % 2) * 2 + (k >> 1)
                at = (z ^ KZ[i // 2]) * 2 + (y ^ (k & 1))
                tw_ref[pair, part(at, 64), :] = refs[k][i, :, 0:512]
                pos_ref[pair, part(at, 32), :] = refs[k][i, 0:32, 512:640]
                pos_ref[pair, part(at + 8, 32), :] = refs[k][i, 32:64, 512:640]

    return run(
        kernel, list(sets), [shaped((4, 512, 512), BF), shaped((4, 512, 128), BF)], "place_attention"
    )


def ffn1_forward(frames, win, wout, small):
    def kernel(x_ref, win_ref, wout_ref, small_ref, out_ref, normed_ref):
        source = x_ref[...].astype(F32)
        normed, _ = norm(source)
        pre = (normed * row(small_ref, GAIN) + row(small_ref, BIAS)).astype(BF)
        total = jnp.zeros_like(source)
        for column in range(win_ref.shape[0]):
            hidden = dot(pre, win_ref[column])
            active = (hidden * jax.nn.sigmoid(hidden)).astype(BF)
            total = total + dot(active, wout_ref[512 * column : 512 * column + 512, :])
        source = source + 0.5 * total
        out_ref[...] = source
        normed, _ = norm(source)
        normed_ref[...] = (normed * row(small_ref, GAIN + 1) + row(small_ref, BIAS + 1)).astype(BF)

    return run(
        kernel,
        [frames, win, wout, small],
        [shaped(frames.shape, F32), shaped(frames.shape, BF)],
        "ffn1_forward",
        time=3,
    )


def halves(first, value):
    zero = jnp.zeros_like(value)
    return jnp.where(first, value, zero), jnp.where(first, zero, value)


def att_forward_kernel(
    mask_ref, own_ref, k1_ref, k2_ref, k3_ref, x1_ref, small_ref, tw_ref, pos_ref, pb_ref, cs_ref, et_ref,
    w_ref, o_ref, kv_ref, q_ref, att_ref, n2_ref, right_ref, total_ref,
):
    rows, width = own_ref.shape
    half = cs_ref.shape[2]
    step = pl.program_id(0)
    tw = tw_ref[0]

    @pl.when(step == 0)
    def _():
        right_ref[0:width, :] = et_ref[...]
        total_ref[...] = x1_ref[...]

    for k, ref in enumerate((own_ref, k1_ref, k2_ref, k3_ref)):
        here = slice(k * rows, k * rows + rows)
        kv = dot(ref[...], tw[:, 128:384])
        kv_ref[0, here, :] = kv.astype(BF)
        right_ref[width : width + 128, here] = kv[:, :128].T.astype(BF)
    value = kv_ref[0, :, 128:]
    query = dot(own_ref[...], tw[:, :128])
    qc = (query + pb_ref[0, 0:1, :]).astype(BF)
    qp = (query + pb_ref[0, 1:2, :]).astype(BF)
    q_ref[0, 0] = qc
    q_ref[0, 1] = qp
    first = lax.broadcasted_iota(jnp.int32, (rows, 128), 1) < 64
    cos, sin = cs_ref[0], cs_ref[1]
    mask = mask_ref[...]
    outs = []
    for qc_h, qp_h in zip(halves(first, qc), halves(first, qp)):
        turned = dot_nt(qp_h, pos_ref[0]) * (SCALE * LOG2E)
        us, uc = turned[:, :half], turned[:, half:]
        left = jnp.concatenate(
            [
                (us * cos + uc * sin).astype(BF),
                (uc * cos - us * sin).astype(BF),
                (qc_h.astype(F32) * (SCALE * LOG2E)).astype(BF),
            ],
            axis=1,
        )
        parts = []
        for r in range(0, rows, CHUNK):
            scores = dot(left[r : r + CHUNK], right_ref[...]) + mask
            top = jnp.max(scores, axis=1, keepdims=True)
            grown = jnp.exp2(scores - top)
            weights = (grown * (1.0 / jnp.sum(grown, axis=1, keepdims=True))).astype(BF)
            w_ref[0, len(outs), r : r + CHUNK, :] = weights
            parts.append(dot(weights, value))
        outs.append(jnp.concatenate(parts, axis=0))
    mixed = jnp.where(first, outs[0], outs[1])
    o_ref[0] = mixed
    total_ref[...] += dot_nt(mixed.astype(BF), tw[:, 384:512])

    @pl.when(step == pl.num_programs(0) - 1)
    def _():
        after = total_ref[...]
        att_ref[...] = after
        normed, _ = norm(after)
        n2_ref[...] = (normed * row(small_ref, GAIN + 2) + row(small_ref, BIAS + 2)).astype(BF)


def att_forward(mask, keys, x1, small, tw, pos, pb, cs, et):
    rows, width = x1.shape
    count = mask.shape[1]
    paired = [
        shaped((4, 2, rows, count), BF),
        shaped((4, rows, 128), F32),
        shaped((4, count, 256), BF),
        shaped((4, 2, rows, 128), BF),
    ]
    shared = [shaped((rows, width), F32), shaped((rows, width), BF)]
    return pl.pallas_call(
        att_forward_kernel,
        grid=(4,),
        in_specs=[whole(mask)]
        + [whole(k) for k in keys]
        + [whole(x1), whole(small), per_pair(tw), per_pair(pos), per_pair(pb), whole(cs), whole(et)],
        out_specs=[per_pair(a) for a in paired] + [whole(a) for a in shared],
        out_shape=paired + shared,
        scratch_shapes=[pltpu.VMEM((width + 128, count), BF), pltpu.VMEM((rows, width), F32)],
        compiler_params=pltpu.CompilerParams(vmem_limit_bytes=56 * 2**20),
        cost_estimate=cost(40),
        name="att_forward",
    )(mask, *keys, x1, small, tw, pos, pb, cs, et)


def att_backward_kernel(fast, *refs):
    (up_ref, n2_ref, dg_ref, own_ref, k1_ref, k2_ref, k3_ref, o_ref, w_ref, kv_ref, q_ref, tw_ref, pos_ref, cs_ref,
     e_ref, near_ref, far_ref, home_ref, db_ref) = refs[:19]
    outs, (dr_ref, dn_ref, dq_ref, og_ref, dconv_ref, tw_grad_ref, pos_grad_ref) = refs[19:-7], refs[-7:]
    rows, width = up_ref.shape
    half = cs_ref.shape[2]
    count = dn_ref.shape[1]
    step = pl.program_id(0)

    @pl.when(step == 0)
    def _():
        og_ref[...] = up_ref[...].astype(BF)
        dn_ref[...] = jnp.zeros_like(dn_ref)
        dq_ref[...] = jnp.zeros_like(dq_ref)
        dconv_ref[...] = dot_tn(n2_ref[...], dg_ref[...]).astype(BF)

    og = og_ref[...]
    tw = tw_ref[0]
    do = dot(og, tw[:, 384:512]).astype(BF)
    key, value = kv_ref[0, :, :128], kv_ref[0, :, 128:]
    first = lax.broadcasted_iota(jnp.int32, (rows, 128), 1) < 64
    do_f = do.astype(F32)
    mixed = o_ref[0]
    do_t = do_f.T.astype(BF)
    qc_t = (q_ref[0, 0].astype(F32) * SCALE).T.astype(BF)
    qp_t = q_ref[0, 1].astype(F32).T.astype(BF)
    cos, sin = cs_ref[0], cs_ref[1]
    dqcs, dqps, dks, dvs, dps = [], [], [], [], []
    for head, (do_h, inner_h) in enumerate(zip(halves(first, do), halves(first, do_f * mixed))):
        mine = slice(head * 64, head * 64 + 64)
        inner = jnp.sum(inner_h, axis=1, keepdims=True)
        for r in range(0, rows, CHUNK):
            dw = dot_nt(do_h[r : r + CHUNK], value)
            weights = w_ref[0, head, r : r + CHUNK, :].astype(F32)
            dr_ref[r : r + CHUNK, :] = (weights * (dw - inner[r : r + CHUNK])).astype(BF)
        dr = dr_ref[...]
        turned = dot(dr, e_ref[...]) * SCALE
        dqcs.append(dot(dr, key) * SCALE)
        dks.append(dot(qc_t[mine], dr).astype(BF))
        dvs.append(dot(do_t[mine], w_ref[0, head]).astype(BF))
        gs, gc = turned[:, :half], turned[:, half:]
        du = jnp.concatenate(
            [(gs * cos - gc * sin).astype(BF), (gs * sin + gc * cos).astype(BF)], axis=1
        )
        dqps.append(dot(du, pos_ref[0]))
        dps.append(dot(qp_t[mine], du))
    dqc = jnp.where(first, dqcs[0], dqcs[1])
    dqp = jnp.where(first, dqps[0], dqps[1])
    db_ref[0, 0:1, :] = jnp.sum(dqc, axis=0, keepdims=True)
    db_ref[0, 1:2, :] = jnp.sum(dqp, axis=0, keepdims=True)
    dq = dqc + dqp
    dq_low = dq.astype(BF)
    dkv = jnp.concatenate(dks + dvs, axis=0)
    dn_ref[...] += dot(tw[:, 128:384], dkv)
    dq_ref[...] += dot_nt(dq_low, tw[:, :128])
    grad_kv = jnp.zeros((256, width), F32)
    for k, ref in enumerate((own_ref, k1_ref, k2_ref, k3_ref)):
        grad_kv = grad_kv + dot(dkv[:, k * rows : k * rows + rows], ref[...])
    grad_q = dot(dq.T.astype(BF), own_ref[...])
    grad_o = dot(mixed.T.astype(BF), og)
    tw_grad_ref[...] = jnp.concatenate([grad_q, grad_kv, grad_o], axis=0).T.astype(BF)
    pos_grad_ref[...] = jnp.concatenate(dps, axis=0).T.astype(BF)

    if fast:
        z, y, x, c = place()
        pair = (x ^ (step // 2)) * 2 + (c ^ (step % 2))

        def write(pack_ref):
            for ky in range(2):
                for i in range(4):
                    at = (z ^ KZ[i]) * 2 + (y ^ ky)
                    pack_ref[ky, i, 0, :, 0:512] = tw_grad_ref[part(at, 64), :]
                    pack_ref[ky, i, 0, 0:32, 512:640] = pos_grad_ref[part(at, 32), :]
                    pack_ref[ky, i, 0, 32:64, 512:640] = pos_grad_ref[part(at + 8, 32), :]
                    for t in range(4):
                        pack_ref[ky, i, 0, 16 * t : 16 * t + 16, 640:896] = dconv_ref[
                            part(at * 4 + pair, 16), 256 * t : 256 * t + 256
                        ]

        pl.when(step % 2 == 0)(lambda: write(outs[0]))
        pl.when(step % 2 == 1)(lambda: write(outs[1]))
    else:
        outs[0][0] = tw_grad_ref[...]
        outs[1][0] = pos_grad_ref[...]
        outs[2][...] = dconv_ref[...]

    @pl.when(step == pl.num_programs(0) - 1)
    def _():
        for k in range(4):
            grad = dn_ref[:, k * rows : k * rows + rows].T
            if k == 0:
                home_ref[...] = grad + dq_ref[...]
            elif k == 2:
                far_ref[...] = grad.astype(BF)
            else:
                near_ref[k // 2] = grad.astype(BF)


def att_backward(fast, upstream, n2, dgated, keys, mixed, weights, kv, queries, tw, pos, cs, e):
    rows, width = upstream.shape
    count = kv.shape[1]
    shared = [shaped((2, rows, width), BF), shaped((rows, width), BF), shaped((rows, width), F32)]
    paired = [shaped((4, 2, 128), F32)]
    specs = [whole(a) for a in shared] + [per_pair(a) for a in paired]
    outs = shared + paired
    if fast:
        extra = [shaped((2, 4, 2, 64, 896), BF)] * 2
        specs += [pl.BlockSpec((2, 4, 1, 64, 896), lambda h: (0, 0, h // 2, 0, 0))] * 2
    else:
        extra = [shaped((4, width, 512), BF), shaped((4, width, 128), BF), shaped((width, 1024), BF)]
        specs += [per_pair(extra[0]), per_pair(extra[1]), whole(extra[2])]
    return pl.pallas_call(
        lambda *refs: att_backward_kernel(fast, *refs),
        grid=(4,),
        in_specs=[whole(upstream), whole(n2), whole(dgated)]
        + [whole(k) for k in keys]
        + [per_pair(mixed), per_pair(weights), per_pair(kv), per_pair(queries), per_pair(tw), per_pair(pos)]
        + [whole(cs), whole(e)],
        out_specs=specs,
        out_shape=outs + extra,
        scratch_shapes=[
            pltpu.VMEM((rows, count), BF),
            pltpu.VMEM((width, count), F32),
            pltpu.VMEM((rows, width), F32),
            pltpu.VMEM((rows, width), BF),
            pltpu.VMEM((width, 1024), BF),
            pltpu.VMEM((width, 512), BF),
            pltpu.VMEM((width, 128), BF),
        ],
        compiler_params=pltpu.CompilerParams(vmem_limit_bytes=VMEM_BYTES),
        cost_estimate=cost(0.01),
        name="att_backward",
    )(upstream, n2, dgated, *keys, mixed, weights, kv, queries, tw, pos, cs, e)


def gate_forward(ints, n2, conv_in):
    rows, width = n2.shape

    def kernel(ints_ref, n2_ref, *refs):
        w_refs, (glu_ref, gated_ref, a_ref, b_ref) = refs[:2], refs[2:]
        a_ref[...] = w_refs[0][...].reshape(width, width)
        b_ref[...] = w_refs[1][...].reshape(width, width)
        left = dot(n2_ref[...], a_ref[...])
        right = dot(n2_ref[...], b_ref[...])
        gated_ref[:, :width] = left
        gated_ref[:, width:] = right
        glu_ref[...] = (left * jax.nn.sigmoid(right) * valid_rows(ints_ref, rows)).astype(BF)

    if len(conv_in) == 1:
        conv_in = conv_in * 2
        specs = [
            pl.BlockSpec((32, 16, 512), lambda *_, at=at: (0, at, 0), pipeline_mode=pl.Buffered(1)) for at in (8, 9)
        ]
    else:
        specs = [whole(a) for a in conv_in]
    return run(
        kernel,
        [ints, n2] + conv_in,
        [shaped((rows, width), BF), shaped((rows, 2 * width), F32)] + [shaped((width, width), BF)] * 2,
        "gate_forward",
        specs=[SMEM, whole(n2)] + specs,
        grid=(1,),
        limit=60,
    )


def extend(ext_ref, before_ref, own_ref, after_ref):
    rows = own_ref.shape[0]
    ext_ref[0, 0:HALO, :] = before_ref[...].astype(F32)
    ext_ref[0, HALO : HALO + rows, :] = own_ref[...].astype(F32)
    ext_ref[0, HALO + rows : 2 * HALO + rows, :] = after_ref[...].astype(F32)
    kept = 2 * HALO + rows - 8
    for shift in range(1, 8):
        ext_ref[shift, 0:kept, :] = ext_ref[0, shift : shift + kept, :]


def shifted(ext_ref, start, size, columns):
    return ext_ref[start % 8, start - start % 8 : start - start % 8 + size, columns]


def conv_forward(ints, glu, rim, small):
    rows, width = glu.shape

    def kernel(ints_ref, before_ref, glu_ref, after_ref, small_ref, depth_ref, sums_ref, ext_ref):
        extend(ext_ref, before_ref, glu_ref, after_ref)
        steps = lax.broadcasted_iota(jnp.int32, (64, 1), 0) + ints_ref[1]
        for c in range(0, width, 128):
            one = jnp.zeros((1, 128), F32)
            two = jnp.zeros((1, 128), F32)
            for r in range(0, rows, 64):
                total = jnp.zeros((64, 128), F32)
                for k in range(2 * HALO):
                    total = total + shifted(ext_ref, r + k + 1, 64, slice(c, c + 128)) * small_ref[k : k + 1, c : c + 128]
                depth_ref[r : r + 64, c : c + 128] = total
                kept = jnp.where(steps + r < ints_ref[0], total, 0.0)
                one = one + jnp.sum(kept, axis=0, keepdims=True)
                two = two + jnp.sum(kept * total, axis=0, keepdims=True)
            sums_ref[0:1, c : c + 128] = one
            sums_ref[1:2, c : c + 128] = two

    return run(
        kernel,
        [ints, rim[0], glu, rim[1], small],
        [shaped((rows, width), F32), shaped((2, width), F32)],
        "conv_forward",
        time=4,
        specs=[SMEM] + [VMEM] * 4,
        scratch=[pltpu.VMEM((8, rows + 2 * HALO, width), F32)],
    )


def conv_backward(ints, glu, rim, depth_low, depth_rim, small, gated, conv_in, after_att, upstream):
    rows, width = glu.shape

    def kernel(
        ints_ref, gb_ref, glu_ref, ga_ref, db_ref, d_ref, da_ref, small_ref, gated_ref, att_ref, up_ref, *refs
    ):
        w_refs, (out_ref, dg_ref, grads_ref, ext_ref, extd_ref, dglu_ref) = refs[:-6], refs[-6:]
        extend(ext_ref, gb_ref, glu_ref, ga_ref)
        extend(extd_ref, db_ref, d_ref, da_ref)
        taps = 2 * HALO
        for c in range(0, width, 128):
            cols = slice(c, c + 128)
            for r in range(0, rows, 64):
                total = jnp.zeros((64, 128), F32)
                for k in range(taps):
                    at = r + taps - 1 - k
                    total = total + shifted(extd_ref, at, 64, cols) * small_ref[k : k + 1, cols]
                dglu_ref[r : r + 64, cols] = total
            for k in range(taps):
                total = jnp.zeros((8, 128), F32)
                for r in range(0, rows, 64):
                    product = shifted(ext_ref, r + k + 1, 64, cols) * shifted(extd_ref, HALO + r, 64, cols)
                    total = total + jnp.sum(product.reshape(8, 8, 128), axis=0)
                grads_ref[k : k + 1, cols] = jnp.sum(total, axis=0, keepdims=True)
        grad = dglu_ref[...] * valid_rows(ints_ref, rows)
        gate = jax.nn.sigmoid(gated_ref[:, width:])
        left = (grad * gate).astype(BF)
        right = (grad * gated_ref[:, :width] * gate * (1.0 - gate)).astype(BF)
        dg_ref[:, :width] = left
        dg_ref[:, width:] = right
        inner = dot_nt(left, w_refs[0][...]) + dot_nt(right, w_refs[1][...])
        normed, scale = norm(att_ref[...])
        grad, gain_grad, bias_grad = norm_back(inner, normed, scale, row(small_ref, GAIN + 2))
        out_ref[...] = up_ref[...] + grad
        grads_ref[taps : taps + 1, :] = gain_grad
        grads_ref[taps + 1 : taps + 2, :] = bias_grad

    inputs = [ints, rim[0], glu, rim[1], depth_rim[0], depth_low, depth_rim[1], small, gated]
    return run(
        kernel,
        inputs + [after_att, upstream] + conv_in,
        [shaped((rows, width), F32), shaped((rows, 2 * width), BF), shaped((40, width), F32)],
        "conv_backward",
        time=0.01,
        specs=[SMEM] + [VMEM] * (len(inputs) + 1 + len(conv_in)),
        scratch=[pltpu.VMEM((8, rows + 2 * HALO, width), F32)] * 2 + [pltpu.VMEM((rows, width), F32)],
    )


def middle(ints, floats, depth, sums, after_att, cotangent, small, weights):
    rows, width = depth.shape

    def kernel(
        ints_ref, floats_ref, depth_ref, sums_ref, att_ref, cot_ref, small_ref, *refs
    ):
        w_refs = refs[:-12]
        (layer_ref, up_ref, raw_ref, gsum_ref, grads_ref, pre_ref, act_ref, dhid_ref, branch_ref, swish_ref, low_ref,
         hid_ref) = refs[-12:]
        packed = len(w_refs) == 1
        columns = hid_ref.shape[0]

        def w_in(column):
            if packed:
                return w_refs[0][:, 16 * column : 16 * column + 16, :].reshape(width, 512)
            return w_refs[0][column]

        def w_out(column):
            if packed:
                return w_refs[0][8 * column : 8 * column + 8, 64:128, :].reshape(512, width)
            return w_refs[1][column]

        total_valid = floats_ref[1]
        mean_bn = sums_ref[0:1, :] / total_valid
        var_bn = sums_ref[1:2, :] / total_valid - mean_bn * mean_bn
        inv = lax.rsqrt(var_bn + epsilon)
        center = depth_ref[...] - mean_bn
        bn_gain = row(small_ref, GAIN + 5)
        z = center * inv * bn_gain + row(small_ref, BIAS + 5)
        swish = (z * jax.nn.sigmoid(z)).astype(BF)
        swish_ref[...] = swish
        conv_out = w_refs[0][:, 160:176, :].reshape(width, width) if packed else w_refs[2][...]
        after_conv = att_ref[...] + dot(swish, conv_out)
        normed3, scale3 = norm(after_conv)
        pre = (normed3 * row(small_ref, GAIN + 3) + row(small_ref, BIAS + 3)).astype(BF)
        pre_ref[...] = pre
        total = jnp.zeros((rows, width), F32)
        for column in range(columns):
            hidden = dot(pre, w_in(column))
            hid_ref[column] = hidden
            active = (hidden * jax.nn.sigmoid(hidden)).astype(BF)
            act_ref[column] = active
            total = total + dot(active, w_out(column))
        normed4, scale4 = norm(after_conv + 0.5 * total)
        gain4 = row(small_ref, GAIN + 4)
        layer_ref[...] = (normed4 * gain4 + row(small_ref, BIAS + 4)).astype(BF)
        seed = cot_ref[...].astype(F32) * (valid_rows(ints_ref, rows) * floats_ref[0])
        up, gain_grad, bias_grad = norm_back(seed, normed4, scale4, gain4)
        grads_ref[...] = jnp.zeros_like(grads_ref)
        grads_ref[2:3, :] = gain_grad
        grads_ref[3:4, :] = bias_grad
        branch = (0.5 * up).astype(BF)
        branch_ref[...] = branch
        total = jnp.zeros((rows, width), F32)
        for column in range(columns):
            hidden = hid_ref[column]
            gate = jax.nn.sigmoid(hidden)
            grad = dot_nt(branch, w_out(column)) * (gate * (1.0 + hidden * (1.0 - gate)))
            grad = grad.astype(BF)
            dhid_ref[column] = grad
            total = total + dot_nt(grad, w_in(column))
        grad, gain_grad, bias_grad = norm_back(total, normed3, scale3, row(small_ref, GAIN + 3))
        grads_ref[0:1, :] = gain_grad
        grads_ref[1:2, :] = bias_grad
        up = up + grad
        up_ref[...] = up
        low = up.astype(BF)
        low_ref[...] = low
        gate = jax.nn.sigmoid(z)
        dz = dot_nt(low, conv_out) * (gate * (1.0 + z * (1.0 - gate)))
        grads_ref[4:5, :] = jnp.sum(dz * center, axis=0, keepdims=True) * inv
        grads_ref[5:6, :] = jnp.sum(dz, axis=0, keepdims=True)
        raw = dz * (bn_gain * inv)
        raw_ref[...] = raw
        gsum_ref[0:1, :] = -jnp.sum(raw, axis=0, keepdims=True)
        gsum_ref[1:2, :] = jnp.sum(raw * center, axis=0, keepdims=True) * (-0.5 * inv * inv)

    square_f, square = shaped((rows, width), F32), shaped((rows, width), BF)
    wide = shaped((4, rows, 512), BF)
    inputs = [ints, floats, depth, sums, after_att, cotangent, small]
    return run(
        kernel,
        inputs + weights,
        [square, square_f, square_f, shaped((2, width), F32), shaped((8, width), F32)]
        + [square, wide, wide, square, square, square],
        "middle",
        time=8,
        specs=[SMEM, SMEM] + [VMEM] * (len(inputs) - 2 + len(weights)),
        scratch=[pltpu.VMEM((4, rows, 512), F32)],
    )


def middle_grads(fast, pre, act, dhid, branch, swish, low):
    width = pre.shape[1]

    def kernel(pre_ref, act_ref, dhid_ref, branch_ref, swish_ref, low_ref, *outs):
        for column in range(act_ref.shape[0]):
            grad_in = dot_tn(pre_ref[...], dhid_ref[column]).astype(BF)
            grad_out = dot_tn(act_ref[column], branch_ref[...]).astype(BF)
            if fast:
                outs[0][:, 16 * column : 16 * column + 16, :] = grad_in.reshape(32, 16, 512)
                outs[0][8 * column : 8 * column + 8, 64:128, :] = grad_out.reshape(8, 64, 512)
            else:
                outs[0][column] = grad_in
                outs[1][column] = grad_out
        grad = dot_tn(swish_ref[...], low_ref[...]).astype(BF)
        if fast:
            outs[0][:, 128:144, :] = grad.reshape(32, 16, 512)
        else:
            outs[2][...] = grad

    if fast:
        outs = [shaped((32, 144, 512), BF)]
    else:
        outs = [shaped((4, width, 512), BF), shaped((4, 512, width), BF), shaped((width, width), BF)]
    return run(kernel, [pre, act, dhid, branch, swish, low], outs, "middle_grads", time=3)


def ffn1_again(frames, x1, win, wout, small):
    rows, width = x1.shape

    def kernel(
        x_in, x1_in, win_in, wout_in, small_ref, pre_ref, act_ref, slope_ref, x1_ref, x_ref, win_ref, wout_ref, sems
    ):
        pairs = ((x_in, x_ref), (win_in, win_ref), (x1_in, x1_ref), (wout_in, wout_ref))
        copies = [pltpu.make_async_copy(a, b, sems.at[k]) for k, (a, b) in enumerate(pairs)]
        for copy in copies:
            copy.start()
        copies[0].wait()
        normed, _ = norm(x_ref[...].astype(F32))
        pre = (normed * row(small_ref, GAIN) + row(small_ref, BIAS)).astype(BF)
        pre_ref[...] = pre
        copies[1].wait()
        for column in range(win.shape[0]):
            hidden = dot(pre, win_ref[column])
            gate = jax.nn.sigmoid(hidden)
            act_ref[column] = (hidden * gate).astype(BF)
            slope_ref[column] = gate * (1.0 + hidden * (1.0 - gate))
        copies[2].wait()
        copies[3].wait()

    wide = (win.shape[0], rows, 512)
    return run(
        kernel,
        [frames, x1, win, wout, small],
        [shaped((rows, width), BF), shaped(wide, BF), shaped(wide, F32), shaped(x1.shape, F32)]
        + [shaped(frames.shape, BF), shaped(win.shape, BF), shaped(wout.shape, BF)],
        "ffn1_again",
        time=0.01,
        specs=[pl.BlockSpec(memory_space=pltpu.HBM)] * 4 + [VMEM],
        scratch=[pltpu.SemaphoreType.DMA((4,))],
    )


def ffn1_backward(fast, again, upstream, home, near, far, small, conv_rows, mid_rows, grad_bias):
    pre, active, slope, x1, frames, win, wout = again
    rows, width = x1.shape

    def kernel(
        pre_ref, act_ref, slope_ref, x1_ref, x_ref, win_ref, wout_ref, up_ref, home_ref, near_ref, far_ref, small_ref,
        conv_ref, mid_ref, bias_ref,
        *refs,
    ):
        frames_ref, outs, (chan_ref, gin_ref, gout_ref) = refs[0], refs[1:-3], refs[-3:]
        dn = home_ref[...] + near_ref[0].astype(F32) + far_ref[...].astype(F32)
        normed, scale = norm(x1_ref[...])
        grad, gain1, bias1 = norm_back(dn, normed, scale, row(small_ref, GAIN + 1))
        up = up_ref[...] + grad
        branch = (0.5 * up).astype(BF)
        normed, scale = norm(x_ref[...].astype(F32))
        gain0 = row(small_ref, GAIN)
        pre = pre_ref[...]
        total = jnp.zeros((rows, width), F32)
        for column in range(win_ref.shape[0]):
            gout_ref[512 * column : 512 * column + 512, :] = dot_tn(act_ref[column], branch).astype(BF)
            grad = dot_nt(branch, wout_ref[512 * column : 512 * column + 512, :])
            grad = (grad * slope_ref[column]).astype(BF)
            gin_ref[column] = dot_tn(pre, grad).astype(BF)
            total = total + dot_nt(grad, win_ref[column])
        grad, gain_grad, bias_grad = norm_back(total, normed, scale, gain0)
        frames_ref[...] = (up + grad).astype(BF)
        chan_ref[...] = jnp.zeros_like(chan_ref)
        taps = GAIN
        chan_ref[0:taps, :] = conv_ref[0:taps, :]
        for first, at in ((GAIN, 0), (BIAS, 1)):
            chan_ref[first + 2 : first + 3, :] = conv_ref[taps + at : taps + at + 1, :]
            for k in range(3):
                chan_ref[first + 3 + k : first + 4 + k, :] = mid_ref[2 * k + at : 2 * k + at + 1, :]
        chan_ref[POS_BIAS : POS_BIAS + 2, :] = bias_ref[...]
        chan_ref[GAIN : GAIN + 1, :] = gain_grad
        chan_ref[GAIN + 1 : GAIN + 2, :] = gain1
        chan_ref[BIAS : BIAS + 1, :] = bias_grad
        chan_ref[BIAS + 1 : BIAS + 2, :] = bias1
        if fast:
            a_far, a_own, b_far, b_own = outs
            turned = chan_ref[...].T.astype(BF)
            for kc, a_out, b_out in ((1, a_far, b_far), (0, a_own, b_own)):
                a_out[:, :, :, 64:80, 128:512] = jnp.zeros((2, 2, 4, 16, 384), BF)
                for one in range(2):
                    for two in range(2):
                        for i in range(4):
                            at = block_index(KZ[i], two, one, kc)
                            for column in range(4):
                                a_out[one, two, i, 16 * column : 16 * column + 16, :] = gin_ref[
                                    column, part(at, 16), :
                                ]
                            at = block_index(KZ[i], one, two, kc)
                            b_out[one, two, i] = gout_ref[part(at, 64), :]
            gin_ref[0, :, 0:128] = turned
            for kc, a_out in ((1, a_far), (0, a_own)):
                for one in range(2):
                    for two in range(2):
                        for i in range(4):
                            at = block_index(KZ[i], two, one, kc)
                            a_out[one, two, i, 64:80, 0:128] = gin_ref[0, part(at, 16), 0:128]
        else:
            outs[0][...] = gin_ref[...]
            outs[1][...] = gout_ref[...]
            outs[2][...] = chan_ref[...].T.astype(BF)

    if fast:
        outs = [shaped((2, 2, 4, 80, 512), BF)] * 2 + [shaped((2, 2, 4, 64, 512), BF)] * 2
    else:
        outs = [shaped((4, width, 512), BF), shaped((2048, width), BF), shaped((width, 128), BF)]
    return run(
        kernel,
        list(again) + [upstream, home, near, far, small, conv_rows, mid_rows, grad_bias],
        [shaped((rows, width), BF)] + outs,
        "ffn1_backward",
        time=0.01,
        scratch=[
            pltpu.VMEM((128, width), F32),
            pltpu.VMEM((4, width, 512), BF),
            pltpu.VMEM((2048, width), BF),
        ],
    )


def tables(head_index, own_length, rows, width):
    pairs = lax.axis_size("heads")
    freq = jnp.exp(
        jnp.arange(width // 2, dtype=jnp.int32).astype(F32) * (-2.0 * math.log(10000.0) / width)
    )
    steps = rows // 128
    others = jnp.arange(pairs, dtype=jnp.int32) ^ head_index
    coarse = (others[:, None] * steps + jnp.arange(steps, dtype=jnp.int32)[None, :]).reshape(-1)
    coarse_phase = (coarse * 128).astype(F32)[:, None] * freq[None, :]
    fine_phase = jnp.arange(128, dtype=jnp.int32).astype(F32)[:, None] * freq[None, :]
    phase = jnp.concatenate([coarse_phase, fine_phase])
    info = jnp.stack([head_index, own_length]).astype(jnp.int32)
    count = pairs * rows
    half = width // 2

    def kernel(info_ref, sin_ref, cos_ref, table_ref, turned_ref, own_ref, mask_ref):
        sin_b, cos_b = sin_ref[pairs * steps :, :], cos_ref[pairs * steps :, :]
        for a in range(pairs * steps):
            here = slice(128 * a, 128 * a + 128)
            sin_a, cos_a = sin_ref[a : a + 1, :], cos_ref[a : a + 1, :]
            sin = sin_a * cos_b + cos_a * sin_b
            cos = cos_a * cos_b - sin_a * sin_b
            table_ref[here, :half] = sin.astype(BF)
            table_ref[here, half:] = cos.astype(BF)
            turned_ref[:half, here] = sin.T.astype(BF)
            turned_ref[half:, here] = cos.T.astype(BF)
            if a < steps:
                own_ref[0, here, :] = cos
                own_ref[1, here, :] = sin
            at = lax.broadcasted_iota(jnp.int32, (1, 128), 1)
            at = at + ((info_ref[0] ^ (a // steps)) * rows + 128 * (a % steps))
            mask_ref[0:1, here] = jnp.where(at < info_ref[1], 0.0, -1e30)

    return run(
        kernel,
        [info, jnp.sin(phase), jnp.cos(phase)],
        [shaped((count, width), BF), shaped((width, count), BF), shaped((2, rows, half), F32), shaped((1, count), F32)],
        "tables",
        specs=[SMEM, VMEM, VMEM],
    )


def prepare(ffn1_out, dw_kernel, norm_gain, norm_bias, pos_bias, att_proj, att_out, ffn2_in, ffn2_out, conv_in, conv_out):
    head_dim = att_out.shape[1]

    def kernel(
        out1_ref, dw_ref, gain_ref, bias_ref, posb_ref, proj_ref, att_ref, in2_ref, out2_ref, cin_ref, cout_ref,
        b_ref, t_ref, pack_ref, square_ref, pos_ref,
    ):
        b_ref[0:64, :] = out1_ref[...]
        square_ref[...] = jnp.zeros_like(square_ref)
        square_ref[0:GAIN, 0:16] = dw_ref[...].astype(F32)
        square_ref[GAIN:BIAS, 0:16] = gain_ref[...].astype(F32)
        square_ref[BIAS:POS_BIAS, 0:16] = bias_ref[...].astype(F32)
        square_ref[POS_BIAS : POS_BIAS + 2, 0:16] = posb_ref[...].astype(F32)
        b_ref[64:80, :] = jnp.zeros((16, 512), BF)
        b_ref[64:80, 0:128] = square_ref[...].T[0:16].astype(BF)
        both = [proj_ref[h].astype(F32) for h in range(2)]
        for k in range(3):
            columns = slice(k * head_dim, k * head_dim + head_dim)
            t_ref[:, 128 * k : 128 * k + 128] = jnp.concatenate([p[:, columns] for p in both], axis=1).astype(BF)
        square_ref[...] = jnp.zeros_like(square_ref)
        square_ref[0:64, 0:64] = att_ref[0].astype(F32)
        square_ref[64:128, 0:64] = att_ref[1].astype(F32)
        t_ref[:, 384:512] = square_ref[...].T[0:64].astype(BF)
        pos_ref[...] = jnp.concatenate([p[:, 3 * head_dim :] for p in both], axis=1)
        for k in range(2):
            t_ref[32 * k : 32 * k + 32, 512:640] = pos_ref[pl.ds(k, 32, stride=2), :].astype(BF)
        for k in range(4):
            pack_ref[16 * k : 16 * k + 16, :] = in2_ref[:, 512 * k : 512 * k + 512]
        pack_ref[64:128, :] = out2_ref[...]
        for k in range(2):
            pack_ref[128 + 16 * k : 144 + 16 * k, :] = cin_ref[:, 512 * k : 512 * k + 512]
        pack_ref[160:176, :] = cout_ref[...]

    return run(
        kernel,
        [ffn1_out, dw_kernel, norm_gain, norm_bias, pos_bias, att_proj, att_out, ffn2_in, ffn2_out, conv_in, conv_out],
        [shaped((80, 512), BF), shaped((64, 640), BF), shaped((176, 512), BF)],
        "prepare",
        specs=[whole(a) for a in (ffn1_out, dw_kernel, norm_gain, norm_bias, pos_bias, att_proj, att_out)]
        + [whole(a) for a in (ffn2_in, ffn2_out, conv_in, conv_out)],
        grid=(1,),
        scratch=[pltpu.VMEM((128, 128), F32), pltpu.VMEM((64, 128), F32)],
        limit=60,
    )


def own_terms(terms):
    def spec(array):
        lead = len(array.shape) - 2
        return pl.BlockSpec((1,) * lead + array.shape[lead:], lambda *_: (0,) * (lead + 2))

    return list(terms), [spec(t) for t in terms]


def add_terms(refs):
    rows, columns = refs[0].shape[-2:]
    total = refs[0][...].reshape(rows, columns).astype(F32)
    for ref in refs[1:]:
        total = total + ref[...].reshape(rows, columns).astype(F32)
    return total


def finish_first(terms_a, terms_b):
    inputs, specs = own_terms(terms_a + terms_b)

    def kernel(*refs):
        in_ref, out_ref, dw_ref, gain_ref, bias_ref, posb_ref, square_ref = refs[12:]
        total = add_terms(refs[:6])
        for k in range(4):
            in_ref[:, 512 * k : 512 * k + 512] = total[16 * k : 16 * k + 16, :]
        square_ref[...] = jnp.zeros_like(square_ref)
        square_ref[0:16, :] = total[64:80, 0:128]
        turned = square_ref[...].T
        dw_ref[...] = turned[0:GAIN, 0:16]
        gain_ref[...] = turned[GAIN:BIAS, 0:16]
        bias_ref[...] = turned[BIAS:POS_BIAS, 0:16]
        posb_ref[...] = turned[POS_BIAS : POS_BIAS + 2, 0:16]
        out_ref[...] = add_terms(refs[6:12])

    outs = [(16, 2048), (64, 512), (32, 16), (6, 16), (6, 16), (2, 16)]
    return run(
        kernel,
        inputs,
        [shaped(o, F32) for o in outs],
        "finish_first",
        specs=specs,
        grid=(1,),
        scratch=[pltpu.VMEM((128, 128), F32)],
    )


def finish_attention(terms):
    inputs, specs = own_terms(terms)

    def kernel(*refs):
        proj_ref, out_ref, cin_ref, square_ref, pos_ref = refs[6:]
        total = add_terms(refs[:6])
        square_ref[...] = jnp.zeros_like(square_ref)
        square_ref[0:64, :] = total[:, 384:512]
        turned = square_ref[...].T
        for k in range(2):
            pos_ref[pl.ds(k, 32, stride=2), :] = total[32 * k : 32 * k + 32, 512:640]
        for h in range(2):
            for k in range(3):
                at = 128 * k + 64 * h
                proj_ref[h, :, 64 * k : 64 * k + 64] = total[:, at : at + 64]
            proj_ref[h, :, 192:256] = pos_ref[:, 64 * h : 64 * h + 64]
            out_ref[h] = turned[64 * h : 64 * h + 64, 0:64]
        for k in range(4):
            cin_ref[:, 256 * k : 256 * k + 256] = total[16 * k : 16 * k + 16, 640:896]

    return run(
        kernel,
        inputs,
        [shaped((2, 64, 256), F32), shaped((2, 64, 64), F32), shaped((16, 1024), F32)],
        "finish_attention",
        specs=specs,
        grid=(1,),
        scratch=[pltpu.VMEM((128, 128), F32), pltpu.VMEM((64, 128), F32)],
    )


def finish_middle(sums):
    def kernel(sum_ref, in_ref, out_ref, conv_ref):
        for k in range(4):
            in_ref[:, 512 * k : 512 * k + 512] = sum_ref[16 * k : 16 * k + 16, :].astype(F32)
        out_ref[...] = sum_ref[64:128, :].astype(F32)
        conv_ref[...] = sum_ref[128:144, :].astype(F32)

    return run(
        kernel,
        [sums],
        [shaped((16, 2048), F32), shaped((64, 512), F32), shaped((16, 512), F32)],
        "finish_middle",
    )


def small_shard(dw_kernel, norm_gain, norm_bias, pos_bias):
    stacked = jnp.concatenate([dw_kernel, norm_gain, norm_bias, pos_bias], axis=0)
    return jnp.pad(stacked.T, ((0, 0), (0, 128 - stacked.shape[0])))


def att_shard(att_proj, att_out):
    two, rows, four = att_proj.shape
    head_dim = four // 4
    parts = att_proj.reshape(two, rows, 4, head_dim).transpose(1, 2, 0, 3)
    parts = parts.reshape(rows, 4, two * head_dim)
    out_t = att_out.transpose(2, 0, 1).reshape(rows, two * head_dim)
    turned = parts[:, 3].reshape(rows // 2, 2, two * head_dim).transpose(1, 0, 2)
    turned = turned.reshape(rows, two * head_dim)
    return jnp.concatenate([parts[:, 0], parts[:, 1], parts[:, 2], out_t, turned], axis=1)


def column_chunks(array):
    rows, columns = array.shape
    return array.reshape(rows, columns // 512, 512).transpose(1, 0, 2)


def xor_order(array, index):
    bit = 1
    while bit < array.shape[0]:
        flipped = jnp.stack([array[i ^ bit] for i in range(array.shape[0])])
        array = jnp.where((index & bit) != 0, flipped, array)
        bit *= 2
    return array


def rows_of(shard):
    return lax.all_gather(shard, BOTH, axis=0, tiled=True)


def sum_rows(grad):
    return lax.psum_scatter(grad.astype(F32), BOTH, scatter_dimension=0, tiled=True)


def local(
    frames_in,
    cotangent,
    lengths,
    sample_weight,
    ffn1_in,
    ffn1_out,
    att_proj,
    att_out,
    pos_bias,
    conv_in,
    dw_kernel,
    conv_out,
    ffn2_in,
    ffn2_out,
    norm_gain,
    norm_bias,
):
    row_count, model_width = frames_in.shape
    pairs = lax.axis_size("heads")
    batches = lax.axis_size("batch")
    head_index = lax.axis_index("heads")
    batch_index = lax.axis_index("batch")
    channels = ffn1_in.shape[0]
    fast = channels == 16 and batches == 8 and pairs == 4
    kernel_len = dw_kernel.shape[0]
    head_dim = att_out.shape[1]
    width = model_width // batches

    utter_ids = jnp.arange(lengths.shape[0], dtype=jnp.int32)
    own_length = jnp.sum(jnp.where(utter_ids == batch_index, lengths, 0))
    own_weight = jnp.sum(jnp.where(utter_ids == batch_index, sample_weight, 0)).astype(F32) * 0.25
    total_valid = jnp.sum(lengths).astype(F32)
    ints = jnp.stack([own_length, head_index * row_count]).astype(jnp.int32)
    floats = jnp.stack([own_weight, total_valid])

    if fast:
        shard_b, shard_t, pack = prepare(
            ffn1_out, dw_kernel, norm_gain, norm_bias, pos_bias, att_proj, att_out, ffn2_in, ffn2_out, conv_in, conv_out
        )
        held_a, held_b = gather_depth(ffn1_in), gather_depth(shard_b)
        held_t = jnp.stack([shard_t, swap(shard_t, "heads", 2)])
        held_a, held_b, held_t = lax.optimization_barrier((held_a, held_b, held_t))
        side_a, side_b, deep_t = swap(held_a, "batch", 1), swap(held_b, "heads", 2), swap(held_t, "batch", 4)
        side_a, side_b, deep_t = lax.optimization_barrier((side_a, side_b, deep_t))
        held_a, held_b, held_t = (jnp.concatenate(p) for p in ((held_a, side_a), (held_b, side_b), (held_t, deep_t)))
        side_a, side_b, deep_t = swap(held_a, "heads", 2), swap(held_b, "batch", 1), swap(held_t, "batch", 2)
        table, table_t, own_turn, key_mask = tables(behind(head_index, held_a, held_b), own_length, row_count, model_width)
        table, table_t, own_turn, key_mask, side_a, side_b, deep_t = lax.optimization_barrier(
            (table, table_t, own_turn, key_mask, side_a, side_b, deep_t)
        )
        held_t = jnp.concatenate([held_t, deep_t])
        side_t = swap(held_t, "batch", 1)
        pack = lax.all_gather(behind(pack, side_a, side_b), BOTH, axis=0)
        win, wout, small_t, pos_b = place_first(
            (held_a, side_a, swap(held_a, "heads", 1), swap(side_a, "heads", 1)),
            (held_b, side_b, swap(held_b, "heads", 1), swap(side_b, "heads", 1)),
        )
        x1, n1 = ffn1_forward(frames_in, win, wout, small_t)
        held_t, side_t = behind(held_t, n1), behind(side_t, n1)
        sides_t = held_t, side_t
        tw, pos_w = place_attention(sides_t + tuple(swap(t, "heads", 1) for t in sides_t))
        conv_in_w = middle_w = [pack]
    else:
        table, table_t, own_turn, key_mask = tables(head_index, own_length, row_count, model_width)
        small = small_shard(dw_kernel, norm_gain, norm_bias, pos_bias)
        att_part = att_shard(att_proj, att_out)
        win, wout = column_chunks(rows_of(ffn1_in)), rows_of(ffn1_out)
        small_t = rows_of(small).T.astype(F32)
        pos_b = small_t[POS_BIAS : POS_BIAS + 2].reshape(2, batches, pairs, channels).transpose(2, 0, 1, 3)
        pos_b = pos_b.reshape(pairs, 2, 2, head_dim).transpose(0, 2, 1, 3).reshape(pairs, 2, 2 * head_dim)
        pos_b = xor_order(pos_b, head_index)
        att_all = lax.all_gather(lax.all_gather(att_part, "batch", axis=0), "heads", axis=0)
        att_all = xor_order(att_all, head_index)
        tw = att_all[..., :512].reshape(pairs, model_width, 512)
        pos_w = att_all[..., 512:].reshape(pairs, batches, 2, width // 2, 128).transpose(0, 2, 1, 3, 4)
        pos_w = pos_w.reshape(pairs, model_width, 128)
        halves_in = column_chunks(rows_of(conv_in))
        conv_in_w = [halves_in[0], halves_in[1]]
        middle_w = [
            column_chunks(rows_of(ffn2_in)),
            rows_of(ffn2_out).reshape(4, 512, model_width),
            rows_of(conv_out),
        ]

    if not fast:
        x1, n1 = ffn1_forward(frames_in, win, wout, small_t)
    across = swap(n1, "heads", 2)
    keys = [n1, swap(n1, "heads", 1), across, swap(across, "heads", 1)]
    weights, mixed, kv, queries, after_att, n2 = att_forward(
        key_mask, keys, x1, small_t, tw, pos_w, pos_b, own_turn, table_t
    )
    glu, gated, *conv_in_w = gate_forward(ints, n2, conv_in_w)
    rim = halo(glu)
    depth, sums = conv_forward(ints, glu, rim, small_t)
    sums = sum_over(sum_over(sums, "heads"), "batch")
    layer_out, upstream, raw, gsum, mid_rows, pre, act, dhid, branch, swish, low = middle(
        ints, floats, depth, sums, after_att, cotangent, small_t, middle_w
    )

    gsum = sum_over(gsum, "heads")
    pre = behind(pre, gsum)
    gsum = sum_over(gsum, "batch")
    mid_grads = middle_grads(fast, pre, act, dhid, branch, swish, low)
    positions = head_index * row_count + jnp.arange(row_count, dtype=jnp.int32)
    row_valid = (positions < own_length).astype(F32)[:, None]
    mean_bn = sums[0] / total_valid
    grad_first = (gsum[0] - 2.0 * mean_bn * gsum[1]) / total_valid
    grad_second = gsum[1] / total_valid
    raw = behind(raw, *mid_grads)
    depth_low = (raw + row_valid * (grad_first + 2.0 * depth * grad_second)).astype(BF)
    depth_rim = halo(depth_low)
    if fast:
        mid = lax.psum_scatter(mid_grads[0].reshape(32 * 144, 512), BOTH, scatter_dimension=0, tiled=True)
    upstream, dgated, conv_rows = conv_backward(
        ints, glu, rim, depth_low, depth_rim, small_t, gated, conv_in_w, after_att, upstream
    )
    near, far, home, grad_bias, *att_grads = att_backward(
        fast, upstream, n2, dgated, keys, mixed, weights, kv, queries, tw, pos_w, own_turn, table
    )
    near = swap(near, "heads", 1)
    far = swap((far.astype(F32) + near[1].astype(F32)).astype(BF), "heads", 2)
    grad_bias = xor_order(grad_bias, head_index).reshape(pairs, 2, 2, head_dim).transpose(0, 2, 1, 3)
    grad_bias = grad_bias.reshape(pairs, 2, batches, channels).transpose(1, 2, 0, 3).reshape(2, model_width)
    again = ffn1_again(behind(frames_in, near), x1, win, wout, small_t)
    if fast:
        heard = swap(att_grads[1], "heads", 1)
        home = behind(home, heard)
        t = Exchange(att_grads[0], heard, steps_attention())
        t.send()
    frames_grad, *first_grads = ffn1_backward(
        fast, again, upstream, home, near, far, small_t, conv_rows, mid_rows, grad_bias
    )

    if fast:
        *first_grads, t.terms[-1] = lax.optimization_barrier((*first_grads, t.terms[-1]))
        own_ffn2_a, own_ffn2_b, own_conv_b = finish_middle(mid)
        a_far, a_own, b_far, b_own = first_grads
        a = Exchange(a_own, swap(a_far, "heads", 1), steps_first("xy"))
        b = Exchange(b_own, swap(b_far, "heads", 1), steps_first("yx"))
        t.terms[-1] = behind(t.terms[-1], mid)
        for group in ((a, b, t), (a, b, t), (a, b, t), (a, b)):
            heard = lax.optimization_barrier(tuple(g.terms[-1] for g in group))
            for g, last in zip(group, heard, strict=True):
                g.terms[-1] = last
                g.send()
        own_proj, own_out, own_conv_a = finish_attention(t.terms)
        own_ffn1_a, own_ffn1_b, own_taps, own_gain, own_bias, own_pos = finish_first(a.terms, b.terms)
    else:

        def to_rows(chunks):
            rows = chunks.shape[1]
            return sum_rows(chunks.transpose(1, 0, 2).reshape(rows, -1))

        own_ffn2_a = to_rows(mid_grads[0])
        own_ffn2_b = sum_rows(mid_grads[1].reshape(-1, model_width))
        own_conv_b = sum_rows(mid_grads[2])
        tw_grad, pos_grad, conv_grad = att_grads
        own_conv_a = sum_rows(conv_grad)
        pos_grad = pos_grad.reshape(pairs, 2, batches, width // 2, 128).transpose(0, 2, 1, 3, 4)
        grad_att = jnp.concatenate([tw_grad, pos_grad.reshape(pairs, model_width, 128)], axis=2)
        grad_att = xor_order(grad_att, head_index).astype(F32)
        own_att = lax.psum_scatter(
            lax.psum_scatter(grad_att, "batch", scatter_dimension=1, tiled=True),
            "heads",
            scatter_dimension=0,
            tiled=True,
        )[0]
        own_ffn1_a, own_ffn1_b = to_rows(first_grads[0]), sum_rows(first_grads[1])
        own_small = sum_rows(first_grads[2])
        own_small = own_small.T
        turned = own_att[:, 512:640].reshape(2, width // 2, 128).transpose(1, 0, 2).reshape(width, 128)
        parts = jnp.stack([own_att[:, :128], own_att[:, 128:256], own_att[:, 256:384], turned], axis=1)
        own_proj = parts.reshape(width, 4, 2, head_dim).transpose(2, 0, 1, 3)
        own_proj = own_proj.reshape(2, width, 4 * head_dim)
        own_out = own_att[:, 384:512].T.reshape(2, head_dim, width)
        own_pos = own_small[POS_BIAS : POS_BIAS + 2]
        own_taps = own_small[:kernel_len]
        own_gain, own_bias = own_small[GAIN : GAIN + 6], own_small[BIAS : BIAS + 6]
    return (
        layer_out,
        frames_grad,
        own_ffn1_a,
        own_ffn1_b,
        own_proj,
        own_out,
        own_pos,
        own_conv_a,
        own_taps,
        own_conv_b,
        own_ffn2_a,
        own_ffn2_b,
        own_gain,
        own_bias,
    )


def solution(mesh):
    placed = (
        P(("batch", "heads"), None),
        P(("batch", "heads"), None),
        P(),
        P(),
        P(("batch", "heads"), None),
        P(("batch", "heads"), None),
        P("heads", "batch", None),
        P("heads", None, "batch"),
        P("heads", "batch"),
        P(("batch", "heads"), None),
        P(None, ("batch", "heads")),
        P(("batch", "heads"), None),
        P(("batch", "heads"), None),
        P(("batch", "heads"), None),
        P(None, ("batch", "heads")),
        P(None, ("batch", "heads")),
    )
    return jax.shard_map(
        local,
        mesh=mesh,
        in_specs=placed,
        out_specs=(
            P(("batch", "heads"), None),
            P(("batch", "heads"), None),
            P(("batch", "heads"), None),
            P(("batch", "heads"), None),
            P("heads", "batch", None),
            P("heads", None, "batch"),
            P("heads", "batch"),
            P(("batch", "heads"), None),
            P(None, ("batch", "heads")),
            P(("batch", "heads"), None),
            P(("batch", "heads"), None),
            P(("batch", "heads"), None),
            P(None, ("batch", "heads")),
            P(None, ("batch", "heads")),
        ),
        check_vma=False,
    )
```

```python
import math

import jax
import jax.numpy as jnp
from jax import lax
from jax.experimental import pallas as pl
from jax.experimental.pallas import tpu as pltpu
from jax.sharding import PartitionSpec as P

epsilon = 1e-05
BF = jnp.bfloat16
F32 = jnp.float32
BOTH = ("batch", "heads")
CHUNK = 256
HALO = 16
SCALE = 0.125
LOG2E = 1.4426950408889634
GAIN, BIAS, POS_BIAS = 32, 38, 44
KZ = (0, 2, 1, 3)
DIMS = {"y": ("batch", 1), "x": ("heads", 2)}
VMEM_BYTES = 40 * 2**20


def swap(source, axis, mask):
    count = lax.axis_size(axis)
    return lax.ppermute(source, axis, [(i, i ^ mask) for i in range(count)])


def sum_over(source, axis):
    mask = 1
    while mask < lax.axis_size(axis):
        source = source + swap(source, axis, mask)
        mask *= 2
    return source


def halo(cells):
    ends = lax.axis_size("heads") - 1
    rows = cells.shape[0]
    before = lax.ppermute(cells[rows - HALO :], "heads", [(i, i + 1) for i in range(ends)])
    after = lax.ppermute(cells[:HALO], "heads", [(i + 1, i) for i in range(ends)])
    return before, after


def behind(source, *others):
    return lax.optimization_barrier((source,) + others)[0]


def gather_depth(shard):
    held = shard[None]
    for mask in (4, 2):
        held = jnp.concatenate([held, swap(held, "batch", mask)])
    return held


class Exchange:
    def __init__(self, own, heard, steps):
        self.terms, self.steps = [own, heard], list(steps)

def send_all(group):
    inputs, specs, outs, sizes = [], [], [], []
    for one in group:
        parts = one.steps[0][0]
        for term, index in zip(one.terms, parts, strict=True):
            index = index + (slice(None),) * (term.ndim - len(index))
            ends = [(k, 1) if isinstance(k, int) else (k.start // 2, 2) if k.start else (0, n) for k, n in zip(index, term.shape)]
            specs.append(pl.BlockSpec(tuple(e[1] for e in ends), lambda *_, at=tuple(e[0] for e in ends): at))
            inputs.append(term)
        shape = [2 if k.start else n for k, n in zip(index, term.shape) if not isinstance(k, int)]
        outs.append(shaped(tuple(shape), BF))
        sizes.append(len(parts))

    def kernel(*refs):
        at = 0
        for size, out_ref in zip(sizes, refs[-len(outs) :], strict=True):
            value = refs[at][...].reshape(out_ref.shape).astype(F32)
            for ref in refs[at + 1 : at + size]:
                value = value + ref[...].reshape(out_ref.shape).astype(F32)
            out_ref[...] = value.astype(BF)
            at += size

    moving = run(kernel, inputs, outs, "send_all", specs=specs, grid=(1,), limit=24)
    for one, array in zip(group, moving, strict=True):
        _, axis, mask = one.steps.pop(0)
        one.terms.append(swap(array, axis, mask))


def steps_first(order):
    one, two = DIMS[order[0]], DIMS[order[1]]
    return [
        ([(1,), (1,)],) + one,
        ([(0, 1), (0, 1), (1,)],) + two,
        ([(0, 0, slice(2, 4)), (0, 0, slice(2, 4)), (0, slice(2, 4)), (slice(2, 4),)],) + ("batch", 2),
        ([(0, 0, 1), (0, 0, 1), (0, 1), (1,), (1,)],) + ("batch", 4),
    ]


def steps_attention():
    high = slice(2, 4)
    return [
        ([(1,), (1,)], "batch", 1),
        ([(0, high), (0, high), (high,)], "batch", 2),
        ([(0, 1), (0, 1), (1,), (1,)], "batch", 4),
        ([(0, 0, 1), (0, 0, 1), (0, 1), (0, 1), (1,)], "heads", 2),
    ]


def dot(left, right):
    return jnp.dot(left, right, preferred_element_type=F32)


def dot_nt(left, right):
    return lax.dot_general(left, right, (((1,), (1,)), ((), ())), preferred_element_type=F32)


def dot_tn(left, right):
    return lax.dot_general(left, right, (((0,), (0,)), ((), ())), preferred_element_type=F32)


def norm(source):
    center = source - jnp.mean(source, axis=-1, keepdims=True)
    scale = lax.rsqrt(jnp.mean(center * center, axis=-1, keepdims=True) + epsilon)
    return center * scale, scale


def norm_back(upstream, normed, scale, gain_row):
    inner = upstream * gain_row
    mean = jnp.mean(inner, axis=-1, keepdims=True)
    along = jnp.mean(inner * normed, axis=-1, keepdims=True)
    gain_grad = jnp.sum(upstream * normed, axis=0, keepdims=True)
    return scale * (inner - mean - normed * along), gain_grad, jnp.sum(upstream, axis=0, keepdims=True)


def row(small_ref, index):
    return small_ref[index : index + 1, :]


def place():
    batch_at = lax.axis_index("batch")
    heads_at = lax.axis_index("heads")
    return batch_at // 2, batch_at % 2, heads_at // 2, heads_at % 2


def block_index(kz, ky, kx, kc):
    z, y, x, c = place()
    return ((z ^ kz) * 2 + (y ^ ky)) * 4 + (x ^ kx) * 2 + (c ^ kc)


def part(index, size):
    return pl.ds(pl.multiple_of(index * size, size), size)


def valid_rows(ints_ref, rows):
    steps = lax.broadcasted_iota(jnp.int32, (rows, 1), 0) + ints_ref[1]
    return (steps < ints_ref[0]).astype(F32)


def whole(array):
    return pl.BlockSpec(array.shape, lambda *_: (0,) * len(array.shape), pipeline_mode=pl.Buffered(1))


def per_pair(array):
    return pl.BlockSpec((1,) + array.shape[1:], lambda h: (h,) + (0,) * (len(array.shape) - 1))


def shaped(shape, kind):
    return jax.ShapeDtypeStruct(shape, kind)


SMEM = pl.BlockSpec(memory_space=pltpu.SMEM)


VMEM = pl.BlockSpec(memory_space=pltpu.VMEM)


def cost(time):
    return pl.CostEstimate(flops=int(time * 10**9), bytes_accessed=2**12, transcendentals=0)


def run(kernel, inputs, outs, name, specs=None, grid=(), scratch=(), limit=24, time=0.01):
    return pl.pallas_call(
        kernel,
        grid=grid,
        in_specs=specs or [VMEM] * len(inputs),
        out_specs=[whole(o) for o in outs] if grid else [VMEM] * len(outs),
        out_shape=outs,
        scratch_shapes=list(scratch),
        compiler_params=pltpu.CompilerParams(vmem_limit_bytes=limit * 2**20),
        cost_estimate=cost(time),
        name=name,
    )(*inputs)


def fetch(*arrays):
    def kernel(*refs):
        count = len(arrays)
        copies = [pltpu.make_async_copy(refs[i], refs[count + i], refs[-1].at[i]) for i in range(count)]
        for copy in copies:
            copy.start()
        for copy in copies:
            copy.wait()

    return run(
        kernel,
        list(arrays),
        [shaped(a.shape, a.dtype) for a in arrays],
        "fetch",
        specs=[pl.BlockSpec(memory_space=pltpu.HBM)] * len(arrays),
        scratch=[pltpu.SemaphoreType.DMA((len(arrays),))],
    )


def place_first(sets_a, sets_b):
    def kernel(*refs):
        a_refs, b_refs = refs[:4], refs[4:8]
        win_ref, wout_ref, small_ref, pb_ref, chan_ref, stage_ref = refs[8:]
        for k in range(4):
            for i in range(8):
                at = block_index(KZ[i % 4], i // 4, k & 1, k >> 1)
                for column in range(4):
                    win_ref[column, part(at, 16), :] = a_refs[k][i, :, 512 * column : 512 * column + 512]
                at = block_index(KZ[i % 4], k & 1, i // 4, k >> 1)
                wout_ref[part(at, 64), :] = b_refs[k][i, 0:64, :]
                small = b_refs[k][i, 64:72, 0:256].astype(F32)
                chan_ref[part(at, 16), :] = jnp.concatenate([small[:, 0:128], small[:, 128:256]], axis=0)
        small_ref[...] = chan_ref[...].T
        for mask in range(4):
            pair = lax.axis_index("heads") ^ mask
            for b in range(8):
                stage_ref[16 * b : 16 * b + 16, :] = chan_ref[part(4 * b + pair, 16), :]
            one, two = (stage_ref[...].T[at : at + 1] for at in (POS_BIAS, POS_BIAS + 1))
            pb_ref[mask, 0:1, :] = jnp.concatenate([one[:, :64], two[:, :64]], axis=1)
            pb_ref[mask, 1:2, :] = jnp.concatenate([one[:, 64:], two[:, 64:]], axis=1)

    return run(
        kernel,
        list(sets_a) + list(sets_b),
        [shaped((4, 512, 512), BF), shaped((2048, 512), BF), shaped((128, 512), F32), shaped((4, 2, 128), F32)],
        "place_first",
        scratch=[pltpu.VMEM((512, 128), F32), pltpu.VMEM((128, 128), F32)],
    )


def place_attention(sets):
    def kernel(*refs):
        tw_ref, pos_ref = refs[4:]
        z, y, _, _ = place()
        for k in range(4):
            for i in range(8):
                pair = (i % 2) * 2 + (k >> 1)
                at = (z ^ KZ[i // 2]) * 2 + (y ^ (k & 1))
                tw_ref[pair, part(at, 64), :] = refs[k][i, :, 0:512]
                pos_ref[pair, part(at, 32), :] = refs[k][i, 0:32, 512:640]
                pos_ref[pair, part(at + 8, 32), :] = refs[k][i, 32:64, 512:640]

    return run(
        kernel, list(sets), [shaped((4, 512, 512), BF), shaped((4, 512, 128), BF)], "place_attention"
    )


def ffn1_forward(frames, win, wout, small):
    def kernel(x_ref, win_ref, wout_ref, small_ref, out_ref, normed_ref):
        source = x_ref[...].astype(F32)
        normed, _ = norm(source)
        pre = (normed * row(small_ref, GAIN) + row(small_ref, BIAS)).astype(BF)
        total = jnp.zeros_like(source)
        for column in range(win_ref.shape[0]):
            hidden = dot(pre, win_ref[column])
            active = (hidden * jax.nn.sigmoid(hidden)).astype(BF)
            total = total + dot(active, wout_ref[512 * column : 512 * column + 512, :])
        source = source + 0.5 * total
        out_ref[...] = source
        normed, _ = norm(source)
        normed_ref[...] = (normed * row(small_ref, GAIN + 1) + row(small_ref, BIAS + 1)).astype(BF)

    return run(
        kernel,
        [frames, win, wout, small],
        [shaped(frames.shape, F32), shaped(frames.shape, BF)],
        "ffn1_forward",
        time=3,
    )


def halves(first, value):
    zero = jnp.zeros_like(value)
    return jnp.where(first, value, zero), jnp.where(first, zero, value)


def att_forward_kernel(
    mask_ref, own_ref, k1_ref, k2_ref, k3_ref, x1_ref, small_ref, tw_ref, pos_ref, pb_ref, cs_ref, et_ref,
    w_ref, o_ref, scale_ref, kv_ref, q_ref, att_ref, n2_ref, right_ref, value_ref, total_ref,
):
    rows, width = own_ref.shape
    half = cs_ref.shape[2]
    step = pl.program_id(0)
    tw = tw_ref[0]

    @pl.when(step == 0)
    def _():
        right_ref[0:width, :] = et_ref[...]
        value_ref[:, 128:256] = jnp.ones((value_ref.shape[0], 128), BF)
        total_ref[...] = x1_ref[...]

    for k, ref in enumerate((own_ref, k1_ref, k2_ref, k3_ref)):
        here = slice(k * rows, k * rows + rows)
        kv = dot(ref[...], tw[:, 128:384])
        kv_ref[0, here, :] = kv.astype(BF)
        right_ref[width : width + 128, here] = kv[:, :128].T.astype(BF)
    value_ref[:, 0:128] = kv_ref[0, :, 128:]
    query = dot(own_ref[...], tw[:, :128])
    qc = (query + pb_ref[0, 0:1, :]).astype(BF)
    qp = (query + pb_ref[0, 1:2, :]).astype(BF)
    q_ref[0, 0] = qc
    q_ref[0, 1] = qp
    first = lax.broadcasted_iota(jnp.int32, (rows, 128), 1) < 64
    cos, sin = cs_ref[0], cs_ref[1]
    mask = mask_ref[...]
    outs = []
    for qc_h, qp_h in zip(halves(first, qc), halves(first, qp)):
        turned = dot_nt(qp_h, pos_ref[0]) * (SCALE * LOG2E)
        us, uc = turned[:, :half], turned[:, half:]
        left = jnp.concatenate(
            [
                (us * cos + uc * sin).astype(BF),
                (uc * cos - us * sin).astype(BF),
                (qc_h.astype(F32) * (SCALE * LOG2E)).astype(BF),
            ],
            axis=1,
        )
        parts = []
        for r in range(0, rows, CHUNK):
            scores = dot(left[r : r + CHUNK], right_ref[...]) + mask
            top = jnp.max(scores, axis=1, keepdims=True)
            weights = jnp.exp2(scores - top).astype(BF)
            w_ref[0, len(outs), r : r + CHUNK, :] = weights
            parts.append(dot(weights, value_ref[...]))
        outs.append(jnp.concatenate(parts, axis=0))
    scale = 1.0 / jnp.where(first, outs[0][:, 128:], outs[1][:, 128:])
    scale_ref[0] = scale
    mixed = jnp.where(first, outs[0][:, :128], outs[1][:, :128]) * scale
    o_ref[0] = mixed
    total_ref[...] += dot_nt(mixed.astype(BF), tw[:, 384:512])

    @pl.when(step == pl.num_programs(0) - 1)
    def _():
        after = total_ref[...]
        att_ref[...] = after
        normed, _ = norm(after)
        n2_ref[...] = (normed * row(small_ref, GAIN + 2) + row(small_ref, BIAS + 2)).astype(BF)


def att_forward(mask, keys, x1, small, tw, pos, pb, cs, et):
    rows, width = x1.shape
    count = mask.shape[1]
    paired = [
        shaped((4, 2, rows, count), BF),
        shaped((4, rows, 128), F32),
        shaped((4, rows, 128), F32),
        shaped((4, count, 256), BF),
        shaped((4, 2, rows, 128), BF),
    ]
    shared = [shaped((rows, width), F32), shaped((rows, width), BF)]
    return pl.pallas_call(
        att_forward_kernel,
        grid=(4,),
        in_specs=[whole(mask)]
        + [whole(k) for k in keys]
        + [whole(x1), whole(small), per_pair(tw), per_pair(pos), per_pair(pb), whole(cs), whole(et)],
        out_specs=[per_pair(a) for a in paired] + [whole(a) for a in shared],
        out_shape=paired + shared,
        scratch_shapes=[
            pltpu.VMEM((width + 128, count), BF),
            pltpu.VMEM((count, 256), BF),
            pltpu.VMEM((rows, width), F32),
        ],
        compiler_params=pltpu.CompilerParams(vmem_limit_bytes=56 * 2**20),
        cost_estimate=cost(40),
        name="att_forward",
    )(mask, *keys, x1, small, tw, pos, pb, cs, et)


def att_backward_kernel(fast, *refs):
    (up_ref, n2_ref, dg_ref, own_ref, k1_ref, k2_ref, k3_ref, o_ref, scale_ref, w_ref, kv_ref, q_ref, tw_ref, pos_ref, cs_ref,
     e_ref, near_ref, far_ref, home_ref, db_ref) = refs[:20]
    outs, (dr_ref, dn_ref, dq_ref, og_ref, dconv_ref, tw_grad_ref, pos_grad_ref) = refs[20:-7], refs[-7:]
    rows, width = up_ref.shape
    half = cs_ref.shape[2]
    count = dn_ref.shape[1]
    step = pl.program_id(0)

    @pl.when(step == 0)
    def _():
        og_ref[...] = up_ref[...].astype(BF)
        dn_ref[...] = jnp.zeros_like(dn_ref)
        dq_ref[...] = jnp.zeros_like(dq_ref)
        dconv_ref[...] = dot_tn(n2_ref[...], dg_ref[...]).astype(BF)

    og = og_ref[...]
    tw = tw_ref[0]
    do_f = dot(og, tw[:, 384:512]).astype(BF).astype(F32) * scale_ref[0]
    do = do_f.astype(BF)
    key, value = kv_ref[0, :, :128], kv_ref[0, :, 128:]
    first = lax.broadcasted_iota(jnp.int32, (rows, 128), 1) < 64
    mixed = o_ref[0]
    do_t = do_f.T.astype(BF)
    qc_t = (q_ref[0, 0].astype(F32) * SCALE).T.astype(BF)
    qp_t = q_ref[0, 1].astype(F32).T.astype(BF)
    cos, sin = cs_ref[0], cs_ref[1]
    dqcs, dqps, dks, dvs, dps = [], [], [], [], []
    for head, (do_h, inner_h) in enumerate(zip(halves(first, do), halves(first, do_f * mixed))):
        mine = slice(head * 64, head * 64 + 64)
        inner = jnp.sum(inner_h, axis=1, keepdims=True)
        for r in range(0, rows, CHUNK):
            dw = dot_nt(do_h[r : r + CHUNK], value)
            weights = w_ref[0, head, r : r + CHUNK, :].astype(F32)
            dr_ref[r : r + CHUNK, :] = (weights * (dw - inner[r : r + CHUNK])).astype(BF)
        dr = dr_ref[...]
        turned = dot(dr, e_ref[...]) * SCALE
        dqcs.append(dot(dr, key) * SCALE)
        dks.append(dot(qc_t[mine], dr).astype(BF))
        dvs.append(dot(do_t[mine], w_ref[0, head]).astype(BF))
        gs, gc = turned[:, :half], turned[:, half:]
        du = jnp.concatenate(
            [(gs * cos - gc * sin).astype(BF), (gs * sin + gc * cos).astype(BF)], axis=1
        )
        dqps.append(dot(du, pos_ref[0]))
        dps.append(dot(qp_t[mine], du))
    dqc = jnp.where(first, dqcs[0], dqcs[1])
    dqp = jnp.where(first, dqps[0], dqps[1])
    db_ref[0, 0:1, :] = jnp.sum(dqc, axis=0, keepdims=True)
    db_ref[0, 1:2, :] = jnp.sum(dqp, axis=0, keepdims=True)
    dq = dqc + dqp
    dq_low = dq.astype(BF)
    dkv = jnp.concatenate(dks + dvs, axis=0)
    dn_ref[...] += dot(tw[:, 128:384], dkv)
    dq_ref[...] += dot_nt(dq_low, tw[:, :128])
    grad_kv = jnp.zeros((256, width), F32)
    for k, ref in enumerate((own_ref, k1_ref, k2_ref, k3_ref)):
        grad_kv = grad_kv + dot(dkv[:, k * rows : k * rows + rows], ref[...])
    grad_q = dot(dq.T.astype(BF), own_ref[...])
    grad_o = dot(mixed.T.astype(BF), og)
    tw_grad_ref[...] = jnp.concatenate([grad_q, grad_kv, grad_o], axis=0).T.astype(BF)
    pos_grad_ref[...] = jnp.concatenate(dps, axis=0).T.astype(BF)

    if fast:
        z, y, x, c = place()
        pair = (x ^ (step // 2)) * 2 + (c ^ (step % 2))

        def write(pack_ref):
            for ky in range(2):
                for i in range(4):
                    at = (z ^ KZ[i]) * 2 + (y ^ ky)
                    pack_ref[ky, i, 0, :, 0:512] = tw_grad_ref[part(at, 64), :]
                    pack_ref[ky, i, 0, 0:32, 512:640] = pos_grad_ref[part(at, 32), :]
                    pack_ref[ky, i, 0, 32:64, 512:640] = pos_grad_ref[part(at + 8, 32), :]
                    for t in range(4):
                        pack_ref[ky, i, 0, 16 * t : 16 * t + 16, 640:896] = dconv_ref[
                            part(at * 4 + pair, 16), 256 * t : 256 * t + 256
                        ]

        pl.when(step % 2 == 0)(lambda: write(outs[0]))
        pl.when(step % 2 == 1)(lambda: write(outs[1]))
    else:
        outs[0][0] = tw_grad_ref[...]
        outs[1][0] = pos_grad_ref[...]
        outs[2][...] = dconv_ref[...]

    @pl.when(step == pl.num_programs(0) - 1)
    def _():
        for k in range(4):
            grad = dn_ref[:, k * rows : k * rows + rows].T
            if k == 0:
                home_ref[...] = grad + dq_ref[...]
            elif k == 2:
                far_ref[...] = grad.astype(BF)
            else:
                near_ref[k // 2] = grad.astype(BF)


def att_backward(fast, upstream, n2, dgated, keys, mixed, scale, weights, kv, queries, tw, pos, cs, e):
    rows, width = upstream.shape
    count = kv.shape[1]
    shared = [shaped((2, rows, width), BF), shaped((rows, width), BF), shaped((rows, width), F32)]
    paired = [shaped((4, 2, 128), F32)]
    specs = [whole(a) for a in shared] + [per_pair(a) for a in paired]
    outs = shared + paired
    if fast:
        extra = [shaped((2, 4, 2, 64, 896), BF)] * 2
        specs += [pl.BlockSpec((2, 4, 1, 64, 896), lambda h: (0, 0, h // 2, 0, 0))] * 2
    else:
        extra = [shaped((4, width, 512), BF), shaped((4, width, 128), BF), shaped((width, 1024), BF)]
        specs += [per_pair(extra[0]), per_pair(extra[1]), whole(extra[2])]
    return pl.pallas_call(
        lambda *refs: att_backward_kernel(fast, *refs),
        grid=(4,),
        in_specs=[whole(upstream), whole(n2), whole(dgated)]
        + [whole(k) for k in keys]
        + [per_pair(mixed), per_pair(scale), per_pair(weights), per_pair(kv), per_pair(queries), per_pair(tw), per_pair(pos)]
        + [whole(cs), whole(e)],
        out_specs=specs,
        out_shape=outs + extra,
        scratch_shapes=[
            pltpu.VMEM((rows, count), BF),
            pltpu.VMEM((width, count), F32),
            pltpu.VMEM((rows, width), F32),
            pltpu.VMEM((rows, width), BF),
            pltpu.VMEM((width, 1024), BF),
            pltpu.VMEM((width, 512), BF),
            pltpu.VMEM((width, 128), BF),
        ],
        compiler_params=pltpu.CompilerParams(vmem_limit_bytes=VMEM_BYTES),
        cost_estimate=cost(0.01),
        name="att_backward",
    )(upstream, n2, dgated, *keys, mixed, scale, weights, kv, queries, tw, pos, cs, e)


def gate_forward(ints, n2, conv_in):
    rows, width = n2.shape

    def kernel(ints_ref, n2_ref, *refs):
        w_refs, (glu_ref, gated_ref, a_ref, b_ref) = refs[:2], refs[2:]
        a_ref[...] = w_refs[0][...].reshape(width, width)
        b_ref[...] = w_refs[1][...].reshape(width, width)
        left = dot(n2_ref[...], a_ref[...])
        right = dot(n2_ref[...], b_ref[...])
        gated_ref[:, :width] = left
        gated_ref[:, width:] = right
        glu_ref[...] = (left * jax.nn.sigmoid(right) * valid_rows(ints_ref, rows)).astype(BF)

    if len(conv_in) == 1:
        conv_in = conv_in * 2
        specs = [
            pl.BlockSpec((32, 16, 512), lambda *_, at=at: (0, at, 0), pipeline_mode=pl.Buffered(1)) for at in (8, 9)
        ]
    else:
        specs = [whole(a) for a in conv_in]
    return run(
        kernel,
        [ints, n2] + conv_in,
        [shaped((rows, width), BF), shaped((rows, 2 * width), F32)] + [shaped((width, width), BF)] * 2,
        "gate_forward",
        specs=[SMEM, whole(n2)] + specs,
        grid=(1,),
        limit=60,
    )


def extend(ext_ref, before_ref, own_ref, after_ref):
    rows = own_ref.shape[0]
    ext_ref[0, 0:HALO, :] = before_ref[...].astype(F32)
    ext_ref[0, HALO : HALO + rows, :] = own_ref[...].astype(F32)
    ext_ref[0, HALO + rows : 2 * HALO + rows, :] = after_ref[...].astype(F32)
    kept = 2 * HALO + rows - 8
    for shift in range(1, 8):
        ext_ref[shift, 0:kept, :] = ext_ref[0, shift : shift + kept, :]


def shifted(ext_ref, start, size, columns):
    return ext_ref[start % 8, start - start % 8 : start - start % 8 + size, columns]


def conv_forward(ints, glu, rim, small):
    rows, width = glu.shape

    def kernel(ints_ref, before_ref, glu_ref, after_ref, small_ref, depth_ref, sums_ref, ext_ref):
        extend(ext_ref, before_ref, glu_ref, after_ref)
        steps = lax.broadcasted_iota(jnp.int32, (64, 1), 0) + ints_ref[1]
        for c in range(0, width, 128):
            one = jnp.zeros((1, 128), F32)
            two = jnp.zeros((1, 128), F32)
            for r in range(0, rows, 64):
                total = jnp.zeros((64, 128), F32)
                for k in range(2 * HALO):
                    total = total + shifted(ext_ref, r + k + 1, 64, slice(c, c + 128)) * small_ref[k : k + 1, c : c + 128]
                depth_ref[r : r + 64, c : c + 128] = total
                kept = jnp.where(steps + r < ints_ref[0], total, 0.0)
                one = one + jnp.sum(kept, axis=0, keepdims=True)
                two = two + jnp.sum(kept * total, axis=0, keepdims=True)
            sums_ref[0:1, c : c + 128] = one
            sums_ref[1:2, c : c + 128] = two

    return run(
        kernel,
        [ints, rim[0], glu, rim[1], small],
        [shaped((rows, width), F32), shaped((2, width), F32)],
        "conv_forward",
        time=4,
        specs=[SMEM] + [VMEM] * 4,
        scratch=[pltpu.VMEM((8, rows + 2 * HALO, width), F32)],
    )


def conv_backward(ints, glu, rim, depth_low, depth_rim, small, gated, conv_in, after_att, upstream):
    rows, width = glu.shape

    def kernel(
        ints_ref, gb_ref, glu_ref, ga_ref, db_ref, d_ref, da_ref, small_ref, gated_ref, att_ref, up_ref, *refs
    ):
        w_refs, (out_ref, dg_ref, grads_ref, ext_ref, extd_ref, dglu_ref) = refs[:-6], refs[-6:]
        extend(ext_ref, gb_ref, glu_ref, ga_ref)
        extend(extd_ref, db_ref, d_ref, da_ref)
        taps = 2 * HALO
        for c in range(0, width, 128):
            cols = slice(c, c + 128)
            for r in range(0, rows, 64):
                total = jnp.zeros((64, 128), F32)
                for k in range(taps):
                    at = r + taps - 1 - k
                    total = total + shifted(extd_ref, at, 64, cols) * small_ref[k : k + 1, cols]
                dglu_ref[r : r + 64, cols] = total
            for k in range(taps):
                total = jnp.zeros((8, 128), F32)
                for r in range(0, rows, 64):
                    product = shifted(ext_ref, r + k + 1, 64, cols) * shifted(extd_ref, HALO + r, 64, cols)
                    total = total + jnp.sum(product.reshape(8, 8, 128), axis=0)
                grads_ref[k : k + 1, cols] = jnp.sum(total, axis=0, keepdims=True)
        grad = dglu_ref[...] * valid_rows(ints_ref, rows)
        gate = jax.nn.sigmoid(gated_ref[:, width:])
        left = (grad * gate).astype(BF)
        right = (grad * gated_ref[:, :width] * gate * (1.0 - gate)).astype(BF)
        dg_ref[:, :width] = left
        dg_ref[:, width:] = right
        inner = dot_nt(left, w_refs[0][...]) + dot_nt(right, w_refs[1][...])
        normed, scale = norm(att_ref[...])
        grad, gain_grad, bias_grad = norm_back(inner, normed, scale, row(small_ref, GAIN + 2))
        out_ref[...] = up_ref[...] + grad
        grads_ref[taps : taps + 1, :] = gain_grad
        grads_ref[taps + 1 : taps + 2, :] = bias_grad

    inputs = [ints, rim[0], glu, rim[1], depth_rim[0], depth_low, depth_rim[1], small, gated]
    return run(
        kernel,
        inputs + [after_att, upstream] + conv_in,
        [shaped((rows, width), F32), shaped((rows, 2 * width), BF), shaped((40, width), F32)],
        "conv_backward",
        time=0.01,
        specs=[SMEM] + [VMEM] * (len(inputs) + 1 + len(conv_in)),
        scratch=[pltpu.VMEM((8, rows + 2 * HALO, width), F32)] * 2 + [pltpu.VMEM((rows, width), F32)],
    )


def middle(ints, floats, depth, sums, after_att, cotangent, small, weights):
    rows, width = depth.shape

    def kernel(
        ints_ref, floats_ref, depth_ref, sums_ref, att_ref, cot_ref, small_ref, *refs
    ):
        w_refs = refs[:-12]
        (layer_ref, up_ref, raw_ref, gsum_ref, grads_ref, pre_ref, act_ref, dhid_ref, branch_ref, swish_ref, low_ref,
         hid_ref) = refs[-12:]
        packed = len(w_refs) == 1
        columns = hid_ref.shape[0]

        def w_in(column):
            if packed:
                return w_refs[0][:, 16 * column : 16 * column + 16, :].reshape(width, 512)
            return w_refs[0][column]

        def w_out(column):
            if packed:
                return w_refs[0][8 * column : 8 * column + 8, 64:128, :].reshape(512, width)
            return w_refs[1][column]

        total_valid = floats_ref[1]
        mean_bn = sums_ref[0:1, :] / total_valid
        var_bn = sums_ref[1:2, :] / total_valid - mean_bn * mean_bn
        inv = lax.rsqrt(var_bn + epsilon)
        center = depth_ref[...] - mean_bn
        bn_gain = row(small_ref, GAIN + 5)
        z = center * inv * bn_gain + row(small_ref, BIAS + 5)
        swish = (z * jax.nn.sigmoid(z)).astype(BF)
        swish_ref[...] = swish
        conv_out = w_refs[0][:, 160:176, :].reshape(width, width) if packed else w_refs[2][...]
        after_conv = att_ref[...] + dot(swish, conv_out)
        normed3, scale3 = norm(after_conv)
        pre = (normed3 * row(small_ref, GAIN + 3) + row(small_ref, BIAS + 3)).astype(BF)
        pre_ref[...] = pre
        total = jnp.zeros((rows, width), F32)
        for column in range(columns):
            hidden = dot(pre, w_in(column))
            hid_ref[column] = hidden
            active = (hidden * jax.nn.sigmoid(hidden)).astype(BF)
            act_ref[column] = active
            total = total + dot(active, w_out(column))
        normed4, scale4 = norm(after_conv + 0.5 * total)
        gain4 = row(small_ref, GAIN + 4)
        layer_ref[...] = (normed4 * gain4 + row(small_ref, BIAS + 4)).astype(BF)
        seed = cot_ref[...].astype(F32) * (valid_rows(ints_ref, rows) * floats_ref[0])
        up, gain_grad, bias_grad = norm_back(seed, normed4, scale4, gain4)
        grads_ref[...] = jnp.zeros_like(grads_ref)
        grads_ref[2:3, :] = gain_grad
        grads_ref[3:4, :] = bias_grad
        branch = (0.5 * up).astype(BF)
        branch_ref[...] = branch
        total = jnp.zeros((rows, width), F32)
        for column in range(columns):
            hidden = hid_ref[column]
            gate = jax.nn.sigmoid(hidden)
            grad = dot_nt(branch, w_out(column)) * (gate * (1.0 + hidden * (1.0 - gate)))
            grad = grad.astype(BF)
            dhid_ref[column] = grad
            total = total + dot_nt(grad, w_in(column))
        grad, gain_grad, bias_grad = norm_back(total, normed3, scale3, row(small_ref, GAIN + 3))
        grads_ref[0:1, :] = gain_grad
        grads_ref[1:2, :] = bias_grad
        up = up + grad
        up_ref[...] = up
        low = up.astype(BF)
        low_ref[...] = low
        gate = jax.nn.sigmoid(z)
        dz = dot_nt(low, conv_out) * (gate * (1.0 + z * (1.0 - gate)))
        grads_ref[4:5, :] = jnp.sum(dz * center, axis=0, keepdims=True) * inv
        grads_ref[5:6, :] = jnp.sum(dz, axis=0, keepdims=True)
        raw = dz * (bn_gain * inv)
        raw_ref[...] = raw
        gsum_ref[0:1, :] = -jnp.sum(raw, axis=0, keepdims=True)
        gsum_ref[1:2, :] = jnp.sum(raw * center, axis=0, keepdims=True) * (-0.5 * inv * inv)

    square_f, square = shaped((rows, width), F32), shaped((rows, width), BF)
    wide = shaped((4, rows, 512), BF)
    inputs = [ints, floats, depth, sums, after_att, cotangent, small]
    return run(
        kernel,
        inputs + weights,
        [square, square_f, square_f, shaped((2, width), F32), shaped((8, width), F32)]
        + [square, wide, wide, square, square, square],
        "middle",
        time=8,
        specs=[SMEM, SMEM] + [VMEM] * (len(inputs) - 2 + len(weights)),
        scratch=[pltpu.VMEM((4, rows, 512), F32)],
    )


def middle_grads(fast, pre, act, dhid, branch, swish, low):
    width = pre.shape[1]

    def kernel(pre_ref, act_ref, dhid_ref, branch_ref, swish_ref, low_ref, *outs):
        for column in range(act_ref.shape[0]):
            grad_in = dot_tn(pre_ref[...], dhid_ref[column]).astype(BF)
            grad_out = dot_tn(act_ref[column], branch_ref[...]).astype(BF)
            if fast:
                outs[0][:, 16 * column : 16 * column + 16, :] = grad_in.reshape(32, 16, 512)
                outs[0][8 * column : 8 * column + 8, 64:128, :] = grad_out.reshape(8, 64, 512)
            else:
                outs[0][column] = grad_in
                outs[1][column] = grad_out
        grad = dot_tn(swish_ref[...], low_ref[...]).astype(BF)
        if fast:
            outs[0][:, 128:144, :] = grad.reshape(32, 16, 512)
        else:
            outs[2][...] = grad

    if fast:
        outs = [shaped((32, 144, 512), BF)]
    else:
        outs = [shaped((4, width, 512), BF), shaped((4, 512, width), BF), shaped((width, width), BF)]
    return run(kernel, [pre, act, dhid, branch, swish, low], outs, "middle_grads", time=3)


def ffn1_again(frames, x1, win, wout, small):
    rows, width = x1.shape

    def kernel(
        x_in, x1_in, win_in, wout_in, small_ref, pre_ref, act_ref, slope_ref, x1_ref, x_ref, win_ref, wout_ref, sems
    ):
        pairs = ((x_in, x_ref), (win_in, win_ref), (x1_in, x1_ref), (wout_in, wout_ref))
        copies = [pltpu.make_async_copy(a, b, sems.at[k]) for k, (a, b) in enumerate(pairs)]
        for copy in copies:
            copy.start()
        copies[0].wait()
        normed, _ = norm(x_ref[...].astype(F32))
        pre = (normed * row(small_ref, GAIN) + row(small_ref, BIAS)).astype(BF)
        pre_ref[...] = pre
        copies[1].wait()
        for column in range(win.shape[0]):
            hidden = dot(pre, win_ref[column])
            gate = jax.nn.sigmoid(hidden)
            act_ref[column] = (hidden * gate).astype(BF)
            slope_ref[column] = gate * (1.0 + hidden * (1.0 - gate))
        copies[2].wait()
        copies[3].wait()

    wide = (win.shape[0], rows, 512)
    return run(
        kernel,
        [frames, x1, win, wout, small],
        [shaped((rows, width), BF), shaped(wide, BF), shaped(wide, F32), shaped(x1.shape, F32)]
        + [shaped(frames.shape, BF), shaped(win.shape, BF), shaped(wout.shape, BF)],
        "ffn1_again",
        time=0.01,
        specs=[pl.BlockSpec(memory_space=pltpu.HBM)] * 4 + [VMEM],
        scratch=[pltpu.SemaphoreType.DMA((4,))],
    )


def ffn1_backward(fast, again, upstream, home, near, far, small, conv_rows, mid_rows, grad_bias):
    pre, active, slope, x1, frames, win, wout = again
    rows, width = x1.shape

    def kernel(
        pre_ref, act_ref, slope_ref, x1_ref, x_ref, win_ref, wout_ref, up_ref, home_ref, near_ref, far_ref, small_ref,
        conv_ref, mid_ref, bias_ref,
        *refs,
    ):
        frames_ref, outs, (chan_ref, gin_ref, gout_ref) = refs[0], refs[1:-3], refs[-3:]
        dn = home_ref[...] + near_ref[0].astype(F32) + far_ref[...].astype(F32)
        normed, scale = norm(x1_ref[...])
        grad, gain1, bias1 = norm_back(dn, normed, scale, row(small_ref, GAIN + 1))
        up = up_ref[...] + grad
        branch = (0.5 * up).astype(BF)
        normed, scale = norm(x_ref[...].astype(F32))
        gain0 = row(small_ref, GAIN)
        pre = pre_ref[...]
        total = jnp.zeros((rows, width), F32)
        for column in range(win_ref.shape[0]):
            gout_ref[512 * column : 512 * column + 512, :] = dot_tn(act_ref[column], branch).astype(BF)
            grad = dot_nt(branch, wout_ref[512 * column : 512 * column + 512, :])
            grad = (grad * slope_ref[column]).astype(BF)
            gin_ref[column] = dot_tn(pre, grad).astype(BF)
            total = total + dot_nt(grad, win_ref[column])
        grad, gain_grad, bias_grad = norm_back(total, normed, scale, gain0)
        frames_ref[...] = (up + grad).astype(BF)
        chan_ref[...] = jnp.zeros_like(chan_ref)
        taps = GAIN
        chan_ref[0:taps, :] = conv_ref[0:taps, :]
        for first, at in ((GAIN, 0), (BIAS, 1)):
            chan_ref[first + 2 : first + 3, :] = conv_ref[taps + at : taps + at + 1, :]
            for k in range(3):
                chan_ref[first + 3 + k : first + 4 + k, :] = mid_ref[2 * k + at : 2 * k + at + 1, :]
        chan_ref[POS_BIAS : POS_BIAS + 2, :] = bias_ref[...]
        chan_ref[GAIN : GAIN + 1, :] = gain_grad
        chan_ref[GAIN + 1 : GAIN + 2, :] = gain1
        chan_ref[BIAS : BIAS + 1, :] = bias_grad
        chan_ref[BIAS + 1 : BIAS + 2, :] = bias1
        if fast:
            a_far, a_own, b_far, b_own = outs
            turned = chan_ref[...].T.astype(BF)
            for kc, a_out, b_out in ((1, a_far, b_far), (0, a_own, b_own)):
                for one in range(2):
                    for two in range(2):
                        for i in range(4):
                            at = block_index(KZ[i], two, one, kc)
                            for column in range(4):
                                a_out[one, two, i, 16 * column : 16 * column + 16, :] = gin_ref[
                                    column, part(at, 16), :
                                ]
                            at = block_index(KZ[i], one, two, kc)
                            b_out[one, two, i] = gout_ref[part(at, 64), :]
            gin_ref[0, :, 0:128] = turned
            for kc, a_out in ((1, a_far), (0, a_own)):
                for one in range(2):
                    for two in range(2):
                        for i in range(4):
                            at = block_index(KZ[i], two, one, kc)
                            own = gin_ref[0, part(at, 16), 0:128].astype(F32)
                            own = jnp.concatenate([own[0:8], own[8:16], jnp.zeros((8, 256), F32)], axis=1)
                            a_out[one, two, i, 64:72, :] = own.astype(BF)
        else:
            outs[0][...] = gin_ref[...]
            outs[1][...] = gout_ref[...]
            outs[2][...] = chan_ref[...].T.astype(BF)

    if fast:
        outs = [shaped((2, 2, 4, 72, 512), BF)] * 2 + [shaped((2, 2, 4, 64, 512), BF)] * 2
    else:
        outs = [shaped((4, width, 512), BF), shaped((2048, width), BF), shaped((width, 128), BF)]
    return run(
        kernel,
        list(again) + [upstream, home, near, far, small, conv_rows, mid_rows, grad_bias],
        [shaped((rows, width), BF)] + outs,
        "ffn1_backward",
        time=0.01,
        scratch=[
            pltpu.VMEM((128, width), F32),
            pltpu.VMEM((4, width, 512), BF),
            pltpu.VMEM((2048, width), BF),
        ],
    )


def tables(head_index, own_length, rows, width):
    pairs = lax.axis_size("heads")
    freq = jnp.exp(
        jnp.arange(width // 2, dtype=jnp.int32).astype(F32) * (-2.0 * math.log(10000.0) / width)
    )
    steps = rows // 128
    others = jnp.arange(pairs, dtype=jnp.int32) ^ head_index
    coarse = (others[:, None] * steps + jnp.arange(steps, dtype=jnp.int32)[None, :]).reshape(-1)
    coarse_phase = (coarse * 128).astype(F32)[:, None] * freq[None, :]
    fine_phase = jnp.arange(128, dtype=jnp.int32).astype(F32)[:, None] * freq[None, :]
    phase = jnp.concatenate([coarse_phase, fine_phase])
    info = jnp.stack([head_index, own_length]).astype(jnp.int32)
    count = pairs * rows
    half = width // 2

    def kernel(info_ref, sin_ref, cos_ref, table_ref, turned_ref, own_ref, mask_ref):
        sin_b, cos_b = sin_ref[pairs * steps :, :], cos_ref[pairs * steps :, :]
        for a in range(pairs * steps):
            here = slice(128 * a, 128 * a + 128)
            sin_a, cos_a = sin_ref[a : a + 1, :], cos_ref[a : a + 1, :]
            sin = sin_a * cos_b + cos_a * sin_b
            cos = cos_a * cos_b - sin_a * sin_b
            table_ref[here, :half] = sin.astype(BF)
            table_ref[here, half:] = cos.astype(BF)
            turned_ref[:half, here] = sin.T.astype(BF)
            turned_ref[half:, here] = cos.T.astype(BF)
            if a < steps:
                own_ref[0, here, :] = cos
                own_ref[1, here, :] = sin
            at = lax.broadcasted_iota(jnp.int32, (1, 128), 1)
            at = at + ((info_ref[0] ^ (a // steps)) * rows + 128 * (a % steps))
            mask_ref[0:1, here] = jnp.where(at < info_ref[1], 0.0, -1e30)

    return run(
        kernel,
        [info, jnp.sin(phase), jnp.cos(phase)],
        [shaped((count, width), BF), shaped((width, count), BF), shaped((2, rows, half), F32), shaped((1, count), F32)],
        "tables",
        specs=[SMEM, VMEM, VMEM],
    )


def prepare(ffn1_out, dw_kernel, norm_gain, norm_bias, pos_bias, att_proj, att_out, ffn2_in, ffn2_out, conv_in, conv_out):
    head_dim = att_out.shape[1]

    def kernel(
        out1_ref, dw_ref, gain_ref, bias_ref, posb_ref, proj_ref, att_ref, in2_ref, out2_ref, cin_ref, cout_ref,
        b_ref, t_ref, pack_ref, square_ref, pos_ref,
    ):
        b_ref[0:64, :] = out1_ref[...]
        square_ref[...] = jnp.zeros_like(square_ref)
        square_ref[0:GAIN, 0:16] = dw_ref[...].astype(F32)
        square_ref[GAIN:BIAS, 0:16] = gain_ref[...].astype(F32)
        square_ref[BIAS:POS_BIAS, 0:16] = bias_ref[...].astype(F32)
        square_ref[POS_BIAS : POS_BIAS + 2, 0:16] = posb_ref[...].astype(F32)
        turned = square_ref[...].T
        b_ref[64:72, :] = jnp.concatenate([turned[0:8], turned[8:16], jnp.zeros((8, 256), F32)], axis=1).astype(BF)
        both = [proj_ref[h].astype(F32) for h in range(2)]
        for k in range(3):
            columns = slice(k * head_dim, k * head_dim + head_dim)
            t_ref[:, 128 * k : 128 * k + 128] = jnp.concatenate([p[:, columns] for p in both], axis=1).astype(BF)
        square_ref[...] = jnp.zeros_like(square_ref)
        square_ref[0:64, 0:64] = att_ref[0].astype(F32)
        square_ref[64:128, 0:64] = att_ref[1].astype(F32)
        t_ref[:, 384:512] = square_ref[...].T[0:64].astype(BF)
        pos_ref[...] = jnp.concatenate([p[:, 3 * head_dim :] for p in both], axis=1)
        for k in range(2):
            t_ref[32 * k : 32 * k + 32, 512:640] = pos_ref[pl.ds(k, 32, stride=2), :].astype(BF)
        for k in range(4):
            pack_ref[16 * k : 16 * k + 16, :] = in2_ref[:, 512 * k : 512 * k + 512]
        pack_ref[64:128, :] = out2_ref[...]
        for k in range(2):
            pack_ref[128 + 16 * k : 144 + 16 * k, :] = cin_ref[:, 512 * k : 512 * k + 512]
        pack_ref[160:176, :] = cout_ref[...]

    return run(
        kernel,
        [ffn1_out, dw_kernel, norm_gain, norm_bias, pos_bias, att_proj, att_out, ffn2_in, ffn2_out, conv_in, conv_out],
        [shaped((72, 512), BF), shaped((64, 640), BF), shaped((176, 512), BF)],
        "prepare",
        specs=[whole(a) for a in (ffn1_out, dw_kernel, norm_gain, norm_bias, pos_bias, att_proj, att_out)]
        + [whole(a) for a in (ffn2_in, ffn2_out, conv_in, conv_out)],
        grid=(1,),
        scratch=[pltpu.VMEM((128, 128), F32), pltpu.VMEM((64, 128), F32)],
        limit=60,
    )


def own_terms(terms):
    def spec(array):
        lead = len(array.shape) - 2
        return pl.BlockSpec((1,) * lead + array.shape[lead:], lambda *_: (0,) * (lead + 2))

    return list(terms), [spec(t) for t in terms]


def add_terms(refs):
    rows, columns = refs[0].shape[-2:]
    total = refs[0][...].reshape(rows, columns).astype(F32)
    for ref in refs[1:]:
        total = total + ref[...].reshape(rows, columns).astype(F32)
    return total


def finish_first(terms_a, terms_b):
    inputs, specs = own_terms(terms_a + terms_b)

    def kernel(*refs):
        in_ref, out_ref, dw_ref, gain_ref, bias_ref, posb_ref, square_ref = refs[12:]
        total = add_terms(refs[:6])
        for k in range(4):
            in_ref[:, 512 * k : 512 * k + 512] = total[16 * k : 16 * k + 16, :]
        square_ref[...] = jnp.zeros_like(square_ref)
        square_ref[0:8, :] = total[64:72, 0:128]
        square_ref[8:16, :] = total[64:72, 128:256]
        turned = square_ref[...].T
        dw_ref[...] = turned[0:GAIN, 0:16]
        gain_ref[...] = turned[GAIN:BIAS, 0:16]
        bias_ref[...] = turned[BIAS:POS_BIAS, 0:16]
        posb_ref[...] = turned[POS_BIAS : POS_BIAS + 2, 0:16]
        out_ref[...] = add_terms(refs[6:12])

    outs = [(16, 2048), (64, 512), (32, 16), (6, 16), (6, 16), (2, 16)]
    return run(
        kernel,
        inputs,
        [shaped(o, F32) for o in outs],
        "finish_first",
        specs=specs,
        grid=(1,),
        scratch=[pltpu.VMEM((128, 128), F32)],
    )


def finish_attention(terms):
    inputs, specs = own_terms(terms)

    def kernel(*refs):
        proj_ref, out_ref, cin_ref, square_ref, pos_ref = refs[6:]
        total = add_terms(refs[:6])
        square_ref[...] = jnp.zeros_like(square_ref)
        square_ref[0:64, :] = total[:, 384:512]
        turned = square_ref[...].T
        for k in range(2):
            pos_ref[pl.ds(k, 32, stride=2), :] = total[32 * k : 32 * k + 32, 512:640]
        for h in range(2):
            for k in range(3):
                at = 128 * k + 64 * h
                proj_ref[h, :, 64 * k : 64 * k + 64] = total[:, at : at + 64]
            proj_ref[h, :, 192:256] = pos_ref[:, 64 * h : 64 * h + 64]
            out_ref[h] = turned[64 * h : 64 * h + 64, 0:64]
        for k in range(4):
            cin_ref[:, 256 * k : 256 * k + 256] = total[16 * k : 16 * k + 16, 640:896]

    return run(
        kernel,
        inputs,
        [shaped((2, 64, 256), F32), shaped((2, 64, 64), F32), shaped((16, 1024), F32)],
        "finish_attention",
        specs=specs,
        grid=(1,),
        scratch=[pltpu.VMEM((128, 128), F32), pltpu.VMEM((64, 128), F32)],
    )


def finish_middle(sums):
    def kernel(sum_ref, in_ref, out_ref, conv_ref):
        for k in range(4):
            in_ref[:, 512 * k : 512 * k + 512] = sum_ref[16 * k : 16 * k + 16, :].astype(F32)
        out_ref[...] = sum_ref[64:128, :].astype(F32)
        conv_ref[...] = sum_ref[128:144, :].astype(F32)

    return run(
        kernel,
        [sums],
        [shaped((16, 2048), F32), shaped((64, 512), F32), shaped((16, 512), F32)],
        "finish_middle",
    )


def small_shard(dw_kernel, norm_gain, norm_bias, pos_bias):
    stacked = jnp.concatenate([dw_kernel, norm_gain, norm_bias, pos_bias], axis=0)
    return jnp.pad(stacked.T, ((0, 0), (0, 128 - stacked.shape[0])))


def att_shard(att_proj, att_out):
    two, rows, four = att_proj.shape
    head_dim = four // 4
    parts = att_proj.reshape(two, rows, 4, head_dim).transpose(1, 2, 0, 3)
    parts = parts.reshape(rows, 4, two * head_dim)
    out_t = att_out.transpose(2, 0, 1).reshape(rows, two * head_dim)
    turned = parts[:, 3].reshape(rows // 2, 2, two * head_dim).transpose(1, 0, 2)
    turned = turned.reshape(rows, two * head_dim)
    return jnp.concatenate([parts[:, 0], parts[:, 1], parts[:, 2], out_t, turned], axis=1)


def column_chunks(array):
    rows, columns = array.shape
    return array.reshape(rows, columns // 512, 512).transpose(1, 0, 2)


def xor_order(array, index):
    bit = 1
    while bit < array.shape[0]:
        flipped = jnp.stack([array[i ^ bit] for i in range(array.shape[0])])
        array = jnp.where((index & bit) != 0, flipped, array)
        bit *= 2
    return array


def rows_of(shard):
    return lax.all_gather(shard, BOTH, axis=0, tiled=True)


def sum_rows(grad):
    return lax.psum_scatter(grad.astype(F32), BOTH, scatter_dimension=0, tiled=True)


def local(
    frames_in,
    cotangent,
    lengths,
    sample_weight,
    ffn1_in,
    ffn1_out,
    att_proj,
    att_out,
    pos_bias,
    conv_in,
    dw_kernel,
    conv_out,
    ffn2_in,
    ffn2_out,
    norm_gain,
    norm_bias,
):
    row_count, model_width = frames_in.shape
    pairs = lax.axis_size("heads")
    batches = lax.axis_size("batch")
    head_index = lax.axis_index("heads")
    batch_index = lax.axis_index("batch")
    channels = ffn1_in.shape[0]
    fast = channels == 16 and batches == 8 and pairs == 4
    kernel_len = dw_kernel.shape[0]
    head_dim = att_out.shape[1]
    width = model_width // batches

    utter_ids = jnp.arange(lengths.shape[0], dtype=jnp.int32)
    own_length = jnp.sum(jnp.where(utter_ids == batch_index, lengths, 0))
    own_weight = jnp.sum(jnp.where(utter_ids == batch_index, sample_weight, 0)).astype(F32) * 0.25
    total_valid = jnp.sum(lengths).astype(F32)
    ints = jnp.stack([own_length, head_index * row_count]).astype(jnp.int32)
    floats = jnp.stack([own_weight, total_valid])

    if fast:
        shard_b, shard_t, pack = prepare(
            ffn1_out, dw_kernel, norm_gain, norm_bias, pos_bias, att_proj, att_out, ffn2_in, ffn2_out, conv_in, conv_out
        )
        held_a, held_b = gather_depth(ffn1_in), gather_depth(shard_b)
        held_t = jnp.stack([shard_t, swap(shard_t, "heads", 2)])
        held_a, held_b, held_t = lax.optimization_barrier((held_a, held_b, held_t))
        side_a, side_b, deep_t = swap(held_a, "batch", 1), swap(held_b, "heads", 2), swap(held_t, "batch", 4)
        side_a, side_b, deep_t = lax.optimization_barrier((side_a, side_b, deep_t))
        held_a, held_b, held_t = (jnp.concatenate(p) for p in ((held_a, side_a), (held_b, side_b), (held_t, deep_t)))
        side_a, side_b, deep_t = swap(held_a, "heads", 2), swap(held_b, "batch", 1), swap(held_t, "batch", 2)
        table, table_t, own_turn, key_mask = tables(behind(head_index, held_a, held_b), own_length, row_count, model_width)
        table, table_t, own_turn, key_mask, ints, floats, side_a, side_b, deep_t = lax.optimization_barrier(
            (table, table_t, own_turn, key_mask, ints, floats, side_a, side_b, deep_t)
        )
        held_t = jnp.concatenate([held_t, deep_t])
        side_t = swap(held_t, "batch", 1)
        pack = lax.all_gather(behind(pack, held_a, held_b), BOTH, axis=0)
        win, wout, small_t, pos_b = place_first(
            (held_a, side_a, swap(held_a, "heads", 1), swap(side_a, "heads", 1)),
            (held_b, side_b, swap(held_b, "heads", 1), swap(side_b, "heads", 1)),
        )
        x1, n1 = ffn1_forward(frames_in, win, wout, small_t)
        held_t, side_t = behind(held_t, n1), behind(side_t, n1)
        sides_t = held_t, side_t
        tw, pos_w = place_attention(sides_t + tuple(swap(t, "heads", 1) for t in sides_t))
        conv_in_w = middle_w = [pack]
    else:
        table, table_t, own_turn, key_mask = tables(head_index, own_length, row_count, model_width)
        small = small_shard(dw_kernel, norm_gain, norm_bias, pos_bias)
        att_part = att_shard(att_proj, att_out)
        win, wout = column_chunks(rows_of(ffn1_in)), rows_of(ffn1_out)
        small_t = rows_of(small).T.astype(F32)
        pos_b = small_t[POS_BIAS : POS_BIAS + 2].reshape(2, batches, pairs, channels).transpose(2, 0, 1, 3)
        pos_b = pos_b.reshape(pairs, 2, 2, head_dim).transpose(0, 2, 1, 3).reshape(pairs, 2, 2 * head_dim)
        pos_b = xor_order(pos_b, head_index)
        att_all = lax.all_gather(lax.all_gather(att_part, "batch", axis=0), "heads", axis=0)
        att_all = xor_order(att_all, head_index)
        tw = att_all[..., :512].reshape(pairs, model_width, 512)
        pos_w = att_all[..., 512:].reshape(pairs, batches, 2, width // 2, 128).transpose(0, 2, 1, 3, 4)
        pos_w = pos_w.reshape(pairs, model_width, 128)
        halves_in = column_chunks(rows_of(conv_in))
        conv_in_w = [halves_in[0], halves_in[1]]
        middle_w = [
            column_chunks(rows_of(ffn2_in)),
            rows_of(ffn2_out).reshape(4, 512, model_width),
            rows_of(conv_out),
        ]

    if not fast:
        x1, n1 = ffn1_forward(frames_in, win, wout, small_t)
    across = swap(n1, "heads", 2)
    keys = [n1, swap(n1, "heads", 1), across, swap(across, "heads", 1)]
    weights, mixed, scale, kv, queries, after_att, n2 = att_forward(
        key_mask, keys, x1, small_t, tw, pos_w, pos_b, own_turn, table_t
    )
    glu, gated, *conv_in_w = gate_forward(ints, n2, conv_in_w)
    rim = halo(glu)
    depth, sums = conv_forward(ints, glu, rim, small_t)
    sums = sum_over(sum_over(sums, "heads"), "batch")
    layer_out, upstream, raw, gsum, mid_rows, pre, act, dhid, branch, swish, low = middle(
        ints, floats, depth, sums, after_att, cotangent, small_t, middle_w
    )

    gsum = sum_over(gsum, "heads")
    pre = behind(pre, gsum)
    gsum = sum_over(gsum, "batch")
    mid_grads = middle_grads(fast, pre, act, dhid, branch, swish, low)
    positions = head_index * row_count + jnp.arange(row_count, dtype=jnp.int32)
    row_valid = (positions < own_length).astype(F32)[:, None]
    mean_bn = sums[0] / total_valid
    grad_first = (gsum[0] - 2.0 * mean_bn * gsum[1]) / total_valid
    grad_second = gsum[1] / total_valid
    raw = behind(raw, *mid_grads)
    depth_low = (raw + row_valid * (grad_first + 2.0 * depth * grad_second)).astype(BF)
    depth_rim = halo(depth_low)
    if fast:
        mid = lax.psum_scatter(mid_grads[0].reshape(32 * 144, 512), BOTH, scatter_dimension=0, tiled=True)
    upstream, dgated, conv_rows = conv_backward(
        ints, glu, rim, depth_low, depth_rim, small_t, gated, conv_in_w, after_att, upstream
    )
    near, far, home, grad_bias, *att_grads = att_backward(
        fast, upstream, n2, dgated, keys, mixed, scale, weights, kv, queries, tw, pos_w, own_turn, table
    )
    near = swap(near, "heads", 1)
    moving = (far.astype(F32) + near[1].astype(F32)).astype(BF)
    far = swap(moving, "heads", 2)
    grad_bias = xor_order(grad_bias, head_index).reshape(pairs, 2, 2, head_dim).transpose(0, 2, 1, 3)
    grad_bias = grad_bias.reshape(pairs, 2, batches, channels).transpose(1, 2, 0, 3).reshape(2, model_width)
    again = ffn1_again(behind(frames_in, near), x1, win, wout, small_t)
    if fast:
        heard = swap(behind(att_grads[1], near), "heads", 1)
        home = behind(home, heard)
        t = Exchange(att_grads[0], behind(heard, moving), steps_attention())
        send_all([t])
    frames_grad, *first_grads = ffn1_backward(
        fast, again, upstream, home, near, far, small_t, conv_rows, mid_rows, grad_bias
    )

    if fast:
        *first_grads, t.terms[-1] = lax.optimization_barrier((*first_grads, t.terms[-1]))
        own_ffn2_a, own_ffn2_b, own_conv_b = finish_middle(mid)
        a_far, a_own, b_far, b_own = first_grads
        a = Exchange(a_own, swap(a_far, "heads", 1), steps_first("xy"))
        b = Exchange(b_own, swap(b_far, "heads", 1), steps_first("yx"))
        t.terms[-1] = behind(t.terms[-1], mid)
        for group in ((a, b, t), (a, b, t), (a, b, t), (a, b)):
            send_all(group)
        own_proj, own_out, own_conv_a = finish_attention(t.terms)
        own_ffn1_a, own_ffn1_b, own_taps, own_gain, own_bias, own_pos = finish_first(a.terms, b.terms)
    else:

        def to_rows(chunks):
            rows = chunks.shape[1]
            return sum_rows(chunks.transpose(1, 0, 2).reshape(rows, -1))

        own_ffn2_a = to_rows(mid_grads[0])
        own_ffn2_b = sum_rows(mid_grads[1].reshape(-1, model_width))
        own_conv_b = sum_rows(mid_grads[2])
        tw_grad, pos_grad, conv_grad = att_grads
        own_conv_a = sum_rows(conv_grad)
        pos_grad = pos_grad.reshape(pairs, 2, batches, width // 2, 128).transpose(0, 2, 1, 3, 4)
        grad_att = jnp.concatenate([tw_grad, pos_grad.reshape(pairs, model_width, 128)], axis=2)
        grad_att = xor_order(grad_att, head_index).astype(F32)
        own_att = lax.psum_scatter(
            lax.psum_scatter(grad_att, "batch", scatter_dimension=1, tiled=True),
            "heads",
            scatter_dimension=0,
            tiled=True,
        )[0]
        own_ffn1_a, own_ffn1_b = to_rows(first_grads[0]), sum_rows(first_grads[1])
        own_small = sum_rows(first_grads[2])
        own_small = own_small.T
        turned = own_att[:, 512:640].reshape(2, width // 2, 128).transpose(1, 0, 2).reshape(width, 128)
        parts = jnp.stack([own_att[:, :128], own_att[:, 128:256], own_att[:, 256:384], turned], axis=1)
        own_proj = parts.reshape(width, 4, 2, head_dim).transpose(2, 0, 1, 3)
        own_proj = own_proj.reshape(2, width, 4 * head_dim)
        own_out = own_att[:, 384:512].T.reshape(2, head_dim, width)
        own_pos = own_small[POS_BIAS : POS_BIAS + 2]
        own_taps = own_small[:kernel_len]
        own_gain, own_bias = own_small[GAIN : GAIN + 6], own_small[BIAS : BIAS + 6]
    return (
        layer_out,
        frames_grad,
        own_ffn1_a,
        own_ffn1_b,
        own_proj,
        own_out,
        own_pos,
        own_conv_a,
        own_taps,
        own_conv_b,
        own_ffn2_a,
        own_ffn2_b,
        own_gain,
        own_bias,
    )


def solution(mesh):
    placed = (
        P(("batch", "heads"), None),
        P(("batch", "heads"), None),
        P(),
        P(),
        P(("batch", "heads"), None),
        P(("batch", "heads"), None),
        P("heads", "batch", None),
        P("heads", None, "batch"),
        P("heads", "batch"),
        P(("batch", "heads"), None),
        P(None, ("batch", "heads")),
        P(("batch", "heads"), None),
        P(("batch", "heads"), None),
        P(("batch", "heads"), None),
        P(None, ("batch", "heads")),
        P(None, ("batch", "heads")),
    )
    return jax.shard_map(
        local,
        mesh=mesh,
        in_specs=placed,
        out_specs=(
            P(("batch", "heads"), None),
            P(("batch", "heads"), None),
            P(("batch", "heads"), None),
            P(("batch", "heads"), None),
            P("heads", "batch", None),
            P("heads", None, "batch"),
            P("heads", "batch"),
            P(("batch", "heads"), None),
            P(None, ("batch", "heads")),
            P(("batch", "heads"), None),
            P(("batch", "heads"), None),
            P(("batch", "heads"), None),
            P(None, ("batch", "heads")),
            P(None, ("batch", "heads")),
        ),
        check_vma=False,
    )
```

```python
import math

import jax
import jax.numpy as jnp
from jax import lax
from jax.experimental import pallas as pl
from jax.experimental.pallas import tpu as pltpu
from jax.sharding import PartitionSpec as P

epsilon = 1e-05
BF = jnp.bfloat16
F32 = jnp.float32
BOTH = ("batch", "heads")
CHUNK = 256
HALO = 16
SCALE = 0.125
LOG2E = 1.4426950408889634
GAIN, BIAS, POS_BIAS = 32, 38, 44
KZ = (0, 2, 1, 3)
DIMS = {"y": ("batch", 1), "x": ("heads", 2)}
VMEM_BYTES = 40 * 2**20


def swap(source, axis, mask):
    count = lax.axis_size(axis)
    return lax.ppermute(source, axis, [(i, i ^ mask) for i in range(count)])


def sum_over(source, axis):
    mask = 1
    while mask < lax.axis_size(axis):
        source = source + swap(source, axis, mask)
        mask *= 2
    return source


def halo(cells):
    ends = lax.axis_size("heads") - 1
    rows = cells.shape[0]
    before = lax.ppermute(cells[rows - HALO :], "heads", [(i, i + 1) for i in range(ends)])
    after = lax.ppermute(cells[:HALO], "heads", [(i + 1, i) for i in range(ends)])
    return before, after


def behind(source, *others):
    return lax.optimization_barrier((source,) + others)[0]


def gather_depth(shard):
    held = shard[None]
    for mask in (4, 2):
        held = jnp.concatenate([held, swap(held, "batch", mask)])
    return held


class Exchange:
    def __init__(self, own, heard, steps):
        self.terms, self.steps = [own, heard], list(steps)

def send_all(group, keep=False):
    inputs, specs, outs, sizes = [], [], [], []
    stays = [[(0,) * len(one.terms)] for one in group] if keep else [[]] * len(group)
    pairs = [(one, parts) for one, stay in zip(group, stays) for parts in [one.steps[0][0]] + [[(k,) for k in s] for s in stay]]
    for one, parts in pairs:
        for term, index in zip(one.terms, parts, strict=True):
            index = index + (slice(None),) * (term.ndim - len(index))
            ends = [(k, 1) if isinstance(k, int) else (k.start // 2, 2) if k.start else (0, n) for k, n in zip(index, term.shape)]
            specs.append(pl.BlockSpec(tuple(e[1] for e in ends), lambda *_, at=tuple(e[0] for e in ends): at))
            inputs.append(term)
        shape = [2 if k.start else n for k, n in zip(index, term.shape) if not isinstance(k, int)]
        outs.append(shaped(tuple(shape), BF))
        sizes.append(len(parts))

    def kernel(*refs):
        at = 0
        for size, out_ref in zip(sizes, refs[-len(outs) :], strict=True):
            value = refs[at][...].reshape(out_ref.shape).astype(F32)
            for ref in refs[at + 1 : at + size]:
                value = value + ref[...].reshape(out_ref.shape).astype(F32)
            out_ref[...] = value.astype(BF)
            at += size

    moving = run(kernel, inputs, outs, "send_all", specs=specs, grid=(1,), limit=24)
    if keep:
        for one, array in zip(group, moving[1::2], strict=True):
            one.terms = [array]
        moving = moving[0::2]
    for one, array in zip(group, moving, strict=True):
        _, axis, mask = one.steps.pop(0)
        one.terms.append(swap(array, axis, mask))


def steps_first(order):
    one, two = DIMS[order[0]], DIMS[order[1]]
    return [
        ([(1,), (1,)],) + one,
        ([(0, 1), (0, 1), (1,)],) + two,
        ([(0, 0, slice(2, 4)), (0, 0, slice(2, 4)), (0, slice(2, 4)), (slice(2, 4),)],) + ("batch", 2),
        ([(0, 0, 1), (0, 0, 1), (0, 1), (1,), (1,)],) + ("batch", 4),
    ]


def steps_attention():
    high = slice(2, 4)
    return [
        ([(1,), (1,)], "batch", 1),
        ([(high,), (high,)], "batch", 2),
        ([(1,), (1,), (1,)], "batch", 4),
        ([(0, 1), (0, 1), (0, 1), (1,)], "heads", 2),
    ]


def dot(left, right):
    return jnp.dot(left, right, preferred_element_type=F32)


def dot_nt(left, right):
    return lax.dot_general(left, right, (((1,), (1,)), ((), ())), preferred_element_type=F32)


def dot_tn(left, right):
    return lax.dot_general(left, right, (((0,), (0,)), ((), ())), preferred_element_type=F32)


def norm(source):
    center = source - jnp.mean(source, axis=-1, keepdims=True)
    scale = lax.rsqrt(jnp.mean(center * center, axis=-1, keepdims=True) + epsilon)
    return center * scale, scale


def norm_back(upstream, normed, scale, gain_row):
    inner = upstream * gain_row
    mean = jnp.mean(inner, axis=-1, keepdims=True)
    along = jnp.mean(inner * normed, axis=-1, keepdims=True)
    gain_grad = jnp.sum(upstream * normed, axis=0, keepdims=True)
    return scale * (inner - mean - normed * along), gain_grad, jnp.sum(upstream, axis=0, keepdims=True)


def row(small_ref, index):
    return small_ref[index : index + 1, :]


def place():
    batch_at = lax.axis_index("batch")
    heads_at = lax.axis_index("heads")
    return batch_at // 2, batch_at % 2, heads_at // 2, heads_at % 2


def block_index(kz, ky, kx, kc):
    z, y, x, c = place()
    return ((z ^ kz) * 2 + (y ^ ky)) * 4 + (x ^ kx) * 2 + (c ^ kc)


def part(index, size):
    return pl.ds(pl.multiple_of(index * size, size), size)


def valid_rows(ints_ref, rows):
    steps = lax.broadcasted_iota(jnp.int32, (rows, 1), 0) + ints_ref[1]
    return (steps < ints_ref[0]).astype(F32)


def whole(array):
    return pl.BlockSpec(array.shape, lambda *_: (0,) * len(array.shape), pipeline_mode=pl.Buffered(1))


def per_pair(array):
    return pl.BlockSpec((1,) + array.shape[1:], lambda h: (h,) + (0,) * (len(array.shape) - 1))


def shaped(shape, kind):
    return jax.ShapeDtypeStruct(shape, kind)


SMEM = pl.BlockSpec(memory_space=pltpu.SMEM)


VMEM = pl.BlockSpec(memory_space=pltpu.VMEM)


def cost(time):
    return pl.CostEstimate(flops=int(time * 10**9), bytes_accessed=2**12, transcendentals=0)


def run(kernel, inputs, outs, name, specs=None, grid=(), scratch=(), limit=24, time=0.01):
    return pl.pallas_call(
        kernel,
        grid=grid,
        in_specs=specs or [VMEM] * len(inputs),
        out_specs=[whole(o) for o in outs] if grid else [VMEM] * len(outs),
        out_shape=outs,
        scratch_shapes=list(scratch),
        compiler_params=pltpu.CompilerParams(vmem_limit_bytes=limit * 2**20),
        cost_estimate=cost(time),
        name=name,
    )(*inputs)


def fetch(*arrays):
    def kernel(*refs):
        count = len(arrays)
        copies = [pltpu.make_async_copy(refs[i], refs[count + i], refs[-1].at[i]) for i in range(count)]
        for copy in copies:
            copy.start()
        for copy in copies:
            copy.wait()

    return run(
        kernel,
        list(arrays),
        [shaped(a.shape, a.dtype) for a in arrays],
        "fetch",
        specs=[pl.BlockSpec(memory_space=pltpu.HBM)] * len(arrays),
        scratch=[pltpu.SemaphoreType.DMA((len(arrays),))],
    )


def place_first(sets_a, sets_b):
    def kernel(*refs):
        a_refs, b_refs = refs[:4], refs[4:8]
        win_ref, wout_ref, small_ref, pb_ref, chan_ref, stage_ref = refs[8:]
        for k in range(4):
            for i in range(8):
                at = block_index(KZ[i % 4], i // 4, k & 1, k >> 1)
                for column in range(4):
                    win_ref[column, part(at, 16), :] = a_refs[k][i, :, 512 * column : 512 * column + 512]
                at = block_index(KZ[i % 4], k & 1, i // 4, k >> 1)
                wout_ref[part(at, 64), :] = b_refs[k][i, 0:64, :]
                small = b_refs[k][i, 64:72, 0:256].astype(F32)
                chan_ref[part(at, 16), :] = jnp.concatenate([small[:, 0:128], small[:, 128:256]], axis=0)
        small_ref[...] = chan_ref[...].T
        for mask in range(4):
            pair = lax.axis_index("heads") ^ mask
            for b in range(8):
                stage_ref[16 * b : 16 * b + 16, :] = chan_ref[part(4 * b + pair, 16), :]
            one, two = (stage_ref[...].T[at : at + 1] for at in (POS_BIAS, POS_BIAS + 1))
            pb_ref[mask, 0:1, :] = jnp.concatenate([one[:, :64], two[:, :64]], axis=1)
            pb_ref[mask, 1:2, :] = jnp.concatenate([one[:, 64:], two[:, 64:]], axis=1)

    return run(
        kernel,
        list(sets_a) + list(sets_b),
        [shaped((4, 512, 512), BF), shaped((2048, 512), BF), shaped((128, 512), F32), shaped((4, 2, 128), F32)],
        "place_first",
        scratch=[pltpu.VMEM((512, 128), F32), pltpu.VMEM((128, 128), F32)],
    )


def place_attention(sets):
    def kernel(*refs):
        tw_ref, pos_ref = refs[4:]
        z, y, _, _ = place()
        for k in range(4):
            for i in range(8):
                pair = (i % 2) * 2 + (k >> 1)
                at = (z ^ KZ[i // 2]) * 2 + (y ^ (k & 1))
                tw_ref[pair, part(at, 64), :] = refs[k][i, :, 0:512]
                pos_ref[pair, part(at, 32), :] = refs[k][i, 0:32, 512:640]
                pos_ref[pair, part(at + 8, 32), :] = refs[k][i, 32:64, 512:640]

    return run(
        kernel, list(sets), [shaped((4, 512, 512), BF), shaped((4, 512, 128), BF)], "place_attention"
    )


def ffn1_forward(frames, win, wout, small):
    def kernel(x_ref, win_ref, wout_ref, small_ref, out_ref, normed_ref):
        source = x_ref[...].astype(F32)
        normed, _ = norm(source)
        pre = (normed * row(small_ref, GAIN) + row(small_ref, BIAS)).astype(BF)
        total = jnp.zeros_like(source)
        for column in range(win_ref.shape[0]):
            hidden = dot(pre, win_ref[column])
            active = (hidden * jax.nn.sigmoid(hidden)).astype(BF)
            total = total + dot(active, wout_ref[512 * column : 512 * column + 512, :])
        source = source + 0.5 * total
        out_ref[...] = source
        normed, _ = norm(source)
        normed_ref[...] = (normed * row(small_ref, GAIN + 1) + row(small_ref, BIAS + 1)).astype(BF)

    return run(
        kernel,
        [frames, win, wout, small],
        [shaped(frames.shape, F32), shaped(frames.shape, BF)],
        "ffn1_forward",
        time=3,
    )


def halves(first, value):
    zero = jnp.zeros_like(value)
    return jnp.where(first, value, zero), jnp.where(first, zero, value)


def att_forward_kernel(
    mask_ref, own_ref, k1_ref, k2_ref, k3_ref, x1_ref, small_ref, tw_ref, pos_ref, pb_ref, cs_ref, et_ref,
    w_ref, o_ref, scale_ref, kv_ref, q_ref, att_ref, n2_ref, right_ref, value_ref, total_ref,
):
    rows, width = own_ref.shape
    half = cs_ref.shape[2]
    step = pl.program_id(0)
    tw = tw_ref[0]

    @pl.when(step == 0)
    def _():
        right_ref[0:width, :] = et_ref[...]
        value_ref[:, 128:256] = jnp.ones((value_ref.shape[0], 128), BF)
        total_ref[...] = x1_ref[...]

    for k, ref in enumerate((own_ref, k1_ref, k2_ref, k3_ref)):
        here = slice(k * rows, k * rows + rows)
        kv = dot(ref[...], tw[:, 128:384])
        kv_ref[0, here, :] = kv.astype(BF)
        right_ref[width : width + 128, here] = kv[:, :128].T.astype(BF)
    value_ref[:, 0:128] = kv_ref[0, :, 128:]
    query = dot(own_ref[...], tw[:, :128])
    qc = (query + pb_ref[0, 0:1, :]).astype(BF)
    qp = (query + pb_ref[0, 1:2, :]).astype(BF)
    q_ref[0, 0] = qc
    q_ref[0, 1] = qp
    first = lax.broadcasted_iota(jnp.int32, (rows, 128), 1) < 64
    cos, sin = cs_ref[0], cs_ref[1]
    mask = mask_ref[...]
    outs = []
    for qc_h, qp_h in zip(halves(first, qc), halves(first, qp)):
        turned = dot_nt(qp_h, pos_ref[0]) * (SCALE * LOG2E)
        us, uc = turned[:, :half], turned[:, half:]
        left = jnp.concatenate(
            [
                (us * cos + uc * sin).astype(BF),
                (uc * cos - us * sin).astype(BF),
                (qc_h.astype(F32) * (SCALE * LOG2E)).astype(BF),
            ],
            axis=1,
        )
        parts = []
        for r in range(0, rows, CHUNK):
            scores = dot(left[r : r + CHUNK], right_ref[...]) + mask
            top = jnp.max(scores, axis=1, keepdims=True)
            weights = jnp.exp2(scores - top).astype(BF)
            w_ref[0, len(outs), r : r + CHUNK, :] = weights
            parts.append(dot(weights, value_ref[...]))
        outs.append(jnp.concatenate(parts, axis=0))
    scale = 1.0 / jnp.where(first, outs[0][:, 128:], outs[1][:, 128:])
    scale_ref[0] = scale
    mixed = jnp.where(first, outs[0][:, :128], outs[1][:, :128]) * scale
    o_ref[0] = mixed
    total_ref[...] += dot_nt(mixed.astype(BF), tw[:, 384:512])

    @pl.when(step == pl.num_programs(0) - 1)
    def _():
        after = total_ref[...]
        att_ref[...] = after
        normed, _ = norm(after)
        n2_ref[...] = (normed * row(small_ref, GAIN + 2) + row(small_ref, BIAS + 2)).astype(BF)


def att_forward(mask, keys, x1, small, tw, pos, pb, cs, et):
    rows, width = x1.shape
    count = mask.shape[1]
    paired = [
        shaped((4, 2, rows, count), BF),
        shaped((4, rows, 128), F32),
        shaped((4, rows, 128), F32),
        shaped((4, count, 256), BF),
        shaped((4, 2, rows, 128), BF),
    ]
    shared = [shaped((rows, width), F32), shaped((rows, width), BF)]
    return pl.pallas_call(
        att_forward_kernel,
        grid=(4,),
        in_specs=[whole(mask)]
        + [whole(k) for k in keys]
        + [whole(x1), whole(small), per_pair(tw), per_pair(pos), per_pair(pb), whole(cs), whole(et)],
        out_specs=[per_pair(a) for a in paired] + [whole(a) for a in shared],
        out_shape=paired + shared,
        scratch_shapes=[
            pltpu.VMEM((width + 128, count), BF),
            pltpu.VMEM((count, 256), BF),
            pltpu.VMEM((rows, width), F32),
        ],
        compiler_params=pltpu.CompilerParams(vmem_limit_bytes=56 * 2**20),
        cost_estimate=cost(40),
        name="att_forward",
    )(mask, *keys, x1, small, tw, pos, pb, cs, et)


def att_backward_kernel(fast, *refs):
    (up_ref, n2_ref, dg_ref, own_ref, k1_ref, k2_ref, k3_ref, o_ref, scale_ref, w_ref, kv_ref, q_ref, tw_ref, pos_ref, cs_ref,
     e_ref, near_ref, far_ref, home_ref, db_ref) = refs[:20]
    outs, (dr_ref, dn_ref, dq_ref, og_ref, dconv_ref, tw_grad_ref, pos_grad_ref) = refs[20:-7], refs[-7:]
    rows, width = up_ref.shape
    half = cs_ref.shape[2]
    count = dn_ref.shape[1]
    step = pl.program_id(0)

    @pl.when(step == 0)
    def _():
        og_ref[...] = up_ref[...].astype(BF)
        dn_ref[...] = jnp.zeros_like(dn_ref)
        dq_ref[...] = jnp.zeros_like(dq_ref)
        dconv_ref[...] = dot_tn(n2_ref[...], dg_ref[...]).astype(BF)

    og = og_ref[...]
    tw = tw_ref[0]
    do_f = dot(og, tw[:, 384:512]).astype(BF).astype(F32) * scale_ref[0]
    do = do_f.astype(BF)
    key, value = kv_ref[0, :, :128], kv_ref[0, :, 128:]
    first = lax.broadcasted_iota(jnp.int32, (rows, 128), 1) < 64
    mixed = o_ref[0]
    do_t = do_f.T.astype(BF)
    qc_t = (q_ref[0, 0].astype(F32) * SCALE).T.astype(BF)
    qp_t = q_ref[0, 1].astype(F32).T.astype(BF)
    cos, sin = cs_ref[0], cs_ref[1]
    dqcs, dqps, dks, dvs, dps = [], [], [], [], []
    for head, (do_h, inner_h) in enumerate(zip(halves(first, do), halves(first, do_f * mixed))):
        mine = slice(head * 64, head * 64 + 64)
        inner = jnp.sum(inner_h, axis=1, keepdims=True)
        for r in range(0, rows, CHUNK):
            dw = dot_nt(do_h[r : r + CHUNK], value)
            weights = w_ref[0, head, r : r + CHUNK, :].astype(F32)
            dr_ref[r : r + CHUNK, :] = (weights * (dw - inner[r : r + CHUNK])).astype(BF)
        dr = dr_ref[...]
        turned = dot(dr, e_ref[...]) * SCALE
        dqcs.append(dot(dr, key) * SCALE)
        dks.append(dot(qc_t[mine], dr).astype(BF))
        dvs.append(dot(do_t[mine], w_ref[0, head]).astype(BF))
        gs, gc = turned[:, :half], turned[:, half:]
        du = jnp.concatenate(
            [(gs * cos - gc * sin).astype(BF), (gs * sin + gc * cos).astype(BF)], axis=1
        )
        dqps.append(dot(du, pos_ref[0]))
        dps.append(dot(qp_t[mine], du))
    dqc = jnp.where(first, dqcs[0], dqcs[1])
    dqp = jnp.where(first, dqps[0], dqps[1])
    db_ref[0, 0:1, :] = jnp.sum(dqc, axis=0, keepdims=True)
    db_ref[0, 1:2, :] = jnp.sum(dqp, axis=0, keepdims=True)
    dq = dqc + dqp
    dq_low = dq.astype(BF)
    dkv = jnp.concatenate(dks + dvs, axis=0)
    dn_ref[...] += dot(tw[:, 128:384], dkv)
    dq_ref[...] += dot_nt(dq_low, tw[:, :128])
    grad_kv = jnp.zeros((256, width), F32)
    for k, ref in enumerate((own_ref, k1_ref, k2_ref, k3_ref)):
        grad_kv = grad_kv + dot(dkv[:, k * rows : k * rows + rows], ref[...])
    grad_q = dot(dq.T.astype(BF), own_ref[...])
    grad_o = dot(mixed.T.astype(BF), og)
    tw_grad_ref[...] = jnp.concatenate([grad_q, grad_kv, grad_o], axis=0).T.astype(BF)
    pos_grad_ref[...] = jnp.concatenate(dps, axis=0).T.astype(BF)

    if fast:
        z, y, x, c = place()
        pair = (x ^ (step // 2)) * 2 + (c ^ (step % 2))

        def write(pack_ref):
            for ky in range(2):
                for i in range(4):
                    at = (z ^ KZ[i]) * 2 + (y ^ ky)
                    pack_ref[ky, i, 0, :, 0:512] = tw_grad_ref[part(at, 64), :]
                    pack_ref[ky, i, 0, 0:32, 512:640] = pos_grad_ref[part(at, 32), :]
                    pack_ref[ky, i, 0, 32:64, 512:640] = pos_grad_ref[part(at + 8, 32), :]
                    for t in range(4):
                        pack_ref[ky, i, 0, 16 * t : 16 * t + 16, 640:896] = dconv_ref[
                            part(at * 4 + pair, 16), 256 * t : 256 * t + 256
                        ]

        pl.when(step % 2 == 0)(lambda: write(outs[0]))
        pl.when(step % 2 == 1)(lambda: write(outs[1]))
    else:
        outs[0][0] = tw_grad_ref[...]
        outs[1][0] = pos_grad_ref[...]
        outs[2][...] = dconv_ref[...]

    @pl.when(step == pl.num_programs(0) - 1)
    def _():
        for k in range(4):
            grad = dn_ref[:, k * rows : k * rows + rows].T
            if k == 0:
                home_ref[...] = grad + dq_ref[...]
            elif k == 2:
                far_ref[...] = grad.astype(BF)
            else:
                near_ref[k // 2] = grad.astype(BF)


def att_backward(fast, upstream, n2, dgated, keys, mixed, scale, weights, kv, queries, tw, pos, cs, e):
    rows, width = upstream.shape
    count = kv.shape[1]
    shared = [shaped((2, rows, width), BF), shaped((rows, width), BF), shaped((rows, width), F32)]
    paired = [shaped((4, 2, 128), F32)]
    specs = [whole(a) for a in shared] + [per_pair(a) for a in paired]
    outs = shared + paired
    if fast:
        extra = [shaped((2, 4, 2, 64, 896), BF)] * 2
        specs += [pl.BlockSpec((2, 4, 1, 64, 896), lambda h: (0, 0, h // 2, 0, 0))] * 2
    else:
        extra = [shaped((4, width, 512), BF), shaped((4, width, 128), BF), shaped((width, 1024), BF)]
        specs += [per_pair(extra[0]), per_pair(extra[1]), whole(extra[2])]
    return pl.pallas_call(
        lambda *refs: att_backward_kernel(fast, *refs),
        grid=(4,),
        in_specs=[whole(upstream), whole(n2), whole(dgated)]
        + [whole(k) for k in keys]
        + [per_pair(mixed), per_pair(scale), per_pair(weights), per_pair(kv), per_pair(queries), per_pair(tw), per_pair(pos)]
        + [whole(cs), whole(e)],
        out_specs=specs,
        out_shape=outs + extra,
        scratch_shapes=[
            pltpu.VMEM((rows, count), BF),
            pltpu.VMEM((width, count), F32),
            pltpu.VMEM((rows, width), F32),
            pltpu.VMEM((rows, width), BF),
            pltpu.VMEM((width, 1024), BF),
            pltpu.VMEM((width, 512), BF),
            pltpu.VMEM((width, 128), BF),
        ],
        compiler_params=pltpu.CompilerParams(vmem_limit_bytes=VMEM_BYTES),
        cost_estimate=cost(0.01),
        name="att_backward",
    )(upstream, n2, dgated, *keys, mixed, scale, weights, kv, queries, tw, pos, cs, e)


def gate_forward(ints, n2, conv_in):
    rows, width = n2.shape

    def kernel(ints_ref, n2_ref, *refs):
        w_refs, (glu_ref, gated_ref, half_ref) = refs[:2], refs[2:]
        half_ref[0] = w_refs[0][...].reshape(width, width)
        half_ref[1] = w_refs[1][...].reshape(width, width)
        left = dot(n2_ref[...], half_ref[0])
        right = dot(n2_ref[...], half_ref[1])
        gated_ref[:, :width] = left
        gated_ref[:, width:] = right
        glu_ref[...] = (left * jax.nn.sigmoid(right) * valid_rows(ints_ref, rows)).astype(BF)

    if len(conv_in) == 1:
        conv_in = conv_in * 2
        specs = [
            pl.BlockSpec((32, 16, 512), lambda *_, at=at: (0, at, 0), pipeline_mode=pl.Buffered(1)) for at in (8, 9)
        ]
    else:
        specs = [whole(a) for a in conv_in]
    return run(
        kernel,
        [ints, n2] + conv_in,
        [shaped((rows, width), BF), shaped((rows, 2 * width), F32)] + [shaped((2, width, width), BF)],
        "gate_forward",
        specs=[SMEM, whole(n2)] + specs,
        grid=(1,),
        limit=60,
    )


def extend(ext_ref, before_ref, own_ref, after_ref):
    rows = own_ref.shape[0]
    ext_ref[0, 0:HALO, :] = before_ref[...].astype(F32)
    ext_ref[0, HALO : HALO + rows, :] = own_ref[...].astype(F32)
    ext_ref[0, HALO + rows : 2 * HALO + rows, :] = after_ref[...].astype(F32)
    kept = 2 * HALO + rows - 8
    for shift in range(1, 8):
        ext_ref[shift, 0:kept, :] = ext_ref[0, shift : shift + kept, :]


def shifted(ext_ref, start, size, columns):
    return ext_ref[start % 8, start - start % 8 : start - start % 8 + size, columns]


def conv_forward(ints, glu, rim, small):
    rows, width = glu.shape

    def kernel(ints_ref, before_ref, glu_ref, after_ref, small_ref, depth_ref, sums_ref, ext_ref):
        extend(ext_ref, before_ref, glu_ref, after_ref)
        steps = lax.broadcasted_iota(jnp.int32, (64, 1), 0) + ints_ref[1]
        for c in range(0, width, 128):
            one = jnp.zeros((1, 128), F32)
            two = jnp.zeros((1, 128), F32)
            for r in range(0, rows, 64):
                total = jnp.zeros((64, 128), F32)
                for k in range(2 * HALO):
                    total = total + shifted(ext_ref, r + k + 1, 64, slice(c, c + 128)) * small_ref[k : k + 1, c : c + 128]
                depth_ref[r : r + 64, c : c + 128] = total
                kept = jnp.where(steps + r < ints_ref[0], total, 0.0)
                one = one + jnp.sum(kept, axis=0, keepdims=True)
                two = two + jnp.sum(kept * total, axis=0, keepdims=True)
            sums_ref[0:1, c : c + 128] = one
            sums_ref[1:2, c : c + 128] = two

    return run(
        kernel,
        [ints, rim[0], glu, rim[1], small],
        [shaped((rows, width), F32), shaped((2, width), F32)],
        "conv_forward",
        time=4,
        specs=[SMEM] + [VMEM] * 4,
        scratch=[pltpu.VMEM((8, rows + 2 * HALO, width), F32)],
    )


def conv_backward(ints, glu, rim, depth_low, depth_rim, small, gated, conv_in, after_att, upstream):
    rows, width = glu.shape

    def kernel(
        ints_ref, gb_ref, glu_ref, ga_ref, db_ref, d_ref, da_ref, small_ref, gated_ref, att_ref, up_ref, *refs
    ):
        w_ref, out_ref, dg_ref, grads_ref, ext_ref, extd_ref, dglu_ref = refs
        extend(ext_ref, gb_ref, glu_ref, ga_ref)
        extend(extd_ref, db_ref, d_ref, da_ref)
        taps = 2 * HALO
        for c in range(0, width, 128):
            cols = slice(c, c + 128)
            for r in range(0, rows, 64):
                total = jnp.zeros((64, 128), F32)
                for k in range(taps):
                    at = r + taps - 1 - k
                    total = total + shifted(extd_ref, at, 64, cols) * small_ref[k : k + 1, cols]
                dglu_ref[r : r + 64, cols] = total
            for k in range(taps):
                total = jnp.zeros((8, 128), F32)
                for r in range(0, rows, 64):
                    product = shifted(ext_ref, r + k + 1, 64, cols) * shifted(extd_ref, HALO + r, 64, cols)
                    total = total + jnp.sum(product.reshape(8, 8, 128), axis=0)
                grads_ref[k : k + 1, cols] = jnp.sum(total, axis=0, keepdims=True)
        grad = dglu_ref[...] * valid_rows(ints_ref, rows)
        gate = jax.nn.sigmoid(gated_ref[:, width:])
        left = (grad * gate).astype(BF)
        right = (grad * gated_ref[:, :width] * gate * (1.0 - gate)).astype(BF)
        dg_ref[:, :width] = left
        dg_ref[:, width:] = right
        inner = dot_nt(left, w_ref[0]) + dot_nt(right, w_ref[1])
        normed, scale = norm(att_ref[...])
        grad, gain_grad, bias_grad = norm_back(inner, normed, scale, row(small_ref, GAIN + 2))
        out_ref[...] = up_ref[...] + grad
        grads_ref[taps : taps + 1, :] = gain_grad
        grads_ref[taps + 1 : taps + 2, :] = bias_grad

    inputs = [ints, rim[0], glu, rim[1], depth_rim[0], depth_low, depth_rim[1], small, gated]
    return run(
        kernel,
        inputs + [after_att, upstream, conv_in],
        [shaped((rows, width), F32), shaped((rows, 2 * width), BF), shaped((40, width), F32)],
        "conv_backward",
        time=0.01,
        specs=[SMEM] + [VMEM] * (len(inputs) + 2),
        scratch=[pltpu.VMEM((8, rows + 2 * HALO, width), F32)] * 2 + [pltpu.VMEM((rows, width), F32)],
    )


def middle(ints, floats, depth, sums, after_att, cotangent, small, weights):
    rows, width = depth.shape

    def kernel(
        ints_ref, floats_ref, depth_ref, sums_ref, att_ref, cot_ref, small_ref, *refs
    ):
        w_refs = refs[:-12]
        (layer_ref, up_ref, raw_ref, gsum_ref, grads_ref, pre_ref, act_ref, dhid_ref, branch_ref, swish_ref, low_ref,
         hid_ref) = refs[-12:]
        packed = len(w_refs) == 1
        columns = hid_ref.shape[0]

        def w_in(column):
            if packed:
                return w_refs[0][:, 16 * column : 16 * column + 16, :].reshape(width, 512)
            return w_refs[0][column]

        def w_out(column):
            if packed:
                return w_refs[0][8 * column : 8 * column + 8, 64:128, :].reshape(512, width)
            return w_refs[1][column]

        total_valid = floats_ref[1]
        mean_bn = sums_ref[0:1, :] / total_valid
        var_bn = sums_ref[1:2, :] / total_valid - mean_bn * mean_bn
        inv = lax.rsqrt(var_bn + epsilon)
        center = depth_ref[...] - mean_bn
        bn_gain = row(small_ref, GAIN + 5)
        z = center * inv * bn_gain + row(small_ref, BIAS + 5)
        swish = (z * jax.nn.sigmoid(z)).astype(BF)
        swish_ref[...] = swish
        conv_out = w_refs[0][:, 160:176, :].reshape(width, width) if packed else w_refs[2][...]
        after_conv = att_ref[...] + dot(swish, conv_out)
        normed3, scale3 = norm(after_conv)
        pre = (normed3 * row(small_ref, GAIN + 3) + row(small_ref, BIAS + 3)).astype(BF)
        pre_ref[...] = pre
        total = jnp.zeros((rows, width), F32)
        for column in range(columns):
            hidden = dot(pre, w_in(column))
            hid_ref[column] = hidden
            active = (hidden * jax.nn.sigmoid(hidden)).astype(BF)
            act_ref[column] = active
            total = total + dot(active, w_out(column))
        normed4, scale4 = norm(after_conv + 0.5 * total)
        gain4 = row(small_ref, GAIN + 4)
        layer_ref[...] = (normed4 * gain4 + row(small_ref, BIAS + 4)).astype(BF)
        seed = cot_ref[...].astype(F32) * (valid_rows(ints_ref, rows) * floats_ref[0])
        up, gain_grad, bias_grad = norm_back(seed, normed4, scale4, gain4)
        grads_ref[...] = jnp.zeros_like(grads_ref)
        grads_ref[2:3, :] = gain_grad
        grads_ref[3:4, :] = bias_grad
        branch = (0.5 * up).astype(BF)
        branch_ref[...] = branch
        total = jnp.zeros((rows, width), F32)
        for column in range(columns):
            hidden = hid_ref[column]
            gate = jax.nn.sigmoid(hidden)
            grad = dot_nt(branch, w_out(column)) * (gate * (1.0 + hidden * (1.0 - gate)))
            grad = grad.astype(BF)
            dhid_ref[column] = grad
            total = total + dot_nt(grad, w_in(column))
        grad, gain_grad, bias_grad = norm_back(total, normed3, scale3, row(small_ref, GAIN + 3))
        grads_ref[0:1, :] = gain_grad
        grads_ref[1:2, :] = bias_grad
        up = up + grad
        up_ref[...] = up
        low = up.astype(BF)
        low_ref[...] = low
        gate = jax.nn.sigmoid(z)
        dz = dot_nt(low, conv_out) * (gate * (1.0 + z * (1.0 - gate)))
        grads_ref[4:5, :] = jnp.sum(dz * center, axis=0, keepdims=True) * inv
        grads_ref[5:6, :] = jnp.sum(dz, axis=0, keepdims=True)
        raw = dz * (bn_gain * inv)
        raw_ref[...] = raw
        gsum_ref[0:1, :] = -jnp.sum(raw, axis=0, keepdims=True)
        gsum_ref[1:2, :] = jnp.sum(raw * center, axis=0, keepdims=True) * (-0.5 * inv * inv)

    square_f, square = shaped((rows, width), F32), shaped((rows, width), BF)
    wide = shaped((4, rows, 512), BF)
    inputs = [ints, floats, depth, sums, after_att, cotangent, small]
    return run(
        kernel,
        inputs + weights,
        [square, square_f, square_f, shaped((2, width), F32), shaped((8, width), F32)]
        + [square, wide, wide, square, square, square],
        "middle",
        time=8,
        specs=[SMEM, SMEM] + [VMEM] * (len(inputs) - 2 + len(weights)),
        scratch=[pltpu.VMEM((4, rows, 512), F32)],
    )


def middle_grads(fast, pre, act, dhid, branch, swish, low):
    width = pre.shape[1]

    def kernel(pre_ref, act_ref, dhid_ref, branch_ref, swish_ref, low_ref, *outs):
        for column in range(act_ref.shape[0]):
            grad_in = dot_tn(pre_ref[...], dhid_ref[column]).astype(BF)
            grad_out = dot_tn(act_ref[column], branch_ref[...]).astype(BF)
            if fast:
                outs[0][:, 16 * column : 16 * column + 16, :] = grad_in.reshape(32, 16, 512)
                outs[0][8 * column : 8 * column + 8, 64:128, :] = grad_out.reshape(8, 64, 512)
            else:
                outs[0][column] = grad_in
                outs[1][column] = grad_out
        grad = dot_tn(swish_ref[...], low_ref[...]).astype(BF)
        if fast:
            outs[0][:, 128:144, :] = grad.reshape(32, 16, 512)
        else:
            outs[2][...] = grad

    if fast:
        outs = [shaped((32, 144, 512), BF)]
    else:
        outs = [shaped((4, width, 512), BF), shaped((4, 512, width), BF), shaped((width, width), BF)]
    return run(kernel, [pre, act, dhid, branch, swish, low], outs, "middle_grads", time=3)


def ffn1_again(frames, x1, win, wout, small, home, near):
    rows, width = x1.shape

    def kernel(
        x_in, x1_in, win_in, wout_in, small_ref, home_ref, near_ref,
        pre_ref, act_ref, slope_ref, x1_ref, x_ref, win_ref, wout_ref, sum_ref, sems,
    ):
        pairs = ((x_in, x_ref), (win_in, win_ref), (x1_in, x1_ref), (wout_in, wout_ref))
        copies = [pltpu.make_async_copy(a, b, sems.at[k]) for k, (a, b) in enumerate(pairs)]
        for copy in copies:
            copy.start()
        copies[0].wait()
        normed, _ = norm(x_ref[...].astype(F32))
        pre = (normed * row(small_ref, GAIN) + row(small_ref, BIAS)).astype(BF)
        pre_ref[...] = pre
        sum_ref[...] = home_ref[...] + near_ref[0].astype(F32)
        copies[1].wait()
        for column in range(win.shape[0]):
            hidden = dot(pre, win_ref[column])
            gate = jax.nn.sigmoid(hidden)
            act_ref[column] = (hidden * gate).astype(BF)
            slope_ref[column] = gate * (1.0 + hidden * (1.0 - gate))
        copies[2].wait()
        copies[3].wait()

    wide = (win.shape[0], rows, 512)
    return run(
        kernel,
        [frames, x1, win, wout, small, home, near],
        [shaped((rows, width), BF), shaped(wide, BF), shaped(wide, F32), shaped(x1.shape, F32)]
        + [shaped(frames.shape, BF), shaped(win.shape, BF), shaped(wout.shape, BF), shaped(home.shape, F32)],
        "ffn1_again",
        time=0.01,
        specs=[pl.BlockSpec(memory_space=pltpu.HBM)] * 4 + [VMEM] * 3,
        scratch=[pltpu.SemaphoreType.DMA((4,))],
    )


def ffn1_backward(fast, again, upstream, far, small, conv_rows, mid_rows, grad_bias):
    pre, active, slope, x1, frames, win, wout, home = again
    rows, width = x1.shape

    def kernel(
        pre_ref, act_ref, slope_ref, x1_ref, x_ref, win_ref, wout_ref, home_ref, up_ref, far_ref, small_ref,
        conv_ref, mid_ref, bias_ref,
        *refs,
    ):
        frames_ref, outs, (chan_ref, gin_ref, gout_ref) = refs[0], refs[1:-3], refs[-3:]
        dn = home_ref[...] + far_ref[...].astype(F32)
        normed, scale = norm(x1_ref[...])
        grad, gain1, bias1 = norm_back(dn, normed, scale, row(small_ref, GAIN + 1))
        up = up_ref[...] + grad
        branch = (0.5 * up).astype(BF)
        normed, scale = norm(x_ref[...].astype(F32))
        gain0 = row(small_ref, GAIN)
        pre = pre_ref[...]
        total = jnp.zeros((rows, width), F32)
        for column in range(win_ref.shape[0]):
            gout_ref[512 * column : 512 * column + 512, :] = dot_tn(act_ref[column], branch).astype(BF)
            grad = dot_nt(branch, wout_ref[512 * column : 512 * column + 512, :])
            grad = (grad * slope_ref[column]).astype(BF)
            gin_ref[column] = dot_tn(pre, grad).astype(BF)
            total = total + dot_nt(grad, win_ref[column])
        grad, gain_grad, bias_grad = norm_back(total, normed, scale, gain0)
        frames_ref[...] = (up + grad).astype(BF)
        chan_ref[...] = jnp.zeros_like(chan_ref)
        taps = GAIN
        chan_ref[0:taps, :] = conv_ref[0:taps, :]
        for first, at in ((GAIN, 0), (BIAS, 1)):
            chan_ref[first + 2 : first + 3, :] = conv_ref[taps + at : taps + at + 1, :]
            for k in range(3):
                chan_ref[first + 3 + k : first + 4 + k, :] = mid_ref[2 * k + at : 2 * k + at + 1, :]
        chan_ref[POS_BIAS : POS_BIAS + 2, :] = bias_ref[...]
        chan_ref[GAIN : GAIN + 1, :] = gain_grad
        chan_ref[GAIN + 1 : GAIN + 2, :] = gain1
        chan_ref[BIAS : BIAS + 1, :] = bias_grad
        chan_ref[BIAS + 1 : BIAS + 2, :] = bias1
        if fast:
            a_far, a_own, b_far, b_own = outs
            turned = chan_ref[...].T.astype(BF)
            for kc, a_out, b_out in ((1, a_far, b_far), (0, a_own, b_own)):
                for one in range(2):
                    for two in range(2):
                        for i in range(4):
                            at = block_index(KZ[i], two, one, kc)
                            for column in range(4):
                                a_out[one, two, i, 16 * column : 16 * column + 16, :] = gin_ref[
                                    column, part(at, 16), :
                                ]
                            at = block_index(KZ[i], one, two, kc)
                            b_out[one, two, i] = gout_ref[part(at, 64), :]
            gin_ref[0, :, 0:128] = turned
            for kc, a_out in ((1, a_far), (0, a_own)):
                for one in range(2):
                    for two in range(2):
                        for i in range(4):
                            at = block_index(KZ[i], two, one, kc)
                            own = gin_ref[0, part(at, 16), 0:128].astype(F32)
                            own = jnp.concatenate([own[0:8], own[8:16], jnp.zeros((8, 256), F32)], axis=1)
                            a_out[one, two, i, 64:72, :] = own.astype(BF)
        else:
            outs[0][...] = gin_ref[...]
            outs[1][...] = gout_ref[...]
            outs[2][...] = chan_ref[...].T.astype(BF)

    if fast:
        outs = [shaped((2, 2, 4, 72, 512), BF)] * 2 + [shaped((2, 2, 4, 64, 512), BF)] * 2
    else:
        outs = [shaped((4, width, 512), BF), shaped((2048, width), BF), shaped((width, 128), BF)]
    return run(
        kernel,
        list(again) + [upstream, far, small, conv_rows, mid_rows, grad_bias],
        [shaped((rows, width), BF)] + outs,
        "ffn1_backward",
        time=0.01,
        scratch=[
            pltpu.VMEM((128, width), F32),
            pltpu.VMEM((4, width, 512), BF),
            pltpu.VMEM((2048, width), BF),
        ],
    )


def tables(head_index, own_length, rows, width):
    pairs = lax.axis_size("heads")
    freq = jnp.exp(
        jnp.arange(width // 2, dtype=jnp.int32).astype(F32) * (-2.0 * math.log(10000.0) / width)
    )
    steps = rows // 128
    others = jnp.arange(pairs, dtype=jnp.int32) ^ head_index
    coarse = (others[:, None] * steps + jnp.arange(steps, dtype=jnp.int32)[None, :]).reshape(-1)
    coarse_phase = (coarse * 128).astype(F32)[:, None] * freq[None, :]
    fine_phase = jnp.arange(128, dtype=jnp.int32).astype(F32)[:, None] * freq[None, :]
    phase = jnp.concatenate([coarse_phase, fine_phase])
    info = jnp.stack([head_index, own_length]).astype(jnp.int32)
    count = pairs * rows
    half = width // 2

    def kernel(info_ref, sin_ref, cos_ref, table_ref, turned_ref, own_ref, mask_ref):
        sin_b, cos_b = sin_ref[pairs * steps :, :], cos_ref[pairs * steps :, :]
        for a in range(pairs * steps):
            here = slice(128 * a, 128 * a + 128)
            sin_a, cos_a = sin_ref[a : a + 1, :], cos_ref[a : a + 1, :]
            sin = sin_a * cos_b + cos_a * sin_b
            cos = cos_a * cos_b - sin_a * sin_b
            table_ref[here, :half] = sin.astype(BF)
            table_ref[here, half:] = cos.astype(BF)
            turned_ref[:half, here] = sin.T.astype(BF)
            turned_ref[half:, here] = cos.T.astype(BF)
            if a < steps:
                own_ref[0, here, :] = cos
                own_ref[1, here, :] = sin
            at = lax.broadcasted_iota(jnp.int32, (1, 128), 1)
            at = at + ((info_ref[0] ^ (a // steps)) * rows + 128 * (a % steps))
            mask_ref[0:1, here] = jnp.where(at < info_ref[1], 0.0, -1e30)

    return run(
        kernel,
        [info, jnp.sin(phase), jnp.cos(phase)],
        [shaped((count, width), BF), shaped((width, count), BF), shaped((2, rows, half), F32), shaped((1, count), F32)],
        "tables",
        specs=[SMEM, VMEM, VMEM],
    )


def prepare(ffn1_out, dw_kernel, norm_gain, norm_bias, pos_bias, att_proj, att_out, ffn2_in, ffn2_out, conv_in, conv_out):
    head_dim = att_out.shape[1]

    dw_kernel = dw_kernel.T

    def kernel(
        out1_ref, dw_ref, gain_ref, bias_ref, posb_ref, proj_ref, att_ref, in2_ref, out2_ref, cin_ref, cout_ref,
        b_ref, t_ref, pack_ref, square_ref, pos_ref,
    ):
        b_ref[0:64, :] = out1_ref[...]
        square_ref[...] = jnp.zeros_like(square_ref)
        square_ref[GAIN:BIAS, 0:16] = gain_ref[...].astype(F32)
        square_ref[BIAS:POS_BIAS, 0:16] = bias_ref[...].astype(F32)
        square_ref[POS_BIAS : POS_BIAS + 2, 0:16] = posb_ref[...].astype(F32)
        square_ref[...] = square_ref[...].T
        square_ref[0:16, 0:GAIN] = dw_ref[...].astype(F32)
        turned = square_ref[0:16, :]
        b_ref[64:72, :] = jnp.concatenate([turned[0:8], turned[8:16], jnp.zeros((8, 256), F32)], axis=1).astype(BF)
        both = [proj_ref[h].astype(F32) for h in range(2)]
        for k in range(3):
            columns = slice(k * head_dim, k * head_dim + head_dim)
            t_ref[:, 128 * k : 128 * k + 128] = jnp.concatenate([p[:, columns] for p in both], axis=1).astype(BF)
        square_ref[...] = jnp.zeros_like(square_ref)
        square_ref[0:64, 0:64] = att_ref[0].astype(F32)
        square_ref[64:128, 0:64] = att_ref[1].astype(F32)
        t_ref[:, 384:512] = square_ref[...].T[0:64].astype(BF)
        pos_ref[...] = jnp.concatenate([p[:, 3 * head_dim :] for p in both], axis=1)
        for k in range(2):
            t_ref[32 * k : 32 * k + 32, 512:640] = pos_ref[pl.ds(k, 32, stride=2), :].astype(BF)
        for k in range(4):
            pack_ref[16 * k : 16 * k + 16, :] = in2_ref[:, 512 * k : 512 * k + 512]
        pack_ref[64:128, :] = out2_ref[...]
        for k in range(2):
            pack_ref[128 + 16 * k : 144 + 16 * k, :] = cin_ref[:, 512 * k : 512 * k + 512]
        pack_ref[160:176, :] = cout_ref[...]

    return run(
        kernel,
        [ffn1_out, dw_kernel, norm_gain, norm_bias, pos_bias, att_proj, att_out, ffn2_in, ffn2_out, conv_in, conv_out],
        [shaped((72, 512), BF), shaped((64, 640), BF), shaped((176, 512), BF)],
        "prepare",
        specs=[whole(a) for a in (ffn1_out, dw_kernel, norm_gain, norm_bias, pos_bias, att_proj, att_out)]
        + [whole(a) for a in (ffn2_in, ffn2_out, conv_in, conv_out)],
        grid=(1,),
        scratch=[pltpu.VMEM((128, 128), F32), pltpu.VMEM((64, 128), F32)],
        limit=60,
    )


def own_terms(terms):
    def spec(array):
        lead = len(array.shape) - 2
        return pl.BlockSpec((1,) * lead + array.shape[lead:], lambda *_: (0,) * (lead + 2))

    return list(terms), [spec(t) for t in terms]


def add_terms(refs):
    rows, columns = refs[0].shape[-2:]
    total = refs[0][...].reshape(rows, columns).astype(F32)
    for ref in refs[1:]:
        total = total + ref[...].reshape(rows, columns).astype(F32)
    return total


def finish_first(terms_a, terms_b):
    inputs, specs = own_terms(terms_a + terms_b)

    def kernel(*refs):
        in_ref, out_ref, dw_ref, gain_ref, bias_ref, posb_ref, square_ref = refs[12:]
        total = add_terms(refs[:6])
        for k in range(4):
            in_ref[:, 512 * k : 512 * k + 512] = total[16 * k : 16 * k + 16, :]
        square_ref[...] = jnp.zeros_like(square_ref)
        square_ref[0:8, :] = total[64:72, 0:128]
        square_ref[8:16, :] = total[64:72, 128:256]
        turned = square_ref[...].T
        dw_ref[...] = square_ref[0:16, 0:GAIN]
        gain_ref[...] = turned[GAIN:BIAS, 0:16]
        bias_ref[...] = turned[BIAS:POS_BIAS, 0:16]
        posb_ref[...] = turned[POS_BIAS : POS_BIAS + 2, 0:16]
        out_ref[...] = add_terms(refs[6:12])

    outs = [(16, 2048), (64, 512), (16, 32), (6, 16), (6, 16), (2, 16)]
    rows_in, rows_out, taps, *rest = run(
        kernel,
        inputs,
        [shaped(o, F32) for o in outs],
        "finish_first",
        specs=specs,
        grid=(1,),
        scratch=[pltpu.VMEM((128, 128), F32)],
    )
    return rows_in, rows_out, taps.T, *rest


def finish_attention(terms):
    inputs, specs = own_terms(terms)

    def kernel(*refs):
        proj_ref, out_ref, cin_ref, square_ref, pos_ref = refs[len(inputs) :]
        total = add_terms(refs[: len(inputs)])
        square_ref[...] = jnp.zeros_like(square_ref)
        square_ref[0:64, :] = total[:, 384:512]
        turned = square_ref[...].T
        for k in range(2):
            pos_ref[pl.ds(k, 32, stride=2), :] = total[32 * k : 32 * k + 32, 512:640]
        for h in range(2):
            for k in range(3):
                at = 128 * k + 64 * h
                proj_ref[h, :, 64 * k : 64 * k + 64] = total[:, at : at + 64]
            proj_ref[h, :, 192:256] = pos_ref[:, 64 * h : 64 * h + 64]
            out_ref[h] = turned[64 * h : 64 * h + 64, 0:64]
        for k in range(4):
            cin_ref[:, 256 * k : 256 * k + 256] = total[16 * k : 16 * k + 16, 640:896]

    return run(
        kernel,
        inputs,
        [shaped((2, 64, 256), F32), shaped((2, 64, 64), F32), shaped((16, 1024), F32)],
        "finish_attention",
        specs=specs,
        grid=(1,),
        scratch=[pltpu.VMEM((128, 128), F32), pltpu.VMEM((64, 128), F32)],
    )


def finish_middle(sums):
    def kernel(sum_ref, in_ref, out_ref, conv_ref):
        for k in range(4):
            in_ref[:, 512 * k : 512 * k + 512] = sum_ref[16 * k : 16 * k + 16, :].astype(F32)
        out_ref[...] = sum_ref[64:128, :].astype(F32)
        conv_ref[...] = sum_ref[128:144, :].astype(F32)

    return run(
        kernel,
        [sums],
        [shaped((16, 2048), F32), shaped((64, 512), F32), shaped((16, 512), F32)],
        "finish_middle",
    )


def small_shard(dw_kernel, norm_gain, norm_bias, pos_bias):
    stacked = jnp.concatenate([dw_kernel, norm_gain, norm_bias, pos_bias], axis=0)
    return jnp.pad(stacked.T, ((0, 0), (0, 128 - stacked.shape[0])))


def att_shard(att_proj, att_out):
    two, rows, four = att_proj.shape
    head_dim = four // 4
    parts = att_proj.reshape(two, rows, 4, head_dim).transpose(1, 2, 0, 3)
    parts = parts.reshape(rows, 4, two * head_dim)
    out_t = att_out.transpose(2, 0, 1).reshape(rows, two * head_dim)
    turned = parts[:, 3].reshape(rows // 2, 2, two * head_dim).transpose(1, 0, 2)
    turned = turned.reshape(rows, two * head_dim)
    return jnp.concatenate([parts[:, 0], parts[:, 1], parts[:, 2], out_t, turned], axis=1)


def column_chunks(array):
    rows, columns = array.shape
    return array.reshape(rows, columns // 512, 512).transpose(1, 0, 2)


def xor_order(array, index):
    bit = 1
    while bit < array.shape[0]:
        flipped = jnp.stack([array[i ^ bit] for i in range(array.shape[0])])
        array = jnp.where((index & bit) != 0, flipped, array)
        bit *= 2
    return array


def rows_of(shard):
    return lax.all_gather(shard, BOTH, axis=0, tiled=True)


def sum_rows(grad):
    return lax.psum_scatter(grad.astype(F32), BOTH, scatter_dimension=0, tiled=True)


def local(
    frames_in,
    cotangent,
    lengths,
    sample_weight,
    ffn1_in,
    ffn1_out,
    att_proj,
    att_out,
    pos_bias,
    conv_in,
    dw_kernel,
    conv_out,
    ffn2_in,
    ffn2_out,
    norm_gain,
    norm_bias,
):
    row_count, model_width = frames_in.shape
    pairs = lax.axis_size("heads")
    batches = lax.axis_size("batch")
    head_index = lax.axis_index("heads")
    batch_index = lax.axis_index("batch")
    channels = ffn1_in.shape[0]
    fast = channels == 16 and batches == 8 and pairs == 4
    kernel_len = dw_kernel.shape[0]
    head_dim = att_out.shape[1]
    width = model_width // batches

    utter_ids = jnp.arange(lengths.shape[0], dtype=jnp.int32)
    own_length = jnp.sum(jnp.where(utter_ids == batch_index, lengths, 0))
    own_weight = jnp.sum(jnp.where(utter_ids == batch_index, sample_weight, 0)).astype(F32) * 0.25
    total_valid = jnp.sum(lengths).astype(F32)
    ints = jnp.stack([own_length, head_index * row_count]).astype(jnp.int32)
    floats = jnp.stack([own_weight, total_valid])

    if fast:
        shard_b, shard_t, pack = prepare(
            ffn1_out, dw_kernel, norm_gain, norm_bias, pos_bias, att_proj, att_out, ffn2_in, ffn2_out, conv_in, conv_out
        )
        held_a, held_b = gather_depth(ffn1_in), gather_depth(shard_b)
        held_t = jnp.stack([shard_t, swap(shard_t, "heads", 2)])
        held_a, held_b, held_t = lax.optimization_barrier((held_a, held_b, held_t))
        side_a, side_b, deep_t = swap(held_a, "batch", 1), swap(held_b, "heads", 2), swap(held_t, "batch", 4)
        side_a, side_b, deep_t = lax.optimization_barrier((side_a, side_b, deep_t))
        held_a, held_b, held_t = (jnp.concatenate(p) for p in ((held_a, side_a), (held_b, side_b), (held_t, deep_t)))
        side_a, side_b, deep_t = swap(held_a, "heads", 2), swap(held_b, "batch", 1), swap(held_t, "batch", 2)
        table, table_t, own_turn, key_mask = tables(behind(head_index, held_a, held_b), own_length, row_count, model_width)
        table, table_t, own_turn, key_mask, ints, floats, side_a, side_b, deep_t = lax.optimization_barrier(
            (table, table_t, own_turn, key_mask, ints, floats, side_a, side_b, deep_t)
        )
        held_t = jnp.concatenate([held_t, deep_t])
        side_t = swap(held_t, "batch", 1)
        pack = lax.all_gather(behind(pack, held_a, held_b), BOTH, axis=0)
        win, wout, small_t, pos_b = place_first(
            (held_a, side_a, swap(held_a, "heads", 1), swap(side_a, "heads", 1)),
            (held_b, side_b, swap(held_b, "heads", 1), swap(side_b, "heads", 1)),
        )
        x1, n1 = ffn1_forward(frames_in, win, wout, small_t)
        held_t, side_t = behind(held_t, n1), behind(side_t, n1)
        sides_t = held_t, side_t
        tw, pos_w = place_attention(sides_t + tuple(swap(t, "heads", 1) for t in sides_t))
        conv_in_w = middle_w = [pack]
    else:
        table, table_t, own_turn, key_mask = tables(head_index, own_length, row_count, model_width)
        small = small_shard(dw_kernel, norm_gain, norm_bias, pos_bias)
        att_part = att_shard(att_proj, att_out)
        win, wout = column_chunks(rows_of(ffn1_in)), rows_of(ffn1_out)
        small_t = rows_of(small).T.astype(F32)
        pos_b = small_t[POS_BIAS : POS_BIAS + 2].reshape(2, batches, pairs, channels).transpose(2, 0, 1, 3)
        pos_b = pos_b.reshape(pairs, 2, 2, head_dim).transpose(0, 2, 1, 3).reshape(pairs, 2, 2 * head_dim)
        pos_b = xor_order(pos_b, head_index)
        att_all = lax.all_gather(lax.all_gather(att_part, "batch", axis=0), "heads", axis=0)
        att_all = xor_order(att_all, head_index)
        tw = att_all[..., :512].reshape(pairs, model_width, 512)
        pos_w = att_all[..., 512:].reshape(pairs, batches, 2, width // 2, 128).transpose(0, 2, 1, 3, 4)
        pos_w = pos_w.reshape(pairs, model_width, 128)
        halves_in = column_chunks(rows_of(conv_in))
        conv_in_w = [halves_in[0], halves_in[1]]
        middle_w = [
            column_chunks(rows_of(ffn2_in)),
            rows_of(ffn2_out).reshape(4, 512, model_width),
            rows_of(conv_out),
        ]

    if not fast:
        x1, n1 = ffn1_forward(frames_in, win, wout, small_t)
    across = swap(n1, "heads", 2)
    keys = [n1, swap(n1, "heads", 1), across, swap(across, "heads", 1)]
    weights, mixed, scale, kv, queries, after_att, n2 = att_forward(
        key_mask, keys, x1, small_t, tw, pos_w, pos_b, own_turn, table_t
    )
    glu, gated, conv_in_w = gate_forward(ints, n2, conv_in_w)
    rim = halo(glu)
    depth, sums = conv_forward(ints, glu, rim, small_t)
    sums = sum_over(sum_over(sums, "heads"), "batch")
    layer_out, upstream, raw, gsum, mid_rows, pre, act, dhid, branch, swish, low = middle(
        ints, floats, depth, sums, after_att, cotangent, small_t, middle_w
    )

    gsum = sum_over(gsum, "heads")
    pre = behind(pre, gsum)
    gsum = sum_over(gsum, "batch")
    mid_grads = middle_grads(fast, pre, act, dhid, branch, swish, low)
    positions = head_index * row_count + jnp.arange(row_count, dtype=jnp.int32)
    row_valid = (positions < own_length).astype(F32)[:, None]
    mean_bn = sums[0] / total_valid
    grad_first = (gsum[0] - 2.0 * mean_bn * gsum[1]) / total_valid
    grad_second = gsum[1] / total_valid
    raw = behind(raw, *mid_grads)
    depth_low = (raw + row_valid * (grad_first + 2.0 * depth * grad_second)).astype(BF)
    depth_rim = halo(depth_low)
    if fast:
        mid = lax.psum_scatter(mid_grads[0].reshape(32 * 144, 512), BOTH, scatter_dimension=0, tiled=True)
    upstream, dgated, conv_rows = conv_backward(
        ints, glu, rim, depth_low, depth_rim, small_t, gated, conv_in_w, after_att, upstream
    )
    near, far, home, grad_bias, *att_grads = att_backward(
        fast, upstream, n2, dgated, keys, mixed, scale, weights, kv, queries, tw, pos_w, own_turn, table
    )
    near = swap(near, "heads", 1)
    moving = (far.astype(F32) + near[1].astype(F32)).astype(BF)
    far = swap(moving, "heads", 2)
    grad_bias = xor_order(grad_bias, head_index).reshape(pairs, 2, 2, head_dim).transpose(0, 2, 1, 3)
    grad_bias = grad_bias.reshape(pairs, 2, batches, channels).transpose(1, 2, 0, 3).reshape(2, model_width)
    if fast:
        heard = swap(behind(att_grads[1], near), "heads", 1)
        home = behind(home, heard)
        t = Exchange(att_grads[0], behind(heard, moving), steps_attention())
        send_all([t], keep=True)
    again = ffn1_again(frames_in, x1, win, wout, small_t, home, near)
    frames_grad, *first_grads = ffn1_backward(
        fast, again, upstream, far, small_t, conv_rows, mid_rows, grad_bias
    )

    if fast:
        *first_grads, t.terms[-1] = lax.optimization_barrier((*first_grads, t.terms[-1]))
        own_ffn2_a, own_ffn2_b, own_conv_b = finish_middle(mid)
        a_far, a_own, b_far, b_own = first_grads
        a = Exchange(a_own, swap(a_far, "heads", 1), steps_first("xy"))
        b = Exchange(b_own, swap(b_far, "heads", 1), steps_first("yx"))
        t.terms[-1] = behind(t.terms[-1], mid)
        for group in ((a, b, t), (a, b, t), (a, b, t), (a, b)):
            send_all(group)
        own_proj, own_out, own_conv_a = finish_attention(t.terms)
        own_ffn1_a, own_ffn1_b, own_taps, own_gain, own_bias, own_pos = finish_first(a.terms, b.terms)
    else:

        def to_rows(chunks):
            rows = chunks.shape[1]
            return sum_rows(chunks.transpose(1, 0, 2).reshape(rows, -1))

        own_ffn2_a = to_rows(mid_grads[0])
        own_ffn2_b = sum_rows(mid_grads[1].reshape(-1, model_width))
        own_conv_b = sum_rows(mid_grads[2])
        tw_grad, pos_grad, conv_grad = att_grads
        own_conv_a = sum_rows(conv_grad)
        pos_grad = pos_grad.reshape(pairs, 2, batches, width // 2, 128).transpose(0, 2, 1, 3, 4)
        grad_att = jnp.concatenate([tw_grad, pos_grad.reshape(pairs, model_width, 128)], axis=2)
        grad_att = xor_order(grad_att, head_index).astype(F32)
        own_att = lax.psum_scatter(
            lax.psum_scatter(grad_att, "batch", scatter_dimension=1, tiled=True),
            "heads",
            scatter_dimension=0,
            tiled=True,
        )[0]
        own_ffn1_a, own_ffn1_b = to_rows(first_grads[0]), sum_rows(first_grads[1])
        own_small = sum_rows(first_grads[2])
        own_small = own_small.T
        turned = own_att[:, 512:640].reshape(2, width // 2, 128).transpose(1, 0, 2).reshape(width, 128)
        parts = jnp.stack([own_att[:, :128], own_att[:, 128:256], own_att[:, 256:384], turned], axis=1)
        own_proj = parts.reshape(width, 4, 2, head_dim).transpose(2, 0, 1, 3)
        own_proj = own_proj.reshape(2, width, 4 * head_dim)
        own_out = own_att[:, 384:512].T.reshape(2, head_dim, width)
        own_pos = own_small[POS_BIAS : POS_BIAS + 2]
        own_taps = own_small[:kernel_len]
        own_gain, own_bias = own_small[GAIN : GAIN + 6], own_small[BIAS : BIAS + 6]
    return (
        layer_out,
        frames_grad,
        own_ffn1_a,
        own_ffn1_b,
        own_proj,
        own_out,
        own_pos,
        own_conv_a,
        own_taps,
        own_conv_b,
        own_ffn2_a,
        own_ffn2_b,
        own_gain,
        own_bias,
    )


def solution(mesh):
    placed = (
        P(("batch", "heads"), None),
        P(("batch", "heads"), None),
        P(),
        P(),
        P(("batch", "heads"), None),
        P(("batch", "heads"), None),
        P("heads", "batch", None),
        P("heads", None, "batch"),
        P("heads", "batch"),
        P(("batch", "heads"), None),
        P(None, ("batch", "heads")),
        P(("batch", "heads"), None),
        P(("batch", "heads"), None),
        P(("batch", "heads"), None),
        P(None, ("batch", "heads")),
        P(None, ("batch", "heads")),
    )
    return jax.shard_map(
        local,
        mesh=mesh,
        in_specs=placed,
        out_specs=(
            P(("batch", "heads"), None),
            P(("batch", "heads"), None),
            P(("batch", "heads"), None),
            P(("batch", "heads"), None),
            P("heads", "batch", None),
            P("heads", None, "batch"),
            P("heads", "batch"),
            P(("batch", "heads"), None),
            P(None, ("batch", "heads")),
            P(("batch", "heads"), None),
            P(("batch", "heads"), None),
            P(("batch", "heads"), None),
            P(None, ("batch", "heads")),
            P(None, ("batch", "heads")),
        ),
        check_vma=False,
    )
```

```python
import math

import jax
import jax.numpy as jnp
from jax import lax
from jax.experimental import pallas as pl
from jax.experimental.pallas import tpu as pltpu
from jax.sharding import PartitionSpec as P

epsilon = 1e-05
BF = jnp.bfloat16
F32 = jnp.float32
BOTH = ("batch", "heads")
CHUNK = 256
HALO = 16
SCALE = 0.125
LOG2E = 1.4426950408889634
GAIN, BIAS, POS_BIAS = 32, 38, 44
KZ = (0, 2, 1, 3)
DIMS = {"y": ("batch", 1), "x": ("heads", 2)}
VMEM_BYTES = 40 * 2**20


def swap(source, axis, mask):
    count = lax.axis_size(axis)
    return lax.ppermute(source, axis, [(i, i ^ mask) for i in range(count)])


def sum_over(source, axis):
    mask = 1
    while mask < lax.axis_size(axis):
        source = source + swap(source, axis, mask)
        mask *= 2
    return source


def halo(cells):
    ends = lax.axis_size("heads") - 1
    rows = cells.shape[0]
    before = lax.ppermute(cells[rows - HALO :], "heads", [(i, i + 1) for i in range(ends)])
    after = lax.ppermute(cells[:HALO], "heads", [(i + 1, i) for i in range(ends)])
    return before, after


def behind(source, *others):
    return lax.optimization_barrier((source,) + others)[0]


def gather_depth(shard):
    held = shard[None]
    for mask in (4, 2):
        held = jnp.concatenate([held, swap(held, "batch", mask)])
    return held


class Exchange:
    def __init__(self, own, heard, steps):
        self.terms, self.steps = [own, heard], list(steps)

def send_all(group, keep=False):
    inputs, specs, outs, sizes = [], [], [], []
    stays = [[(0,) * len(one.terms)] for one in group] if keep else [[]] * len(group)
    pairs = [(one, parts) for one, stay in zip(group, stays) for parts in [one.steps[0][0]] + [[(k,) for k in s] for s in stay]]
    for one, parts in pairs:
        for term, index in zip(one.terms, parts, strict=True):
            index = index + (slice(None),) * (term.ndim - len(index))
            ends = [(k, 1) if isinstance(k, int) else (k.start // 2, 2) if k.start else (0, n) for k, n in zip(index, term.shape)]
            specs.append(pl.BlockSpec(tuple(e[1] for e in ends), lambda *_, at=tuple(e[0] for e in ends): at))
            inputs.append(term)
        shape = [2 if k.start else n for k, n in zip(index, term.shape) if not isinstance(k, int)]
        outs.append(shaped(tuple(shape), BF))
        sizes.append(len(parts))

    def kernel(*refs):
        at = 0
        for size, out_ref in zip(sizes, refs[-len(outs) :], strict=True):
            value = refs[at][...].reshape(out_ref.shape).astype(F32)
            for ref in refs[at + 1 : at + size]:
                value = value + ref[...].reshape(out_ref.shape).astype(F32)
            out_ref[...] = value.astype(BF)
            at += size

    moving = run(kernel, inputs, outs, "send_all", specs=specs, grid=(1,), limit=24)
    if keep:
        for one, array in zip(group, moving[1::2], strict=True):
            one.terms = [array]
        moving = moving[0::2]
    for one, array in zip(group, moving, strict=True):
        _, axis, mask = one.steps.pop(0)
        one.terms.append(swap(array, axis, mask))
    return moving


def steps_first(order):
    one, two = DIMS[order[0]], DIMS[order[1]]
    return [
        ([(1,), (1,)],) + one,
        ([(0, 1), (0, 1), (1,)],) + two,
        ([(0, 0, slice(2, 4)), (0, 0, slice(2, 4)), (0, slice(2, 4)), (slice(2, 4),)],) + ("batch", 2),
        ([(0, 0, 1), (0, 0, 1), (0, 1), (1,), (1,)],) + ("batch", 4),
    ]


def steps_attention():
    high = slice(2, 4)
    return [
        ([(1,), (1,)], "batch", 1),
        ([(high,), (high,)], "batch", 2),
        ([(1,), (1,), (1,)], "batch", 4),
        ([(0, 1), (0, 1), (0, 1), (1,)], "heads", 2),
    ]


def dot(left, right):
    return jnp.dot(left, right, preferred_element_type=F32)


def dot_nt(left, right):
    return lax.dot_general(left, right, (((1,), (1,)), ((), ())), preferred_element_type=F32)


def dot_tn(left, right):
    return lax.dot_general(left, right, (((0,), (0,)), ((), ())), preferred_element_type=F32)


def norm(source):
    center = source - jnp.mean(source, axis=-1, keepdims=True)
    scale = lax.rsqrt(jnp.mean(center * center, axis=-1, keepdims=True) + epsilon)
    return center * scale, scale


def norm_back(upstream, normed, scale, gain_row):
    inner = upstream * gain_row
    mean = jnp.mean(inner, axis=-1, keepdims=True)
    along = jnp.mean(inner * normed, axis=-1, keepdims=True)
    gain_grad = jnp.sum(upstream * normed, axis=0, keepdims=True)
    return scale * (inner - mean - normed * along), gain_grad, jnp.sum(upstream, axis=0, keepdims=True)


def row(small_ref, index):
    return small_ref[index : index + 1, :]


def place():
    batch_at = lax.axis_index("batch")
    heads_at = lax.axis_index("heads")
    return batch_at // 2, batch_at % 2, heads_at // 2, heads_at % 2


def block_index(kz, ky, kx, kc):
    z, y, x, c = place()
    return ((z ^ kz) * 2 + (y ^ ky)) * 4 + (x ^ kx) * 2 + (c ^ kc)


def part(index, size):
    return pl.ds(pl.multiple_of(index * size, size), size)


def valid_rows(ints_ref, rows):
    steps = lax.broadcasted_iota(jnp.int32, (rows, 1), 0) + ints_ref[1]
    return (steps < ints_ref[0]).astype(F32)


def whole(array):
    return pl.BlockSpec(array.shape, lambda *_: (0,) * len(array.shape), pipeline_mode=pl.Buffered(1))


def per_pair(array):
    return pl.BlockSpec((1,) + array.shape[1:], lambda h: (h,) + (0,) * (len(array.shape) - 1))


def shaped(shape, kind):
    return jax.ShapeDtypeStruct(shape, kind)


SMEM = pl.BlockSpec(memory_space=pltpu.SMEM)


VMEM = pl.BlockSpec(memory_space=pltpu.VMEM)


def cost(time):
    return pl.CostEstimate(flops=int(time * 10**9), bytes_accessed=2**12, transcendentals=0)


def run(kernel, inputs, outs, name, specs=None, grid=(), scratch=(), limit=24, time=0.01):
    return pl.pallas_call(
        kernel,
        grid=grid,
        in_specs=specs or [VMEM] * len(inputs),
        out_specs=[whole(o) for o in outs] if grid else [VMEM] * len(outs),
        out_shape=outs,
        scratch_shapes=list(scratch),
        compiler_params=pltpu.CompilerParams(vmem_limit_bytes=limit * 2**20),
        cost_estimate=cost(time),
        name=name,
    )(*inputs)


def fetch(*arrays):
    def kernel(*refs):
        count = len(arrays)
        copies = [pltpu.make_async_copy(refs[i], refs[count + i], refs[-1].at[i]) for i in range(count)]
        for copy in copies:
            copy.start()
        for copy in copies:
            copy.wait()

    return run(
        kernel,
        list(arrays),
        [shaped(a.shape, a.dtype) for a in arrays],
        "fetch",
        specs=[pl.BlockSpec(memory_space=pltpu.HBM)] * len(arrays),
        scratch=[pltpu.SemaphoreType.DMA((len(arrays),))],
    )


def place_first(sets_a, sets_b):
    def kernel(*refs):
        a_refs, b_refs = refs[:4], refs[4:8]
        win_ref, wout_ref, small_ref, pb_ref, chan_ref, stage_ref = refs[8:]
        for k in range(4):
            for i in range(8):
                at = block_index(KZ[i % 4], i // 4, k & 1, k >> 1)
                for column in range(4):
                    win_ref[column, part(at, 16), :] = a_refs[k][i, :, 512 * column : 512 * column + 512]
                at = block_index(KZ[i % 4], k & 1, i // 4, k >> 1)
                wout_ref[part(at, 64), :] = b_refs[k][i, 0:64, :]
                small = b_refs[k][i, 64:72, 0:256].astype(F32)
                chan_ref[part(at, 16), :] = jnp.concatenate([small[:, 0:128], small[:, 128:256]], axis=0)
        small_ref[...] = chan_ref[...].T
        for mask in range(4):
            pair = lax.axis_index("heads") ^ mask
            for b in range(8):
                stage_ref[16 * b : 16 * b + 16, :] = chan_ref[part(4 * b + pair, 16), :]
            one, two = (stage_ref[...].T[at : at + 1] for at in (POS_BIAS, POS_BIAS + 1))
            pb_ref[mask, 0:1, :] = jnp.concatenate([one[:, :64], two[:, :64]], axis=1)
            pb_ref[mask, 1:2, :] = jnp.concatenate([one[:, 64:], two[:, 64:]], axis=1)

    return run(
        kernel,
        list(sets_a) + list(sets_b),
        [shaped((4, 512, 512), BF), shaped((2048, 512), BF), shaped((128, 512), F32), shaped((4, 2, 128), F32)],
        "place_first",
        scratch=[pltpu.VMEM((512, 128), F32), pltpu.VMEM((128, 128), F32)],
    )


def place_attention(sets):
    def kernel(*refs):
        tw_ref, pos_ref = refs[4:]
        z, y, _, _ = place()
        for k in range(4):
            for i in range(8):
                pair = (i % 2) * 2 + (k >> 1)
                at = (z ^ KZ[i // 2]) * 2 + (y ^ (k & 1))
                tw_ref[pair, part(at, 64), :] = refs[k][i, :, 0:512]
                pos_ref[pair, part(at, 32), :] = refs[k][i, 0:32, 512:640]
                pos_ref[pair, part(at + 8, 32), :] = refs[k][i, 32:64, 512:640]

    return run(
        kernel, list(sets), [shaped((4, 512, 512), BF), shaped((4, 512, 128), BF)], "place_attention"
    )


def ffn1_forward(frames, win, wout, small):
    def kernel(x_ref, win_ref, wout_ref, small_ref, out_ref, normed_ref):
        source = x_ref[...].astype(F32)
        normed, _ = norm(source)
        pre = (normed * row(small_ref, GAIN) + row(small_ref, BIAS)).astype(BF)
        total = jnp.zeros_like(source)
        for column in range(win_ref.shape[0]):
            hidden = dot(pre, win_ref[column])
            active = (hidden * jax.nn.sigmoid(hidden)).astype(BF)
            total = total + dot(active, wout_ref[512 * column : 512 * column + 512, :])
        source = source + 0.5 * total
        out_ref[...] = source
        normed, _ = norm(source)
        normed_ref[...] = (normed * row(small_ref, GAIN + 1) + row(small_ref, BIAS + 1)).astype(BF)

    return run(
        kernel,
        [frames, win, wout, small],
        [shaped(frames.shape, F32), shaped(frames.shape, BF)],
        "ffn1_forward",
        time=3,
    )


def halves(first, value):
    zero = jnp.zeros_like(value)
    return jnp.where(first, value, zero), jnp.where(first, zero, value)


def att_forward_kernel(
    mask_ref, own_ref, k1_ref, k2_ref, k3_ref, x1_ref, small_ref, tw_ref, pos_ref, pb_ref, cs_ref, et_ref,
    w_ref, o_ref, scale_ref, kv_ref, q_ref, att_ref, n2_ref, right_ref, value_ref, total_ref,
):
    rows, width = own_ref.shape
    half = cs_ref.shape[2]
    step = pl.program_id(0)
    tw = tw_ref[0]

    @pl.when(step == 0)
    def _():
        right_ref[0:width, :] = et_ref[...]
        value_ref[:, 128:256] = jnp.ones((value_ref.shape[0], 128), BF)
        total_ref[...] = x1_ref[...]

    for k, ref in enumerate((own_ref, k1_ref, k2_ref, k3_ref)):
        here = slice(k * rows, k * rows + rows)
        kv = dot(ref[...], tw[:, 128:384])
        kv_ref[0, here, :] = kv.astype(BF)
        right_ref[width : width + 128, here] = kv[:, :128].T.astype(BF)
    value_ref[:, 0:128] = kv_ref[0, :, 128:]
    query = dot(own_ref[...], tw[:, :128])
    qc = (query + pb_ref[0, 0:1, :]).astype(BF)
    qp = (query + pb_ref[0, 1:2, :]).astype(BF)
    q_ref[0, 0] = qc
    q_ref[0, 1] = qp
    first = lax.broadcasted_iota(jnp.int32, (rows, 128), 1) < 64
    cos, sin = cs_ref[0], cs_ref[1]
    mask = mask_ref[...]
    outs = []
    for qc_h, qp_h in zip(halves(first, qc), halves(first, qp)):
        turned = dot_nt(qp_h, pos_ref[0]) * (SCALE * LOG2E)
        us, uc = turned[:, :half], turned[:, half:]
        left = jnp.concatenate(
            [
                (us * cos + uc * sin).astype(BF),
                (uc * cos - us * sin).astype(BF),
                (qc_h.astype(F32) * (SCALE * LOG2E)).astype(BF),
            ],
            axis=1,
        )
        parts = []
        for r in range(0, rows, CHUNK):
            scores = dot(left[r : r + CHUNK], right_ref[...]) + mask
            top = jnp.max(scores, axis=1, keepdims=True)
            weights = jnp.exp2(scores - top).astype(BF)
            w_ref[0, len(outs), r : r + CHUNK, :] = weights
            parts.append(dot(weights, value_ref[...]))
        outs.append(jnp.concatenate(parts, axis=0))
    scale = 1.0 / jnp.where(first, outs[0][:, 128:], outs[1][:, 128:])
    scale_ref[0] = scale
    mixed = jnp.where(first, outs[0][:, :128], outs[1][:, :128]) * scale
    o_ref[0] = mixed
    total_ref[...] += dot_nt(mixed.astype(BF), tw[:, 384:512])

    @pl.when(step == pl.num_programs(0) - 1)
    def _():
        after = total_ref[...]
        att_ref[...] = after
        normed, _ = norm(after)
        n2_ref[...] = (normed * row(small_ref, GAIN + 2) + row(small_ref, BIAS + 2)).astype(BF)


def att_forward(mask, keys, x1, small, tw, pos, pb, cs, et):
    rows, width = x1.shape
    count = mask.shape[1]
    paired = [
        shaped((4, 2, rows, count), BF),
        shaped((4, rows, 128), F32),
        shaped((4, rows, 128), F32),
        shaped((4, count, 256), BF),
        shaped((4, 2, rows, 128), BF),
    ]
    shared = [shaped((rows, width), F32), shaped((rows, width), BF)]
    return pl.pallas_call(
        att_forward_kernel,
        grid=(4,),
        in_specs=[whole(mask)]
        + [whole(k) for k in keys]
        + [whole(x1), whole(small), per_pair(tw), per_pair(pos), per_pair(pb), whole(cs), whole(et)],
        out_specs=[per_pair(a) for a in paired] + [whole(a) for a in shared],
        out_shape=paired + shared,
        scratch_shapes=[
            pltpu.VMEM((width + 128, count), BF),
            pltpu.VMEM((count, 256), BF),
            pltpu.VMEM((rows, width), F32),
        ],
        compiler_params=pltpu.CompilerParams(vmem_limit_bytes=56 * 2**20),
        cost_estimate=cost(40),
        name="att_forward",
    )(mask, *keys, x1, small, tw, pos, pb, cs, et)


def att_backward_kernel(fast, *refs):
    (up_ref, n2_ref, dg_ref, own_ref, k1_ref, k2_ref, k3_ref, o_ref, scale_ref, w_ref, kv_ref, q_ref, tw_ref, pos_ref, cs_ref,
     e_ref, near_ref, far_ref, home_ref, db_ref) = refs[:20]
    outs, (dr_ref, dn_ref, dq_ref, og_ref, dconv_ref, tw_grad_ref, pos_grad_ref) = refs[20:-7], refs[-7:]
    rows, width = up_ref.shape
    half = cs_ref.shape[2]
    count = dn_ref.shape[1]
    step = pl.program_id(0)

    @pl.when(step == 0)
    def _():
        og_ref[...] = up_ref[...].astype(BF)
        dn_ref[...] = jnp.zeros_like(dn_ref)
        dq_ref[...] = jnp.zeros_like(dq_ref)
        dconv_ref[...] = dot_tn(n2_ref[...], dg_ref[...]).astype(BF)

    og = og_ref[...]
    tw = tw_ref[0]
    do_f = dot(og, tw[:, 384:512]).astype(BF).astype(F32) * scale_ref[0]
    do = do_f.astype(BF)
    key, value = kv_ref[0, :, :128], kv_ref[0, :, 128:]
    first = lax.broadcasted_iota(jnp.int32, (rows, 128), 1) < 64
    mixed = o_ref[0]
    do_t = do_f.T.astype(BF)
    qc_t = (q_ref[0, 0].astype(F32) * SCALE).T.astype(BF)
    qp_t = q_ref[0, 1].astype(F32).T.astype(BF)
    cos, sin = cs_ref[0], cs_ref[1]
    dqcs, dqps, dks, dvs, dps = [], [], [], [], []
    for head, (do_h, inner_h) in enumerate(zip(halves(first, do), halves(first, do_f * mixed))):
        mine = slice(head * 64, head * 64 + 64)
        inner = jnp.sum(inner_h, axis=1, keepdims=True)
        for r in range(0, rows, CHUNK):
            dw = dot_nt(do_h[r : r + CHUNK], value)
            weights = w_ref[0, head, r : r + CHUNK, :].astype(F32)
            dr_ref[r : r + CHUNK, :] = (weights * (dw - inner[r : r + CHUNK])).astype(BF)
        dr = dr_ref[...]
        turned = dot(dr, e_ref[...]) * SCALE
        dqcs.append(dot(dr, key) * SCALE)
        dks.append(dot(qc_t[mine], dr).astype(BF))
        dvs.append(dot(do_t[mine], w_ref[0, head]).astype(BF))
        gs, gc = turned[:, :half], turned[:, half:]
        du = jnp.concatenate(
            [(gs * cos - gc * sin).astype(BF), (gs * sin + gc * cos).astype(BF)], axis=1
        )
        dqps.append(dot(du, pos_ref[0]))
        dps.append(dot(qp_t[mine], du))
    dqc = jnp.where(first, dqcs[0], dqcs[1])
    dqp = jnp.where(first, dqps[0], dqps[1])
    db_ref[0, 0:1, :] = jnp.sum(dqc, axis=0, keepdims=True)
    db_ref[0, 1:2, :] = jnp.sum(dqp, axis=0, keepdims=True)
    dq = dqc + dqp
    dq_low = dq.astype(BF)
    dkv = jnp.concatenate(dks + dvs, axis=0)
    dn_ref[...] += dot(tw[:, 128:384], dkv)
    dq_ref[...] += dot_nt(dq_low, tw[:, :128])
    grad_kv = jnp.zeros((256, width), F32)
    for k, ref in enumerate((own_ref, k1_ref, k2_ref, k3_ref)):
        grad_kv = grad_kv + dot(dkv[:, k * rows : k * rows + rows], ref[...])
    grad_q = dot(dq.T.astype(BF), own_ref[...])
    grad_o = dot(mixed.T.astype(BF), og)
    tw_grad_ref[...] = jnp.concatenate([grad_q, grad_kv, grad_o], axis=0).T.astype(BF)
    pos_grad_ref[...] = jnp.concatenate(dps, axis=0).T.astype(BF)

    if fast:
        z, y, x, c = place()
        pair = (x ^ (step // 2)) * 2 + (c ^ (step % 2))

        def write(pack_ref):
            for ky in range(2):
                for i in range(4):
                    at = (z ^ KZ[i]) * 2 + (y ^ ky)
                    pack_ref[ky, i, 0, :, 0:512] = tw_grad_ref[part(at, 64), :]
                    pack_ref[ky, i, 0, 0:32, 512:640] = pos_grad_ref[part(at, 32), :]
                    pack_ref[ky, i, 0, 32:64, 512:640] = pos_grad_ref[part(at + 8, 32), :]
                    for t in range(4):
                        pack_ref[ky, i, 0, 16 * t : 16 * t + 16, 640:896] = dconv_ref[
                            part(at * 4 + pair, 16), 256 * t : 256 * t + 256
                        ]

        pl.when(step % 2 == 0)(lambda: write(outs[0]))
        pl.when(step % 2 == 1)(lambda: write(outs[1]))
    else:
        outs[0][0] = tw_grad_ref[...]
        outs[1][0] = pos_grad_ref[...]
        outs[2][...] = dconv_ref[...]

    @pl.when(step == pl.num_programs(0) - 1)
    def _():
        for k in range(4):
            grad = dn_ref[:, k * rows : k * rows + rows].T
            if k == 0:
                home_ref[...] = grad + dq_ref[...]
            elif k == 2:
                far_ref[...] = grad.astype(BF)
            else:
                near_ref[k // 2] = grad.astype(BF)


def att_backward(fast, upstream, n2, dgated, keys, mixed, scale, weights, kv, queries, tw, pos, cs, e):
    rows, width = upstream.shape
    count = kv.shape[1]
    shared = [shaped((2, rows, width), BF), shaped((rows, width), BF), shaped((rows, width), F32)]
    paired = [shaped((4, 2, 128), F32)]
    specs = [whole(a) for a in shared] + [per_pair(a) for a in paired]
    outs = shared + paired
    if fast:
        extra = [shaped((2, 4, 2, 64, 896), BF)] * 2
        specs += [pl.BlockSpec((2, 4, 1, 64, 896), lambda h: (0, 0, h // 2, 0, 0))] * 2
    else:
        extra = [shaped((4, width, 512), BF), shaped((4, width, 128), BF), shaped((width, 1024), BF)]
        specs += [per_pair(extra[0]), per_pair(extra[1]), whole(extra[2])]
    return pl.pallas_call(
        lambda *refs: att_backward_kernel(fast, *refs),
        grid=(4,),
        in_specs=[whole(upstream), whole(n2), whole(dgated)]
        + [whole(k) for k in keys]
        + [per_pair(mixed), per_pair(scale), per_pair(weights), per_pair(kv), per_pair(queries), per_pair(tw), per_pair(pos)]
        + [whole(cs), whole(e)],
        out_specs=specs,
        out_shape=outs + extra,
        scratch_shapes=[
            pltpu.VMEM((rows, count), BF),
            pltpu.VMEM((width, count), F32),
            pltpu.VMEM((rows, width), F32),
            pltpu.VMEM((rows, width), BF),
            pltpu.VMEM((width, 1024), BF),
            pltpu.VMEM((width, 512), BF),
            pltpu.VMEM((width, 128), BF),
        ],
        compiler_params=pltpu.CompilerParams(vmem_limit_bytes=VMEM_BYTES),
        cost_estimate=cost(0.01),
        name="att_backward",
    )(upstream, n2, dgated, *keys, mixed, scale, weights, kv, queries, tw, pos, cs, e)


def gate_forward(ints, n2, conv_in):
    rows, width = n2.shape

    def kernel(ints_ref, n2_ref, *refs):
        w_refs, (glu_ref, gated_ref, half_ref) = refs[:2], refs[2:]
        half_ref[0] = w_refs[0][...].reshape(width, width)
        half_ref[1] = w_refs[1][...].reshape(width, width)
        left = dot(n2_ref[...], half_ref[0])
        right = dot(n2_ref[...], half_ref[1])
        gated_ref[:, :width] = left
        gated_ref[:, width:] = right
        glu_ref[...] = (left * jax.nn.sigmoid(right) * valid_rows(ints_ref, rows)).astype(BF)

    if len(conv_in) == 1:
        conv_in = conv_in * 2
        specs = [
            pl.BlockSpec((32, 16, 512), lambda *_, at=at: (0, at, 0), pipeline_mode=pl.Buffered(1)) for at in (8, 9)
        ]
    else:
        specs = [whole(a) for a in conv_in]
    return run(
        kernel,
        [ints, n2] + conv_in,
        [shaped((rows, width), BF), shaped((rows, 2 * width), F32)] + [shaped((2, width, width), BF)],
        "gate_forward",
        specs=[SMEM, whole(n2)] + specs,
        grid=(1,),
        limit=60,
    )


def extend(ext_ref, before_ref, own_ref, after_ref):
    rows = own_ref.shape[0]
    ext_ref[0, 0:HALO, :] = before_ref[...].astype(F32)
    ext_ref[0, HALO : HALO + rows, :] = own_ref[...].astype(F32)
    ext_ref[0, HALO + rows : 2 * HALO + rows, :] = after_ref[...].astype(F32)
    kept = 2 * HALO + rows - 8
    for shift in range(1, 8):
        ext_ref[shift, 0:kept, :] = ext_ref[0, shift : shift + kept, :]


def shifted(ext_ref, start, size, columns):
    return ext_ref[start % 8, start - start % 8 : start - start % 8 + size, columns]


def conv_forward(ints, glu, rim, small):
    rows, width = glu.shape

    def kernel(ints_ref, before_ref, glu_ref, after_ref, small_ref, depth_ref, sums_ref, ext_ref):
        extend(ext_ref, before_ref, glu_ref, after_ref)
        steps = lax.broadcasted_iota(jnp.int32, (64, 1), 0) + ints_ref[1]
        for c in range(0, width, 128):
            one = jnp.zeros((1, 128), F32)
            two = jnp.zeros((1, 128), F32)
            for r in range(0, rows, 64):
                total = jnp.zeros((64, 128), F32)
                for k in range(2 * HALO):
                    total = total + shifted(ext_ref, r + k + 1, 64, slice(c, c + 128)) * small_ref[k : k + 1, c : c + 128]
                depth_ref[r : r + 64, c : c + 128] = total
                kept = jnp.where(steps + r < ints_ref[0], total, 0.0)
                one = one + jnp.sum(kept, axis=0, keepdims=True)
                two = two + jnp.sum(kept * total, axis=0, keepdims=True)
            sums_ref[0:1, c : c + 128] = one
            sums_ref[1:2, c : c + 128] = two

    return run(
        kernel,
        [ints, rim[0], glu, rim[1], small],
        [shaped((rows, width), F32), shaped((2, width), F32)],
        "conv_forward",
        time=4,
        specs=[SMEM] + [VMEM] * 4,
        scratch=[pltpu.VMEM((8, rows + 2 * HALO, width), F32)],
    )


def conv_backward(ints, glu, rim, depth_low, depth_rim, small, gated, conv_in, after_att, upstream):
    rows, width = glu.shape

    def kernel(
        ints_ref, gb_ref, glu_ref, ga_ref, db_ref, d_ref, da_ref, small_ref, gated_ref, att_ref, up_ref, *refs
    ):
        w_ref, out_ref, dg_ref, grads_ref, ext_ref, extd_ref, dglu_ref = refs
        extend(ext_ref, gb_ref, glu_ref, ga_ref)
        extend(extd_ref, db_ref, d_ref, da_ref)
        taps = 2 * HALO
        for c in range(0, width, 128):
            cols = slice(c, c + 128)
            for r in range(0, rows, 64):
                total = jnp.zeros((64, 128), F32)
                for k in range(taps):
                    at = r + taps - 1 - k
                    total = total + shifted(extd_ref, at, 64, cols) * small_ref[k : k + 1, cols]
                dglu_ref[r : r + 64, cols] = total
            for k in range(taps):
                total = jnp.zeros((8, 128), F32)
                for r in range(0, rows, 64):
                    product = shifted(ext_ref, r + k + 1, 64, cols) * shifted(extd_ref, HALO + r, 64, cols)
                    total = total + jnp.sum(product.reshape(8, 8, 128), axis=0)
                grads_ref[k : k + 1, cols] = jnp.sum(total, axis=0, keepdims=True)
        grad = dglu_ref[...] * valid_rows(ints_ref, rows)
        gate = jax.nn.sigmoid(gated_ref[:, width:])
        left = (grad * gate).astype(BF)
        right = (grad * gated_ref[:, :width] * gate * (1.0 - gate)).astype(BF)
        dg_ref[:, :width] = left
        dg_ref[:, width:] = right
        inner = dot_nt(left, w_ref[0]) + dot_nt(right, w_ref[1])
        normed, scale = norm(att_ref[...])
        grad, gain_grad, bias_grad = norm_back(inner, normed, scale, row(small_ref, GAIN + 2))
        out_ref[...] = up_ref[...] + grad
        grads_ref[taps : taps + 1, :] = gain_grad
        grads_ref[taps + 1 : taps + 2, :] = bias_grad

    inputs = [ints, rim[0], glu, rim[1], depth_rim[0], depth_low, depth_rim[1], small, gated]
    return run(
        kernel,
        inputs + [after_att, upstream, conv_in],
        [shaped((rows, width), F32), shaped((rows, 2 * width), BF), shaped((40, width), F32)],
        "conv_backward",
        time=0.01,
        specs=[SMEM] + [VMEM] * (len(inputs) + 2),
        scratch=[pltpu.VMEM((8, rows + 2 * HALO, width), F32)] * 2 + [pltpu.VMEM((rows, width), F32)],
    )


def middle(ints, floats, depth, sums, after_att, cotangent, small, weights):
    rows, width = depth.shape

    def kernel(
        ints_ref, floats_ref, depth_ref, sums_ref, att_ref, cot_ref, small_ref, *refs
    ):
        w_refs = refs[:-12]
        (layer_ref, up_ref, raw_ref, gsum_ref, grads_ref, pre_ref, act_ref, dhid_ref, branch_ref, swish_ref, low_ref,
         hid_ref) = refs[-12:]
        packed = len(w_refs) == 1
        columns = hid_ref.shape[0]

        def w_in(column):
            if packed:
                return w_refs[0][:, 16 * column : 16 * column + 16, :].reshape(width, 512)
            return w_refs[0][column]

        def w_out(column):
            if packed:
                return w_refs[0][8 * column : 8 * column + 8, 64:128, :].reshape(512, width)
            return w_refs[1][column]

        total_valid = floats_ref[1]
        mean_bn = sums_ref[0:1, :] / total_valid
        var_bn = sums_ref[1:2, :] / total_valid - mean_bn * mean_bn
        inv = lax.rsqrt(var_bn + epsilon)
        center = depth_ref[...] - mean_bn
        bn_gain = row(small_ref, GAIN + 5)
        z = center * inv * bn_gain + row(small_ref, BIAS + 5)
        swish = (z * jax.nn.sigmoid(z)).astype(BF)
        swish_ref[...] = swish
        conv_out = w_refs[0][:, 160:176, :].reshape(width, width) if packed else w_refs[2][...]
        after_conv = att_ref[...] + dot(swish, conv_out)
        normed3, scale3 = norm(after_conv)
        pre = (normed3 * row(small_ref, GAIN + 3) + row(small_ref, BIAS + 3)).astype(BF)
        pre_ref[...] = pre
        total = jnp.zeros((rows, width), F32)
        for column in range(columns):
            hidden = dot(pre, w_in(column))
            hid_ref[column] = hidden
            active = (hidden * jax.nn.sigmoid(hidden)).astype(BF)
            act_ref[column] = active
            total = total + dot(active, w_out(column))
        normed4, scale4 = norm(after_conv + 0.5 * total)
        gain4 = row(small_ref, GAIN + 4)
        layer_ref[...] = (normed4 * gain4 + row(small_ref, BIAS + 4)).astype(BF)
        seed = cot_ref[...].astype(F32) * (valid_rows(ints_ref, rows) * floats_ref[0])
        up, gain_grad, bias_grad = norm_back(seed, normed4, scale4, gain4)
        grads_ref[...] = jnp.zeros_like(grads_ref)
        grads_ref[2:3, :] = gain_grad
        grads_ref[3:4, :] = bias_grad
        branch = (0.5 * up).astype(BF)
        branch_ref[...] = branch
        total = jnp.zeros((rows, width), F32)
        for column in range(columns):
            hidden = hid_ref[column]
            gate = jax.nn.sigmoid(hidden)
            grad = dot_nt(branch, w_out(column)) * (gate * (1.0 + hidden * (1.0 - gate)))
            grad = grad.astype(BF)
            dhid_ref[column] = grad
            total = total + dot_nt(grad, w_in(column))
        grad, gain_grad, bias_grad = norm_back(total, normed3, scale3, row(small_ref, GAIN + 3))
        grads_ref[0:1, :] = gain_grad
        grads_ref[1:2, :] = bias_grad
        up = up + grad
        up_ref[...] = up
        low = up.astype(BF)
        low_ref[...] = low
        gate = jax.nn.sigmoid(z)
        dz = dot_nt(low, conv_out) * (gate * (1.0 + z * (1.0 - gate)))
        grads_ref[4:5, :] = jnp.sum(dz * center, axis=0, keepdims=True) * inv
        grads_ref[5:6, :] = jnp.sum(dz, axis=0, keepdims=True)
        raw = dz * (bn_gain * inv)
        raw_ref[...] = raw
        gsum_ref[0:1, :] = -jnp.sum(raw, axis=0, keepdims=True)
        gsum_ref[1:2, :] = jnp.sum(raw * center, axis=0, keepdims=True) * (-0.5 * inv * inv)

    square_f, square = shaped((rows, width), F32), shaped((rows, width), BF)
    wide = shaped((4, rows, 512), BF)
    inputs = [ints, floats, depth, sums, after_att, cotangent, small]
    return run(
        kernel,
        inputs + weights,
        [square, square_f, square_f, shaped((2, width), F32), shaped((8, width), F32)]
        + [square, wide, wide, square, square, square],
        "middle",
        time=8,
        specs=[SMEM, SMEM] + [VMEM] * (len(inputs) - 2 + len(weights)),
        scratch=[pltpu.VMEM((4, rows, 512), F32)],
    )


def middle_grads(fast, pre, act, dhid, branch, swish, low):
    width = pre.shape[1]

    def kernel(pre_ref, act_ref, dhid_ref, branch_ref, swish_ref, low_ref, *outs):
        for column in range(act_ref.shape[0]):
            grad_in = dot_tn(pre_ref[...], dhid_ref[column]).astype(BF)
            grad_out = dot_tn(act_ref[column], branch_ref[...]).astype(BF)
            if fast:
                outs[0][:, 16 * column : 16 * column + 16, :] = grad_in.reshape(32, 16, 512)
                outs[0][8 * column : 8 * column + 8, 64:128, :] = grad_out.reshape(8, 64, 512)
            else:
                outs[0][column] = grad_in
                outs[1][column] = grad_out
        grad = dot_tn(swish_ref[...], low_ref[...]).astype(BF)
        if fast:
            outs[0][:, 128:144, :] = grad.reshape(32, 16, 512)
        else:
            outs[2][...] = grad

    if fast:
        outs = [shaped((32, 144, 512), BF)]
    else:
        outs = [shaped((4, width, 512), BF), shaped((4, 512, width), BF), shaped((width, width), BF)]
    return run(kernel, [pre, act, dhid, branch, swish, low], outs, "middle_grads", time=3)


def ffn1_again(frames, x1, win, wout, small, home, near):
    rows, width = x1.shape

    def kernel(
        x_in, x1_in, win_in, wout_in, small_ref, home_ref, near_ref,
        pre_ref, act_ref, slope_ref, x1_ref, x_ref, win_ref, wout_ref, sum_ref, sems,
    ):
        pairs = ((x_in, x_ref), (win_in, win_ref), (x1_in, x1_ref), (wout_in, wout_ref))
        copies = [pltpu.make_async_copy(a, b, sems.at[k]) for k, (a, b) in enumerate(pairs)]
        for copy in copies:
            copy.start()
        copies[0].wait()
        normed, _ = norm(x_ref[...].astype(F32))
        pre = (normed * row(small_ref, GAIN) + row(small_ref, BIAS)).astype(BF)
        pre_ref[...] = pre
        sum_ref[...] = home_ref[...] + near_ref[0].astype(F32)
        copies[1].wait()
        for column in range(win.shape[0]):
            hidden = dot(pre, win_ref[column])
            gate = jax.nn.sigmoid(hidden)
            act_ref[column] = (hidden * gate).astype(BF)
            slope_ref[column] = gate * (1.0 + hidden * (1.0 - gate))
        copies[2].wait()
        copies[3].wait()

    wide = (win.shape[0], rows, 512)
    return run(
        kernel,
        [frames, x1, win, wout, small, home, near],
        [shaped((rows, width), BF), shaped(wide, BF), shaped(wide, F32), shaped(x1.shape, F32)]
        + [shaped(frames.shape, BF), shaped(win.shape, BF), shaped(wout.shape, BF), shaped(home.shape, F32)],
        "ffn1_again",
        time=0.01,
        specs=[pl.BlockSpec(memory_space=pltpu.HBM)] * 4 + [VMEM] * 3,
        scratch=[pltpu.SemaphoreType.DMA((4,))],
    )


def ffn1_backward(fast, again, upstream, far, small, conv_rows, mid_rows, grad_bias):
    pre, active, slope, x1, frames, win, wout, home = again
    rows, width = x1.shape

    def kernel(
        pre_ref, act_ref, slope_ref, x1_ref, x_ref, win_ref, wout_ref, home_ref, up_ref, far_ref, small_ref,
        conv_ref, mid_ref, bias_ref,
        *refs,
    ):
        frames_ref, outs, (chan_ref, gin_ref, gout_ref) = refs[0], refs[1:-3], refs[-3:]
        dn = home_ref[...] + far_ref[...].astype(F32)
        normed, scale = norm(x1_ref[...])
        grad, gain1, bias1 = norm_back(dn, normed, scale, row(small_ref, GAIN + 1))
        up = up_ref[...] + grad
        branch = (0.5 * up).astype(BF)
        normed, scale = norm(x_ref[...].astype(F32))
        gain0 = row(small_ref, GAIN)
        pre = pre_ref[...]
        total = jnp.zeros((rows, width), F32)
        for column in range(win_ref.shape[0]):
            gout_ref[512 * column : 512 * column + 512, :] = dot_tn(act_ref[column], branch).astype(BF)
            grad = dot_nt(branch, wout_ref[512 * column : 512 * column + 512, :])
            grad = (grad * slope_ref[column]).astype(BF)
            gin_ref[column] = dot_tn(pre, grad).astype(BF)
            total = total + dot_nt(grad, win_ref[column])
        grad, gain_grad, bias_grad = norm_back(total, normed, scale, gain0)
        frames_ref[...] = (up + grad).astype(BF)
        chan_ref[...] = jnp.zeros_like(chan_ref)
        taps = GAIN
        chan_ref[0:taps, :] = conv_ref[0:taps, :]
        for first, at in ((GAIN, 0), (BIAS, 1)):
            chan_ref[first + 2 : first + 3, :] = conv_ref[taps + at : taps + at + 1, :]
            for k in range(3):
                chan_ref[first + 3 + k : first + 4 + k, :] = mid_ref[2 * k + at : 2 * k + at + 1, :]
        chan_ref[POS_BIAS : POS_BIAS + 2, :] = bias_ref[...]
        chan_ref[GAIN : GAIN + 1, :] = gain_grad
        chan_ref[GAIN + 1 : GAIN + 2, :] = gain1
        chan_ref[BIAS : BIAS + 1, :] = bias_grad
        chan_ref[BIAS + 1 : BIAS + 2, :] = bias1
        if fast:
            a_far, a_own, b_far, b_own = outs
            turned = chan_ref[...].T.astype(BF)
            for kc, a_out, b_out in ((1, a_far, b_far), (0, a_own, b_own)):
                for one in range(2):
                    for two in range(2):
                        for i in range(4):
                            at = block_index(KZ[i], two, one, kc)
                            for column in range(4):
                                a_out[one, two, i, 16 * column : 16 * column + 16, :] = gin_ref[
                                    column, part(at, 16), :
                                ]
                            at = block_index(KZ[i], one, two, kc)
                            b_out[one, two, i] = gout_ref[part(at, 64), :]
            gin_ref[0, :, 0:128] = turned
            for kc, a_out in ((1, a_far), (0, a_own)):
                for one in range(2):
                    for two in range(2):
                        for i in range(4):
                            at = block_index(KZ[i], two, one, kc)
                            own = gin_ref[0, part(at, 16), 0:128].astype(F32)
                            own = jnp.concatenate([own[0:8], own[8:16], jnp.zeros((8, 256), F32)], axis=1)
                            a_out[one, two, i, 64:72, :] = own.astype(BF)
        else:
            outs[0][...] = gin_ref[...]
            outs[1][...] = gout_ref[...]
            outs[2][...] = chan_ref[...].T.astype(BF)

    if fast:
        outs = [shaped((2, 2, 4, 72, 512), BF)] * 2 + [shaped((2, 2, 4, 64, 512), BF)] * 2
    else:
        outs = [shaped((4, width, 512), BF), shaped((2048, width), BF), shaped((width, 128), BF)]
    return run(
        kernel,
        list(again) + [upstream, far, small, conv_rows, mid_rows, grad_bias],
        [shaped((rows, width), BF)] + outs,
        "ffn1_backward",
        time=0.01,
        scratch=[
            pltpu.VMEM((128, width), F32),
            pltpu.VMEM((4, width, 512), BF),
            pltpu.VMEM((2048, width), BF),
        ],
    )


def tables(head_index, own_length, rows, width):
    pairs = lax.axis_size("heads")
    freq = jnp.exp(
        jnp.arange(width // 2, dtype=jnp.int32).astype(F32) * (-2.0 * math.log(10000.0) / width)
    )
    steps = rows // 128
    others = jnp.arange(pairs, dtype=jnp.int32) ^ head_index
    coarse = (others[:, None] * steps + jnp.arange(steps, dtype=jnp.int32)[None, :]).reshape(-1)
    coarse_phase = (coarse * 128).astype(F32)[:, None] * freq[None, :]
    fine_phase = jnp.arange(128, dtype=jnp.int32).astype(F32)[:, None] * freq[None, :]
    phase = jnp.concatenate([coarse_phase, fine_phase])
    info = jnp.stack([head_index, own_length]).astype(jnp.int32)
    count = pairs * rows
    half = width // 2

    def kernel(info_ref, sin_ref, cos_ref, table_ref, turned_ref, own_ref, mask_ref):
        sin_b, cos_b = sin_ref[pairs * steps :, :], cos_ref[pairs * steps :, :]
        for a in range(pairs * steps):
            here = slice(128 * a, 128 * a + 128)
            sin_a, cos_a = sin_ref[a : a + 1, :], cos_ref[a : a + 1, :]
            sin = sin_a * cos_b + cos_a * sin_b
            cos = cos_a * cos_b - sin_a * sin_b
            table_ref[here, :half] = sin.astype(BF)
            table_ref[here, half:] = cos.astype(BF)
            turned_ref[:half, here] = sin.T.astype(BF)
            turned_ref[half:, here] = cos.T.astype(BF)
            if a < steps:
                own_ref[0, here, :] = cos
                own_ref[1, here, :] = sin
            at = lax.broadcasted_iota(jnp.int32, (1, 128), 1)
            at = at + ((info_ref[0] ^ (a // steps)) * rows + 128 * (a % steps))
            mask_ref[0:1, here] = jnp.where(at < info_ref[1], 0.0, -1e30)

    return run(
        kernel,
        [info, jnp.sin(phase), jnp.cos(phase)],
        [shaped((count, width), BF), shaped((width, count), BF), shaped((2, rows, half), F32), shaped((1, count), F32)],
        "tables",
        specs=[SMEM, VMEM, VMEM],
    )


def prepare(ffn1_out, dw_kernel, norm_gain, norm_bias, pos_bias, att_proj, att_out, ffn2_in, ffn2_out, conv_in, conv_out):
    head_dim = att_out.shape[1]

    dw_kernel = dw_kernel.T

    def kernel(
        out1_ref, dw_ref, gain_ref, bias_ref, posb_ref, proj_ref, att_ref, in2_ref, out2_ref, cin_ref, cout_ref,
        b_ref, t_ref, pack_ref, square_ref, pos_ref,
    ):
        b_ref[0:64, :] = out1_ref[...]
        square_ref[...] = jnp.zeros_like(square_ref)
        square_ref[GAIN:BIAS, 0:16] = gain_ref[...].astype(F32)
        square_ref[BIAS:POS_BIAS, 0:16] = bias_ref[...].astype(F32)
        square_ref[POS_BIAS : POS_BIAS + 2, 0:16] = posb_ref[...].astype(F32)
        square_ref[...] = square_ref[...].T
        square_ref[0:16, 0:GAIN] = dw_ref[...].astype(F32)
        turned = square_ref[0:16, :]
        b_ref[64:72, :] = jnp.concatenate([turned[0:8], turned[8:16], jnp.zeros((8, 256), F32)], axis=1).astype(BF)
        both = [proj_ref[h].astype(F32) for h in range(2)]
        for k in range(3):
            columns = slice(k * head_dim, k * head_dim + head_dim)
            t_ref[:, 128 * k : 128 * k + 128] = jnp.concatenate([p[:, columns] for p in both], axis=1).astype(BF)
        square_ref[...] = jnp.zeros_like(square_ref)
        square_ref[0:64, 0:64] = att_ref[0].astype(F32)
        square_ref[64:128, 0:64] = att_ref[1].astype(F32)
        t_ref[:, 384:512] = square_ref[...].T[0:64].astype(BF)
        pos_ref[...] = jnp.concatenate([p[:, 3 * head_dim :] for p in both], axis=1)
        for k in range(2):
            t_ref[32 * k : 32 * k + 32, 512:640] = pos_ref[pl.ds(k, 32, stride=2), :].astype(BF)
        for k in range(4):
            pack_ref[16 * k : 16 * k + 16, :] = in2_ref[:, 512 * k : 512 * k + 512]
        pack_ref[64:128, :] = out2_ref[...]
        for k in range(2):
            pack_ref[128 + 16 * k : 144 + 16 * k, :] = cin_ref[:, 512 * k : 512 * k + 512]
        pack_ref[160:176, :] = cout_ref[...]

    return run(
        kernel,
        [ffn1_out, dw_kernel, norm_gain, norm_bias, pos_bias, att_proj, att_out, ffn2_in, ffn2_out, conv_in, conv_out],
        [shaped((72, 512), BF), shaped((64, 640), BF), shaped((176, 512), BF)],
        "prepare",
        specs=[whole(a) for a in (ffn1_out, dw_kernel, norm_gain, norm_bias, pos_bias, att_proj, att_out)]
        + [whole(a) for a in (ffn2_in, ffn2_out, conv_in, conv_out)],
        grid=(1,),
        scratch=[pltpu.VMEM((128, 128), F32), pltpu.VMEM((64, 128), F32)],
        limit=60,
    )


def own_terms(terms):
    def spec(array):
        lead = len(array.shape) - 2
        return pl.BlockSpec((1,) * lead + array.shape[lead:], lambda *_: (0,) * (lead + 2))

    return list(terms), [spec(t) for t in terms]


def add_terms(refs):
    rows, columns = refs[0].shape[-2:]
    total = refs[0][...].reshape(rows, columns).astype(F32)
    for ref in refs[1:]:
        total = total + ref[...].reshape(rows, columns).astype(F32)
    return total


def finish_first(terms_a, terms_b):
    inputs, specs = own_terms(terms_a + terms_b)

    def kernel(*refs):
        in_ref, out_ref, dw_ref, gain_ref, bias_ref, posb_ref, square_ref = refs[12:]
        total = add_terms(refs[:6])
        for k in range(4):
            in_ref[:, 512 * k : 512 * k + 512] = total[16 * k : 16 * k + 16, :]
        square_ref[...] = jnp.zeros_like(square_ref)
        square_ref[0:8, :] = total[64:72, 0:128]
        square_ref[8:16, :] = total[64:72, 128:256]
        turned = square_ref[...].T
        dw_ref[...] = square_ref[0:16, 0:GAIN]
        gain_ref[...] = turned[GAIN:BIAS, 0:16]
        bias_ref[...] = turned[BIAS:POS_BIAS, 0:16]
        posb_ref[...] = turned[POS_BIAS : POS_BIAS + 2, 0:16]
        out_ref[...] = add_terms(refs[6:12])

    outs = [(16, 2048), (64, 512), (16, 32), (6, 16), (6, 16), (2, 16)]
    rows_in, rows_out, taps, *rest = run(
        kernel,
        inputs,
        [shaped(o, F32) for o in outs],
        "finish_first",
        specs=specs,
        grid=(1,),
        scratch=[pltpu.VMEM((128, 128), F32)],
    )
    return rows_in, rows_out, taps.T, *rest


def finish_attention(terms):
    inputs, specs = own_terms(terms)

    def kernel(*refs):
        proj_ref, out_ref, cin_ref, square_ref, pos_ref = refs[len(inputs) :]
        total = add_terms(refs[: len(inputs)])
        square_ref[...] = jnp.zeros_like(square_ref)
        square_ref[0:64, :] = total[:, 384:512]
        turned = square_ref[...].T
        for k in range(2):
            pos_ref[pl.ds(k, 32, stride=2), :] = total[32 * k : 32 * k + 32, 512:640]
        for h in range(2):
            for k in range(3):
                at = 128 * k + 64 * h
                proj_ref[h, :, 64 * k : 64 * k + 64] = total[:, at : at + 64]
            proj_ref[h, :, 192:256] = pos_ref[:, 64 * h : 64 * h + 64]
            out_ref[h] = turned[64 * h : 64 * h + 64, 0:64]
        for k in range(4):
            cin_ref[:, 256 * k : 256 * k + 256] = total[16 * k : 16 * k + 16, 640:896]

    return run(
        kernel,
        inputs,
        [shaped((2, 64, 256), F32), shaped((2, 64, 64), F32), shaped((16, 1024), F32)],
        "finish_attention",
        specs=specs,
        grid=(1,),
        scratch=[pltpu.VMEM((128, 128), F32), pltpu.VMEM((64, 128), F32)],
    )


def finish_middle(sums):
    def kernel(sum_ref, in_ref, out_ref, conv_ref):
        for k in range(4):
            in_ref[:, 512 * k : 512 * k + 512] = sum_ref[16 * k : 16 * k + 16, :].astype(F32)
        out_ref[...] = sum_ref[64:128, :].astype(F32)
        conv_ref[...] = sum_ref[128:144, :].astype(F32)

    return run(
        kernel,
        [sums],
        [shaped((16, 2048), F32), shaped((64, 512), F32), shaped((16, 512), F32)],
        "finish_middle",
    )


def small_shard(dw_kernel, norm_gain, norm_bias, pos_bias):
    stacked = jnp.concatenate([dw_kernel, norm_gain, norm_bias, pos_bias], axis=0)
    return jnp.pad(stacked.T, ((0, 0), (0, 128 - stacked.shape[0])))


def att_shard(att_proj, att_out):
    two, rows, four = att_proj.shape
    head_dim = four // 4
    parts = att_proj.reshape(two, rows, 4, head_dim).transpose(1, 2, 0, 3)
    parts = parts.reshape(rows, 4, two * head_dim)
    out_t = att_out.transpose(2, 0, 1).reshape(rows, two * head_dim)
    turned = parts[:, 3].reshape(rows // 2, 2, two * head_dim).transpose(1, 0, 2)
    turned = turned.reshape(rows, two * head_dim)
    return jnp.concatenate([parts[:, 0], parts[:, 1], parts[:, 2], out_t, turned], axis=1)


def column_chunks(array):
    rows, columns = array.shape
    return array.reshape(rows, columns // 512, 512).transpose(1, 0, 2)


def xor_order(array, index):
    bit = 1
    while bit < array.shape[0]:
        flipped = jnp.stack([array[i ^ bit] for i in range(array.shape[0])])
        array = jnp.where((index & bit) != 0, flipped, array)
        bit *= 2
    return array


def rows_of(shard):
    return lax.all_gather(shard, BOTH, axis=0, tiled=True)


def sum_rows(grad):
    return lax.psum_scatter(grad.astype(F32), BOTH, scatter_dimension=0, tiled=True)


def local(
    frames_in,
    cotangent,
    lengths,
    sample_weight,
    ffn1_in,
    ffn1_out,
    att_proj,
    att_out,
    pos_bias,
    conv_in,
    dw_kernel,
    conv_out,
    ffn2_in,
    ffn2_out,
    norm_gain,
    norm_bias,
):
    row_count, model_width = frames_in.shape
    pairs = lax.axis_size("heads")
    batches = lax.axis_size("batch")
    head_index = lax.axis_index("heads")
    batch_index = lax.axis_index("batch")
    channels = ffn1_in.shape[0]
    fast = channels == 16 and batches == 8 and pairs == 4
    kernel_len = dw_kernel.shape[0]
    head_dim = att_out.shape[1]
    width = model_width // batches

    utter_ids = jnp.arange(lengths.shape[0], dtype=jnp.int32)
    own_length = jnp.sum(jnp.where(utter_ids == batch_index, lengths, 0))
    own_weight = jnp.sum(jnp.where(utter_ids == batch_index, sample_weight, 0)).astype(F32) * 0.25
    total_valid = jnp.sum(lengths).astype(F32)
    ints = jnp.stack([own_length, head_index * row_count]).astype(jnp.int32)
    floats = jnp.stack([own_weight, total_valid])

    if fast:
        shard_b, shard_t, pack = prepare(
            ffn1_out, dw_kernel, norm_gain, norm_bias, pos_bias, att_proj, att_out, ffn2_in, ffn2_out, conv_in, conv_out
        )
        held_a, held_b = gather_depth(ffn1_in), gather_depth(shard_b)
        held_t = jnp.stack([shard_t, swap(shard_t, "heads", 2)])
        held_a, held_b, held_t = lax.optimization_barrier((held_a, held_b, held_t))
        side_a, side_b, deep_t = swap(held_a, "batch", 1), swap(held_b, "heads", 2), swap(held_t, "batch", 4)
        side_a, side_b, deep_t = lax.optimization_barrier((side_a, side_b, deep_t))
        held_a, held_b, held_t = (jnp.concatenate(p) for p in ((held_a, side_a), (held_b, side_b), (held_t, deep_t)))
        side_a, side_b, deep_t = swap(held_a, "heads", 2), swap(held_b, "batch", 1), swap(held_t, "batch", 2)
        table, table_t, own_turn, key_mask = tables(behind(head_index, held_a, held_b), own_length, row_count, model_width)
        table, table_t, own_turn, key_mask, ints, floats, side_a, side_b, deep_t = lax.optimization_barrier(
            (table, table_t, own_turn, key_mask, ints, floats, side_a, side_b, deep_t)
        )
        held_t = jnp.concatenate([held_t, deep_t])
        side_t = swap(held_t, "batch", 1)
        pack = lax.all_gather(behind(pack, held_a, held_b), BOTH, axis=0)
        win, wout, small_t, pos_b = place_first(
            (held_a, side_a, swap(held_a, "heads", 1), swap(side_a, "heads", 1)),
            (held_b, side_b, swap(held_b, "heads", 1), swap(side_b, "heads", 1)),
        )
        x1, n1 = ffn1_forward(frames_in, win, wout, small_t)
        held_t, side_t = behind(held_t, n1), behind(side_t, n1)
        sides_t = held_t, side_t
        tw, pos_w = place_attention(sides_t + tuple(swap(t, "heads", 1) for t in sides_t))
        conv_in_w = middle_w = [pack]
    else:
        table, table_t, own_turn, key_mask = tables(head_index, own_length, row_count, model_width)
        small = small_shard(dw_kernel, norm_gain, norm_bias, pos_bias)
        att_part = att_shard(att_proj, att_out)
        win, wout = column_chunks(rows_of(ffn1_in)), rows_of(ffn1_out)
        small_t = rows_of(small).T.astype(F32)
        pos_b = small_t[POS_BIAS : POS_BIAS + 2].reshape(2, batches, pairs, channels).transpose(2, 0, 1, 3)
        pos_b = pos_b.reshape(pairs, 2, 2, head_dim).transpose(0, 2, 1, 3).reshape(pairs, 2, 2 * head_dim)
        pos_b = xor_order(pos_b, head_index)
        att_all = lax.all_gather(lax.all_gather(att_part, "batch", axis=0), "heads", axis=0)
        att_all = xor_order(att_all, head_index)
        tw = att_all[..., :512].reshape(pairs, model_width, 512)
        pos_w = att_all[..., 512:].reshape(pairs, batches, 2, width // 2, 128).transpose(0, 2, 1, 3, 4)
        pos_w = pos_w.reshape(pairs, model_width, 128)
        halves_in = column_chunks(rows_of(conv_in))
        conv_in_w = [halves_in[0], halves_in[1]]
        middle_w = [
            column_chunks(rows_of(ffn2_in)),
            rows_of(ffn2_out).reshape(4, 512, model_width),
            rows_of(conv_out),
        ]

    if not fast:
        x1, n1 = ffn1_forward(frames_in, win, wout, small_t)
    across = swap(n1, "heads", 2)
    keys = [n1, swap(n1, "heads", 1), across, swap(across, "heads", 1)]
    weights, mixed, scale, kv, queries, after_att, n2 = att_forward(
        key_mask, keys, x1, small_t, tw, pos_w, pos_b, own_turn, table_t
    )
    glu, gated, conv_in_w = gate_forward(ints, n2, conv_in_w)
    rim = halo(glu)
    depth, sums = conv_forward(ints, glu, rim, small_t)
    sums = sum_over(sum_over(sums, "heads"), "batch")
    layer_out, upstream, raw, gsum, mid_rows, pre, act, dhid, branch, swish, low = middle(
        ints, floats, depth, sums, after_att, cotangent, small_t, middle_w
    )

    gsum = sum_over(gsum, "heads")
    pre = behind(pre, gsum)
    gsum = sum_over(gsum, "batch")
    mid_grads = middle_grads(fast, pre, act, dhid, branch, swish, low)
    positions = head_index * row_count + jnp.arange(row_count, dtype=jnp.int32)
    row_valid = (positions < own_length).astype(F32)[:, None]
    mean_bn = sums[0] / total_valid
    grad_first = (gsum[0] - 2.0 * mean_bn * gsum[1]) / total_valid
    grad_second = gsum[1] / total_valid
    raw = behind(raw, *mid_grads)
    depth_low = (raw + row_valid * (grad_first + 2.0 * depth * grad_second)).astype(BF)
    depth_rim = halo(depth_low)
    if fast:
        mid = lax.psum_scatter(mid_grads[0].reshape(32 * 144, 512), BOTH, scatter_dimension=0, tiled=True)
    upstream, dgated, conv_rows = conv_backward(
        ints, glu, rim, depth_low, depth_rim, small_t, gated, conv_in_w, after_att, upstream
    )
    near, far, home, grad_bias, *att_grads = att_backward(
        fast, upstream, n2, dgated, keys, mixed, scale, weights, kv, queries, tw, pos_w, own_turn, table
    )
    near = swap(near, "heads", 1)
    moving = (far.astype(F32) + near[1].astype(F32)).astype(BF)
    far = swap(moving, "heads", 2)
    grad_bias = xor_order(grad_bias, head_index).reshape(pairs, 2, 2, head_dim).transpose(0, 2, 1, 3)
    grad_bias = grad_bias.reshape(pairs, 2, batches, channels).transpose(1, 2, 0, 3).reshape(2, model_width)
    if fast:
        heard = swap(behind(att_grads[1], near), "heads", 1)
        home = behind(home, heard)
        t = Exchange(att_grads[0], behind(heard, moving), steps_attention())
        send_all([t], keep=True)
    again = ffn1_again(frames_in, x1, win, wout, small_t, home, near)
    frames_grad, *first_grads = ffn1_backward(
        fast, again, upstream, far, small_t, conv_rows, mid_rows, grad_bias
    )

    if fast:
        *first_grads, t.terms[-1] = lax.optimization_barrier((*first_grads, t.terms[-1]))
        own_ffn2_a, own_ffn2_b, own_conv_b = finish_middle(mid)
        a_far, a_own, b_far, b_own = first_grads
        a = Exchange(a_own, swap(a_far, "heads", 1), steps_first("xy"))
        b = Exchange(b_own, swap(b_far, "heads", 1), steps_first("yx"))
        t.terms[-1] = behind(t.terms[-1], mid)
        send_all((a, b, t))
        send_all((a, b, t))
        moving = send_all((a, b))
        t.terms[-1] = behind(t.terms[-1], *moving)
        send_all([t])
        send_all((a, b))
        own_proj, own_out, own_conv_a = finish_attention(t.terms)
        own_ffn1_a, own_ffn1_b, own_taps, own_gain, own_bias, own_pos = finish_first(a.terms, b.terms)
    else:

        def to_rows(chunks):
            rows = chunks.shape[1]
            return sum_rows(chunks.transpose(1, 0, 2).reshape(rows, -1))

        own_ffn2_a = to_rows(mid_grads[0])
        own_ffn2_b = sum_rows(mid_grads[1].reshape(-1, model_width))
        own_conv_b = sum_rows(mid_grads[2])
        tw_grad, pos_grad, conv_grad = att_grads
        own_conv_a = sum_rows(conv_grad)
        pos_grad = pos_grad.reshape(pairs, 2, batches, width // 2, 128).transpose(0, 2, 1, 3, 4)
        grad_att = jnp.concatenate([tw_grad, pos_grad.reshape(pairs, model_width, 128)], axis=2)
        grad_att = xor_order(grad_att, head_index).astype(F32)
        own_att = lax.psum_scatter(
            lax.psum_scatter(grad_att, "batch", scatter_dimension=1, tiled=True),
            "heads",
            scatter_dimension=0,
            tiled=True,
        )[0]
        own_ffn1_a, own_ffn1_b = to_rows(first_grads[0]), sum_rows(first_grads[1])
        own_small = sum_rows(first_grads[2])
        own_small = own_small.T
        turned = own_att[:, 512:640].reshape(2, width // 2, 128).transpose(1, 0, 2).reshape(width, 128)
        parts = jnp.stack([own_att[:, :128], own_att[:, 128:256], own_att[:, 256:384], turned], axis=1)
        own_proj = parts.reshape(width, 4, 2, head_dim).transpose(2, 0, 1, 3)
        own_proj = own_proj.reshape(2, width, 4 * head_dim)
        own_out = own_att[:, 384:512].T.reshape(2, head_dim, width)
        own_pos = own_small[POS_BIAS : POS_BIAS + 2]
        own_taps = own_small[:kernel_len]
        own_gain, own_bias = own_small[GAIN : GAIN + 6], own_small[BIAS : BIAS + 6]
    return (
        layer_out,
        frames_grad,
        own_ffn1_a,
        own_ffn1_b,
        own_proj,
        own_out,
        own_pos,
        own_conv_a,
        own_taps,
        own_conv_b,
        own_ffn2_a,
        own_ffn2_b,
        own_gain,
        own_bias,
    )


def solution(mesh):
    placed = (
        P(("batch", "heads"), None),
        P(("batch", "heads"), None),
        P(),
        P(),
        P(("batch", "heads"), None),
        P(("batch", "heads"), None),
        P("heads", "batch", None),
        P("heads", None, "batch"),
        P("heads", "batch"),
        P(("batch", "heads"), None),
        P(None, ("batch", "heads")),
        P(("batch", "heads"), None),
        P(("batch", "heads"), None),
        P(("batch", "heads"), None),
        P(None, ("batch", "heads")),
        P(None, ("batch", "heads")),
    )
    return jax.shard_map(
        local,
        mesh=mesh,
        in_specs=placed,
        out_specs=(
            P(("batch", "heads"), None),
            P(("batch", "heads"), None),
            P(("batch", "heads"), None),
            P(("batch", "heads"), None),
            P("heads", "batch", None),
            P("heads", None, "batch"),
            P("heads", "batch"),
            P(("batch", "heads"), None),
            P(None, ("batch", "heads")),
            P(("batch", "heads"), None),
            P(("batch", "heads"), None),
            P(("batch", "heads"), None),
            P(None, ("batch", "heads")),
            P(None, ("batch", "heads")),
        ),
        check_vma=False,
    )
```

```python
import math

import jax
import jax.numpy as jnp
from jax import lax
from jax.experimental import pallas as pl
from jax.experimental.pallas import tpu as pltpu
from jax.sharding import PartitionSpec as P

epsilon = 1e-05
BF = jnp.bfloat16
F32 = jnp.float32
BOTH = ("batch", "heads")
CHUNK = 256
HALO = 16
SCALE = 0.125
LOG2E = 1.4426950408889634
GAIN, BIAS, POS_BIAS = 32, 38, 44
KZ = (0, 2, 1, 3)
DIMS = {"y": ("batch", 1), "x": ("heads", 2)}
VMEM_BYTES = 40 * 2**20


def swap(source, axis, mask):
    count = lax.axis_size(axis)
    return lax.ppermute(source, axis, [(i, i ^ mask) for i in range(count)])


def sum_over(source, axis):
    mask = 1
    while mask < lax.axis_size(axis):
        source = source + swap(source, axis, mask)
        mask *= 2
    return source


def halo(cells):
    ends = lax.axis_size("heads") - 1
    rows = cells.shape[0]
    before = lax.ppermute(cells[rows - HALO :], "heads", [(i, i + 1) for i in range(ends)])
    after = lax.ppermute(cells[:HALO], "heads", [(i + 1, i) for i in range(ends)])
    return before, after


def behind(source, *others):
    return lax.optimization_barrier((source,) + others)[0]


def gather_depth(shard):
    held = shard[None]
    for mask in (4, 2):
        held = jnp.concatenate([held, swap(held, "batch", mask)])
    return held


class Exchange:
    def __init__(self, own, heard, steps):
        self.terms, self.steps = [own, heard], list(steps)

def send_all(group, keep=False):
    inputs, specs, outs, sizes = [], [], [], []
    stays = [[(0,) * len(one.terms)] for one in group] if keep else [[]] * len(group)
    pairs = [(one, parts) for one, stay in zip(group, stays) for parts in [one.steps[0][0]] + [[(k,) for k in s] for s in stay]]
    for one, parts in pairs:
        for term, index in zip(one.terms, parts, strict=True):
            index = index + (slice(None),) * (term.ndim - len(index))
            ends = [(k, 1) if isinstance(k, int) else (k.start // 2, 2) if k.start else (0, n) for k, n in zip(index, term.shape)]
            specs.append(pl.BlockSpec(tuple(e[1] for e in ends), lambda *_, at=tuple(e[0] for e in ends): at))
            inputs.append(term)
        shape = [2 if k.start else n for k, n in zip(index, term.shape) if not isinstance(k, int)]
        outs.append(shaped(tuple(shape), BF))
        sizes.append(len(parts))

    def kernel(*refs):
        at = 0
        for size, out_ref in zip(sizes, refs[-len(outs) :], strict=True):
            value = refs[at][...].reshape(out_ref.shape).astype(F32)
            for ref in refs[at + 1 : at + size]:
                value = value + ref[...].reshape(out_ref.shape).astype(F32)
            out_ref[...] = value.astype(BF)
            at += size

    moving = run(kernel, inputs, outs, "send_all", specs=specs, grid=(1,), limit=24)
    if keep:
        for one, array in zip(group, moving[1::2], strict=True):
            one.terms = [array]
        moving = moving[0::2]
    for one, array in zip(group, moving, strict=True):
        _, axis, mask = one.steps.pop(0)
        one.terms.append(swap(array, axis, mask))
    return moving


def steps_first(order):
    one, two = DIMS[order[0]], DIMS[order[1]]
    return [
        ([(1,), (1,)],) + one,
        ([(0, 1), (0, 1), (1,)],) + two,
        ([(0, 0, slice(2, 4)), (0, 0, slice(2, 4)), (0, slice(2, 4)), (slice(2, 4),)],) + ("batch", 2),
        ([(0, 0, 1), (0, 0, 1), (0, 1), (1,), (1,)],) + ("batch", 4),
    ]


def steps_attention():
    high = slice(2, 4)
    return [
        ([(1,), (1,)], "batch", 1),
        ([(high,), (high,)], "batch", 2),
        ([(1,), (1,), (1,)], "batch", 4),
        ([(0, 1), (0, 1), (0, 1), (1,)], "heads", 2),
    ]


def dot(left, right):
    return jnp.dot(left, right, preferred_element_type=F32)


def dot_nt(left, right):
    return lax.dot_general(left, right, (((1,), (1,)), ((), ())), preferred_element_type=F32)


def dot_tn(left, right):
    return lax.dot_general(left, right, (((0,), (0,)), ((), ())), preferred_element_type=F32)


def norm(source):
    center = source - jnp.mean(source, axis=-1, keepdims=True)
    scale = lax.rsqrt(jnp.mean(center * center, axis=-1, keepdims=True) + epsilon)
    return center * scale, scale


def norm_back(upstream, normed, scale, gain_row):
    inner = upstream * gain_row
    mean = jnp.mean(inner, axis=-1, keepdims=True)
    along = jnp.mean(inner * normed, axis=-1, keepdims=True)
    gain_grad = jnp.sum(upstream * normed, axis=0, keepdims=True)
    return scale * (inner - mean - normed * along), gain_grad, jnp.sum(upstream, axis=0, keepdims=True)


def row(small_ref, index):
    return small_ref[index : index + 1, :]


def place():
    batch_at = lax.axis_index("batch")
    heads_at = lax.axis_index("heads")
    return batch_at // 2, batch_at % 2, heads_at // 2, heads_at % 2


def block_index(kz, ky, kx, kc):
    z, y, x, c = place()
    return ((z ^ kz) * 2 + (y ^ ky)) * 4 + (x ^ kx) * 2 + (c ^ kc)


def part(index, size):
    return pl.ds(pl.multiple_of(index * size, size), size)


def valid_rows(ints_ref, rows):
    steps = lax.broadcasted_iota(jnp.int32, (rows, 1), 0) + ints_ref[1]
    return (steps < ints_ref[0]).astype(F32)


def whole(array):
    return pl.BlockSpec(array.shape, lambda *_: (0,) * len(array.shape), pipeline_mode=pl.Buffered(1))


def per_pair(array):
    return pl.BlockSpec((1,) + array.shape[1:], lambda h: (h,) + (0,) * (len(array.shape) - 1))


def shaped(shape, kind):
    return jax.ShapeDtypeStruct(shape, kind)


SMEM = pl.BlockSpec(memory_space=pltpu.SMEM)


VMEM = pl.BlockSpec(memory_space=pltpu.VMEM)


def cost(time):
    return pl.CostEstimate(flops=int(time * 10**9), bytes_accessed=2**12, transcendentals=0)


def run(kernel, inputs, outs, name, specs=None, grid=(), scratch=(), limit=24, time=0.01):
    return pl.pallas_call(
        kernel,
        grid=grid,
        in_specs=specs or [VMEM] * len(inputs),
        out_specs=[whole(o) for o in outs] if grid else [VMEM] * len(outs),
        out_shape=outs,
        scratch_shapes=list(scratch),
        compiler_params=pltpu.CompilerParams(vmem_limit_bytes=limit * 2**20),
        cost_estimate=cost(time),
        name=name,
    )(*inputs)


def fetch(*arrays):
    def kernel(*refs):
        count = len(arrays)
        copies = [pltpu.make_async_copy(refs[i], refs[count + i], refs[-1].at[i]) for i in range(count)]
        for copy in copies:
            copy.start()
        for copy in copies:
            copy.wait()

    return run(
        kernel,
        list(arrays),
        [shaped(a.shape, a.dtype) for a in arrays],
        "fetch",
        specs=[pl.BlockSpec(memory_space=pltpu.HBM)] * len(arrays),
        scratch=[pltpu.SemaphoreType.DMA((len(arrays),))],
    )


def place_first(sets_a, sets_b):
    def kernel(*refs):
        a_refs, b_refs = refs[:4], refs[4:8]
        win_ref, wout_ref, small_ref, pb_ref, chan_ref, stage_ref = refs[8:]
        for k in range(4):
            for i in range(8):
                at = block_index(KZ[i % 4], i // 4, k & 1, k >> 1)
                for column in range(4):
                    win_ref[column, part(at, 16), :] = a_refs[k][i, :, 512 * column : 512 * column + 512]
                at = block_index(KZ[i % 4], k & 1, i // 4, k >> 1)
                wout_ref[part(at, 64), :] = b_refs[k][i, 0:64, :]
                small = b_refs[k][i, 64:72, 0:256].astype(F32)
                chan_ref[part(at, 16), :] = jnp.concatenate([small[:, 0:128], small[:, 128:256]], axis=0)
        small_ref[...] = chan_ref[...].T
        for mask in range(4):
            pair = lax.axis_index("heads") ^ mask
            for b in range(8):
                stage_ref[16 * b : 16 * b + 16, :] = chan_ref[part(4 * b + pair, 16), :]
            one, two = (stage_ref[...].T[at : at + 1] for at in (POS_BIAS, POS_BIAS + 1))
            pb_ref[mask, 0:1, :] = jnp.concatenate([one[:, :64], two[:, :64]], axis=1)
            pb_ref[mask, 1:2, :] = jnp.concatenate([one[:, 64:], two[:, 64:]], axis=1)

    return run(
        kernel,
        list(sets_a) + list(sets_b),
        [shaped((4, 512, 512), BF), shaped((2048, 512), BF), shaped((128, 512), F32), shaped((4, 2, 128), F32)],
        "place_first",
        scratch=[pltpu.VMEM((512, 128), F32), pltpu.VMEM((128, 128), F32)],
    )


def place_attention(sets):
    def kernel(*refs):
        tw_ref, pos_ref = refs[4:]
        z, y, _, _ = place()
        for k in range(4):
            for i in range(8):
                pair = (i % 2) * 2 + (k >> 1)
                at = (z ^ KZ[i // 2]) * 2 + (y ^ (k & 1))
                tw_ref[pair, part(at, 64), :] = refs[k][i, :, 0:512]
                pos_ref[pair, part(at, 32), :] = refs[k][i, 0:32, 512:640]
                pos_ref[pair, part(at + 8, 32), :] = refs[k][i, 32:64, 512:640]

    return run(
        kernel, list(sets), [shaped((4, 512, 512), BF), shaped((4, 512, 128), BF)], "place_attention"
    )


def ffn1_forward(frames, win, wout, small):
    def kernel(x_ref, win_ref, wout_ref, small_ref, out_ref, normed_ref):
        source = x_ref[...].astype(F32)
        normed, _ = norm(source)
        pre = (normed * row(small_ref, GAIN) + row(small_ref, BIAS)).astype(BF)
        total = jnp.zeros_like(source)
        for column in range(win_ref.shape[0]):
            hidden = dot(pre, win_ref[column])
            active = (hidden * jax.nn.sigmoid(hidden)).astype(BF)
            total = total + dot(active, wout_ref[512 * column : 512 * column + 512, :])
        source = source + 0.5 * total
        out_ref[...] = source
        normed, _ = norm(source)
        normed_ref[...] = (normed * row(small_ref, GAIN + 1) + row(small_ref, BIAS + 1)).astype(BF)

    return run(
        kernel,
        [frames, win, wout, small],
        [shaped(frames.shape, F32), shaped(frames.shape, BF)],
        "ffn1_forward",
        time=3,
    )


def halves(first, value):
    zero = jnp.zeros_like(value)
    return jnp.where(first, value, zero), jnp.where(first, zero, value)


def att_forward_kernel(
    mask_ref, own_ref, k1_ref, k2_ref, k3_ref, x1_ref, small_ref, tw_ref, pos_ref, pb_ref, cs_ref, et_ref,
    w_ref, o_ref, scale_ref, kv_ref, q_ref, att_ref, n2_ref, right_ref, value_ref, total_ref,
):
    rows, width = own_ref.shape
    half = cs_ref.shape[2]
    step = pl.program_id(0)
    tw = tw_ref[0]

    @pl.when(step == 0)
    def _():
        right_ref[0:width, :] = et_ref[...]
        value_ref[:, 128:256] = jnp.ones((value_ref.shape[0], 128), BF)
        total_ref[...] = x1_ref[...]

    for k, ref in enumerate((own_ref, k1_ref, k2_ref, k3_ref)):
        here = slice(k * rows, k * rows + rows)
        kv = dot(ref[...], tw[:, 128:384])
        kv_ref[0, here, :] = kv.astype(BF)
        right_ref[width : width + 128, here] = kv[:, :128].T.astype(BF)
    value_ref[:, 0:128] = kv_ref[0, :, 128:]
    query = dot(own_ref[...], tw[:, :128])
    qc = (query + pb_ref[0, 0:1, :]).astype(BF)
    qp = (query + pb_ref[0, 1:2, :]).astype(BF)
    q_ref[0, 0] = qc
    q_ref[0, 1] = qp
    first = lax.broadcasted_iota(jnp.int32, (rows, 128), 1) < 64
    cos, sin = cs_ref[0], cs_ref[1]
    mask = mask_ref[...]
    outs = []
    for qc_h, qp_h in zip(halves(first, qc), halves(first, qp)):
        turned = dot_nt(qp_h, pos_ref[0]) * (SCALE * LOG2E)
        us, uc = turned[:, :half], turned[:, half:]
        left = jnp.concatenate(
            [
                (us * cos + uc * sin).astype(BF),
                (uc * cos - us * sin).astype(BF),
                (qc_h.astype(F32) * (SCALE * LOG2E)).astype(BF),
            ],
            axis=1,
        )
        parts = []
        for r in range(0, rows, CHUNK):
            scores = dot(left[r : r + CHUNK], right_ref[...]) + mask
            top = jnp.max(scores, axis=1, keepdims=True)
            weights = jnp.exp2(scores - top).astype(BF)
            w_ref[0, len(outs), r : r + CHUNK, :] = weights
            parts.append(dot(weights, value_ref[...]))
        outs.append(jnp.concatenate(parts, axis=0))
    scale = 1.0 / jnp.where(first, outs[0][:, 128:], outs[1][:, 128:])
    scale_ref[0] = scale
    mixed = jnp.where(first, outs[0][:, :128], outs[1][:, :128]) * scale
    o_ref[0] = mixed
    total_ref[...] += dot_nt(mixed.astype(BF), tw[:, 384:512])

    @pl.when(step == pl.num_programs(0) - 1)
    def _():
        after = total_ref[...]
        att_ref[...] = after
        normed, _ = norm(after)
        n2_ref[...] = (normed * row(small_ref, GAIN + 2) + row(small_ref, BIAS + 2)).astype(BF)


def att_forward(mask, keys, x1, small, tw, pos, pb, cs, et):
    rows, width = x1.shape
    count = mask.shape[1]
    paired = [
        shaped((4, 2, rows, count), BF),
        shaped((4, rows, 128), F32),
        shaped((4, rows, 128), F32),
        shaped((4, count, 256), BF),
        shaped((4, 2, rows, 128), BF),
    ]
    shared = [shaped((rows, width), F32), shaped((rows, width), BF)]
    return pl.pallas_call(
        att_forward_kernel,
        grid=(4,),
        in_specs=[whole(mask)]
        + [whole(k) for k in keys]
        + [whole(x1), whole(small), per_pair(tw), per_pair(pos), per_pair(pb), whole(cs), whole(et)],
        out_specs=[per_pair(a) for a in paired] + [whole(a) for a in shared],
        out_shape=paired + shared,
        scratch_shapes=[
            pltpu.VMEM((width + 128, count), BF),
            pltpu.VMEM((count, 256), BF),
            pltpu.VMEM((rows, width), F32),
        ],
        compiler_params=pltpu.CompilerParams(vmem_limit_bytes=53 * 2**20),
        cost_estimate=cost(40),
        name="att_forward",
    )(mask, *keys, x1, small, tw, pos, pb, cs, et)


def att_backward_kernel(fast, *refs):
    (up_ref, n2_ref, dg_ref, own_ref, k1_ref, k2_ref, k3_ref, o_ref, scale_ref, w_ref, kv_ref, q_ref, tw_ref, pos_ref, cs_ref,
     e_ref, near_ref, far_ref, home_ref, db_ref) = refs[:20]
    outs, (dr_ref, dn_ref, dq_ref, og_ref, dconv_ref, tw_grad_ref, pos_grad_ref) = refs[20:-7], refs[-7:]
    rows, width = up_ref.shape
    half = cs_ref.shape[2]
    count = dn_ref.shape[1]
    step = pl.program_id(0)

    @pl.when(step == 0)
    def _():
        og_ref[...] = up_ref[...].astype(BF)
        dn_ref[...] = jnp.zeros_like(dn_ref)
        dq_ref[...] = jnp.zeros_like(dq_ref)
        dconv_ref[...] = dot_tn(n2_ref[...], dg_ref[...]).astype(BF)

    og = og_ref[...]
    tw = tw_ref[0]
    do_f = dot(og, tw[:, 384:512]).astype(BF).astype(F32) * scale_ref[0]
    do = do_f.astype(BF)
    key, value = kv_ref[0, :, :128], kv_ref[0, :, 128:]
    first = lax.broadcasted_iota(jnp.int32, (rows, 128), 1) < 64
    mixed = o_ref[0]
    do_t = do_f.T.astype(BF)
    qc_t = (q_ref[0, 0].astype(F32) * SCALE).T.astype(BF)
    qp_t = q_ref[0, 1].astype(F32).T.astype(BF)
    cos, sin = cs_ref[0], cs_ref[1]
    dqcs, dqps, dks, dvs, dps = [], [], [], [], []
    for head, (do_h, inner_h) in enumerate(zip(halves(first, do), halves(first, do_f * mixed))):
        mine = slice(head * 64, head * 64 + 64)
        inner = jnp.sum(inner_h, axis=1, keepdims=True)
        for r in range(0, rows, CHUNK):
            dw = dot_nt(do_h[r : r + CHUNK], value)
            weights = w_ref[0, head, r : r + CHUNK, :].astype(F32)
            dr_ref[r : r + CHUNK, :] = (weights * (dw - inner[r : r + CHUNK])).astype(BF)
        dr = dr_ref[...]
        turned = dot(dr, e_ref[...]) * SCALE
        dqcs.append(dot(dr, key) * SCALE)
        dks.append(dot(qc_t[mine], dr).astype(BF))
        dvs.append(dot(do_t[mine], w_ref[0, head]).astype(BF))
        gs, gc = turned[:, :half], turned[:, half:]
        du = jnp.concatenate(
            [(gs * cos - gc * sin).astype(BF), (gs * sin + gc * cos).astype(BF)], axis=1
        )
        dqps.append(dot(du, pos_ref[0]))
        dps.append(dot(qp_t[mine], du))
    dqc = jnp.where(first, dqcs[0], dqcs[1])
    dqp = jnp.where(first, dqps[0], dqps[1])
    db_ref[0, 0:1, :] = jnp.sum(dqc, axis=0, keepdims=True)
    db_ref[0, 1:2, :] = jnp.sum(dqp, axis=0, keepdims=True)
    dq = dqc + dqp
    dq_low = dq.astype(BF)
    dkv = jnp.concatenate(dks + dvs, axis=0)
    dn_ref[...] += dot(tw[:, 128:384], dkv)
    dq_ref[...] += dot_nt(dq_low, tw[:, :128])
    grad_kv = jnp.zeros((256, width), F32)
    for k, ref in enumerate((own_ref, k1_ref, k2_ref, k3_ref)):
        grad_kv = grad_kv + dot(dkv[:, k * rows : k * rows + rows], ref[...])
    grad_q = dot(dq.T.astype(BF), own_ref[...])
    grad_o = dot(mixed.T.astype(BF), og)
    tw_grad_ref[...] = jnp.concatenate([grad_q, grad_kv, grad_o], axis=0).T.astype(BF)
    pos_grad_ref[...] = jnp.concatenate(dps, axis=0).T.astype(BF)

    if fast:
        z, y, x, c = place()
        pair = (x ^ (step // 2)) * 2 + (c ^ (step % 2))

        def write(pack_ref):
            for ky in range(2):
                for i in range(4):
                    at = (z ^ KZ[i]) * 2 + (y ^ ky)
                    pack_ref[ky, i, 0, :, 0:512] = tw_grad_ref[part(at, 64), :]
                    pack_ref[ky, i, 0, 0:32, 512:640] = pos_grad_ref[part(at, 32), :]
                    pack_ref[ky, i, 0, 32:64, 512:640] = pos_grad_ref[part(at + 8, 32), :]
                    for t in range(4):
                        pack_ref[ky, i, 0, 16 * t : 16 * t + 16, 640:896] = dconv_ref[
                            part(at * 4 + pair, 16), 256 * t : 256 * t + 256
                        ]

        pl.when(step % 2 == 0)(lambda: write(outs[0]))
        pl.when(step % 2 == 1)(lambda: write(outs[1]))
    else:
        outs[0][0] = tw_grad_ref[...]
        outs[1][0] = pos_grad_ref[...]
        outs[2][...] = dconv_ref[...]

    @pl.when(step == pl.num_programs(0) - 1)
    def _():
        for k in range(4):
            grad = dn_ref[:, k * rows : k * rows + rows].T
            if k == 0:
                home_ref[...] = grad + dq_ref[...]
            elif k == 2:
                far_ref[...] = grad.astype(BF)
            else:
                near_ref[k // 2] = grad.astype(BF)


def att_backward(fast, upstream, n2, dgated, keys, mixed, scale, weights, kv, queries, tw, pos, cs, e):
    rows, width = upstream.shape
    count = kv.shape[1]
    shared = [shaped((2, rows, width), BF), shaped((rows, width), BF), shaped((rows, width), F32)]
    paired = [shaped((4, 2, 128), F32)]
    specs = [whole(a) for a in shared] + [per_pair(a) for a in paired]
    outs = shared + paired
    if fast:
        extra = [shaped((2, 4, 2, 64, 896), BF)] * 2
        specs += [pl.BlockSpec((2, 4, 1, 64, 896), lambda h: (0, 0, h // 2, 0, 0))] * 2
    else:
        extra = [shaped((4, width, 512), BF), shaped((4, width, 128), BF), shaped((width, 1024), BF)]
        specs += [per_pair(extra[0]), per_pair(extra[1]), whole(extra[2])]
    return pl.pallas_call(
        lambda *refs: att_backward_kernel(fast, *refs),
        grid=(4,),
        in_specs=[whole(upstream), whole(n2), whole(dgated)]
        + [whole(k) for k in keys]
        + [per_pair(mixed), per_pair(scale), per_pair(weights), per_pair(kv), per_pair(queries), per_pair(tw), per_pair(pos)]
        + [whole(cs), whole(e)],
        out_specs=specs,
        out_shape=outs + extra,
        scratch_shapes=[
            pltpu.VMEM((rows, count), BF),
            pltpu.VMEM((width, count), F32),
            pltpu.VMEM((rows, width), F32),
            pltpu.VMEM((rows, width), BF),
            pltpu.VMEM((width, 1024), BF),
            pltpu.VMEM((width, 512), BF),
            pltpu.VMEM((width, 128), BF),
        ],
        compiler_params=pltpu.CompilerParams(vmem_limit_bytes=VMEM_BYTES),
        cost_estimate=cost(0.01),
        name="att_backward",
    )(upstream, n2, dgated, *keys, mixed, scale, weights, kv, queries, tw, pos, cs, e)


def gate_forward(ints, n2, conv_in):
    rows, width = n2.shape

    def kernel(ints_ref, n2_ref, *refs):
        w_refs, (glu_ref, gated_ref, half_ref) = refs[:2], refs[2:]
        half_ref[0] = w_refs[0][...].reshape(width, width)
        half_ref[1] = w_refs[1][...].reshape(width, width)
        left = dot(n2_ref[...], half_ref[0])
        right = dot(n2_ref[...], half_ref[1])
        gated_ref[:, :width] = left
        gated_ref[:, width:] = right
        glu_ref[...] = (left * jax.nn.sigmoid(right) * valid_rows(ints_ref, rows)).astype(BF)

    if len(conv_in) == 1:
        conv_in = conv_in * 2
        specs = [
            pl.BlockSpec((32, 16, 512), lambda *_, at=at: (0, at, 0), pipeline_mode=pl.Buffered(1)) for at in (8, 9)
        ]
    else:
        specs = [whole(a) for a in conv_in]
    return run(
        kernel,
        [ints, n2] + conv_in,
        [shaped((rows, width), BF), shaped((rows, 2 * width), F32)] + [shaped((2, width, width), BF)],
        "gate_forward",
        specs=[SMEM, whole(n2)] + specs,
        grid=(1,),
        limit=60,
    )


def extend(ext_ref, before_ref, own_ref, after_ref):
    rows = own_ref.shape[0]
    ext_ref[0, 0:HALO, :] = before_ref[...].astype(F32)
    ext_ref[0, HALO : HALO + rows, :] = own_ref[...].astype(F32)
    ext_ref[0, HALO + rows : 2 * HALO + rows, :] = after_ref[...].astype(F32)
    kept = 2 * HALO + rows - 8
    for shift in range(1, 8):
        ext_ref[shift, 0:kept, :] = ext_ref[0, shift : shift + kept, :]


def shifted(ext_ref, start, size, columns):
    return ext_ref[start % 8, start - start % 8 : start - start % 8 + size, columns]


def conv_forward(ints, glu, rim, small):
    rows, width = glu.shape

    def kernel(ints_ref, before_ref, glu_ref, after_ref, small_ref, depth_ref, sums_ref, ext_ref):
        extend(ext_ref, before_ref, glu_ref, after_ref)
        steps = lax.broadcasted_iota(jnp.int32, (64, 1), 0) + ints_ref[1]
        for c in range(0, width, 128):
            one = jnp.zeros((1, 128), F32)
            two = jnp.zeros((1, 128), F32)
            for r in range(0, rows, 64):
                total = jnp.zeros((64, 128), F32)
                for k in range(2 * HALO):
                    total = total + shifted(ext_ref, r + k + 1, 64, slice(c, c + 128)) * small_ref[k : k + 1, c : c + 128]
                depth_ref[r : r + 64, c : c + 128] = total
                kept = jnp.where(steps + r < ints_ref[0], total, 0.0)
                one = one + jnp.sum(kept, axis=0, keepdims=True)
                two = two + jnp.sum(kept * total, axis=0, keepdims=True)
            sums_ref[0:1, c : c + 128] = one
            sums_ref[1:2, c : c + 128] = two

    return run(
        kernel,
        [ints, rim[0], glu, rim[1], small],
        [shaped((rows, width), F32), shaped((2, width), F32)],
        "conv_forward",
        time=4,
        specs=[SMEM] + [VMEM] * 4,
        scratch=[pltpu.VMEM((8, rows + 2 * HALO, width), F32)],
    )


def conv_backward(ints, glu, rim, depth_low, depth_rim, small, gated, conv_in, after_att, upstream):
    rows, width = glu.shape

    def kernel(
        ints_ref, gb_ref, glu_ref, ga_ref, db_ref, d_ref, da_ref, small_ref, gated_ref, att_ref, up_ref, *refs
    ):
        w_ref, out_ref, dg_ref, grads_ref, ext_ref, extd_ref, dglu_ref = refs
        extend(ext_ref, gb_ref, glu_ref, ga_ref)
        extend(extd_ref, db_ref, d_ref, da_ref)
        taps = 2 * HALO
        for c in range(0, width, 128):
            cols = slice(c, c + 128)
            for r in range(0, rows, 64):
                total = jnp.zeros((64, 128), F32)
                for k in range(taps):
                    at = r + taps - 1 - k
                    total = total + shifted(extd_ref, at, 64, cols) * small_ref[k : k + 1, cols]
                dglu_ref[r : r + 64, cols] = total
            for k in range(taps):
                total = jnp.zeros((8, 128), F32)
                for r in range(0, rows, 64):
                    product = shifted(ext_ref, r + k + 1, 64, cols) * shifted(extd_ref, HALO + r, 64, cols)
                    total = total + jnp.sum(product.reshape(8, 8, 128), axis=0)
                grads_ref[k : k + 1, cols] = jnp.sum(total, axis=0, keepdims=True)
        grad = dglu_ref[...] * valid_rows(ints_ref, rows)
        gate = jax.nn.sigmoid(gated_ref[:, width:])
        left = (grad * gate).astype(BF)
        right = (grad * gated_ref[:, :width] * gate * (1.0 - gate)).astype(BF)
        dg_ref[:, :width] = left
        dg_ref[:, width:] = right
        inner = dot_nt(left, w_ref[0]) + dot_nt(right, w_ref[1])
        normed, scale = norm(att_ref[...])
        grad, gain_grad, bias_grad = norm_back(inner, normed, scale, row(small_ref, GAIN + 2))
        out_ref[...] = up_ref[...] + grad
        grads_ref[taps : taps + 1, :] = gain_grad
        grads_ref[taps + 1 : taps + 2, :] = bias_grad

    inputs = [ints, rim[0], glu, rim[1], depth_rim[0], depth_low, depth_rim[1], small, gated]
    return run(
        kernel,
        inputs + [after_att, upstream, conv_in],
        [shaped((rows, width), F32), shaped((rows, 2 * width), BF), shaped((40, width), F32)],
        "conv_backward",
        time=0.01,
        specs=[SMEM] + [VMEM] * (len(inputs) + 2),
        scratch=[pltpu.VMEM((8, rows + 2 * HALO, width), F32)] * 2 + [pltpu.VMEM((rows, width), F32)],
    )


def middle(ints, floats, depth, sums, after_att, cotangent, small, weights):
    rows, width = depth.shape

    def kernel(
        ints_ref, floats_ref, depth_ref, sums_ref, att_ref, cot_ref, small_ref, *refs
    ):
        w_refs = refs[:-12]
        (layer_ref, up_ref, raw_ref, gsum_ref, grads_ref, pre_ref, act_ref, dhid_ref, branch_ref, swish_ref, low_ref,
         hid_ref) = refs[-12:]
        packed = len(w_refs) == 1
        columns = hid_ref.shape[0]

        def w_in(column):
            if packed:
                return w_refs[0][:, 16 * column : 16 * column + 16, :].reshape(width, 512)
            return w_refs[0][column]

        def w_out(column):
            if packed:
                return w_refs[0][8 * column : 8 * column + 8, 64:128, :].reshape(512, width)
            return w_refs[1][column]

        total_valid = floats_ref[1]
        mean_bn = sums_ref[0:1, :] / total_valid
        var_bn = sums_ref[1:2, :] / total_valid - mean_bn * mean_bn
        inv = lax.rsqrt(var_bn + epsilon)
        center = depth_ref[...] - mean_bn
        bn_gain = row(small_ref, GAIN + 5)
        z = center * inv * bn_gain + row(small_ref, BIAS + 5)
        swish = (z * jax.nn.sigmoid(z)).astype(BF)
        swish_ref[...] = swish
        conv_out = w_refs[0][:, 160:176, :].reshape(width, width) if packed else w_refs[2][...]
        after_conv = att_ref[...] + dot(swish, conv_out)
        normed3, scale3 = norm(after_conv)
        pre = (normed3 * row(small_ref, GAIN + 3) + row(small_ref, BIAS + 3)).astype(BF)
        pre_ref[...] = pre
        total = jnp.zeros((rows, width), F32)
        for column in range(columns):
            hidden = dot(pre, w_in(column))
            hid_ref[column] = hidden
            active = (hidden * jax.nn.sigmoid(hidden)).astype(BF)
            act_ref[column] = active
            total = total + dot(active, w_out(column))
        normed4, scale4 = norm(after_conv + 0.5 * total)
        gain4 = row(small_ref, GAIN + 4)
        layer_ref[...] = (normed4 * gain4 + row(small_ref, BIAS + 4)).astype(BF)
        seed = cot_ref[...].astype(F32) * (valid_rows(ints_ref, rows) * floats_ref[0])
        up, gain_grad, bias_grad = norm_back(seed, normed4, scale4, gain4)
        grads_ref[...] = jnp.zeros_like(grads_ref)
        grads_ref[2:3, :] = gain_grad
        grads_ref[3:4, :] = bias_grad
        branch = (0.5 * up).astype(BF)
        branch_ref[...] = branch
        total = jnp.zeros((rows, width), F32)
        for column in range(columns):
            hidden = hid_ref[column]
            gate = jax.nn.sigmoid(hidden)
            grad = dot_nt(branch, w_out(column)) * (gate * (1.0 + hidden * (1.0 - gate)))
            grad = grad.astype(BF)
            dhid_ref[column] = grad
            total = total + dot_nt(grad, w_in(column))
        grad, gain_grad, bias_grad = norm_back(total, normed3, scale3, row(small_ref, GAIN + 3))
        grads_ref[0:1, :] = gain_grad
        grads_ref[1:2, :] = bias_grad
        up = up + grad
        up_ref[...] = up
        low = up.astype(BF)
        low_ref[...] = low
        gate = jax.nn.sigmoid(z)
        dz = dot_nt(low, conv_out) * (gate * (1.0 + z * (1.0 - gate)))
        grads_ref[4:5, :] = jnp.sum(dz * center, axis=0, keepdims=True) * inv
        grads_ref[5:6, :] = jnp.sum(dz, axis=0, keepdims=True)
        raw = dz * (bn_gain * inv)
        raw_ref[...] = raw
        gsum_ref[0:1, :] = -jnp.sum(raw, axis=0, keepdims=True)
        gsum_ref[1:2, :] = jnp.sum(raw * center, axis=0, keepdims=True) * (-0.5 * inv * inv)

    square_f, square = shaped((rows, width), F32), shaped((rows, width), BF)
    wide = shaped((4, rows, 512), BF)
    inputs = [ints, floats, depth, sums, after_att, cotangent, small]
    return run(
        kernel,
        inputs + weights,
        [square, square_f, square_f, shaped((2, width), F32), shaped((8, width), F32)]
        + [square, wide, wide, square, square, square],
        "middle",
        time=8,
        specs=[SMEM, SMEM] + [VMEM] * (len(inputs) - 2 + len(weights)),
        scratch=[pltpu.VMEM((4, rows, 512), F32)],
    )


def middle_grads(fast, pre, act, dhid, branch, swish, low):
    width = pre.shape[1]

    def kernel(pre_ref, act_ref, dhid_ref, branch_ref, swish_ref, low_ref, *outs):
        for column in range(act_ref.shape[0]):
            grad_in = dot_tn(pre_ref[...], dhid_ref[column]).astype(BF)
            grad_out = dot_tn(act_ref[column], branch_ref[...]).astype(BF)
            if fast:
                outs[0][:, 16 * column : 16 * column + 16, :] = grad_in.reshape(32, 16, 512)
                outs[0][8 * column : 8 * column + 8, 64:128, :] = grad_out.reshape(8, 64, 512)
            else:
                outs[0][column] = grad_in
                outs[1][column] = grad_out
        grad = dot_tn(swish_ref[...], low_ref[...]).astype(BF)
        if fast:
            outs[0][:, 128:144, :] = grad.reshape(32, 16, 512)
        else:
            outs[2][...] = grad

    if fast:
        outs = [shaped((32, 144, 512), BF)]
    else:
        outs = [shaped((4, width, 512), BF), shaped((4, 512, width), BF), shaped((width, width), BF)]
    return run(kernel, [pre, act, dhid, branch, swish, low], outs, "middle_grads", time=3)


def ffn1_again(frames, x1, win, wout, small, home, near):
    rows, width = x1.shape

    def kernel(
        x_in, x1_in, win_in, wout_in, small_ref, home_ref, near_ref,
        pre_ref, act_ref, slope_ref, x1_ref, x_ref, win_ref, wout_ref, sum_ref, sems,
    ):
        pairs = ((x_in, x_ref), (win_in, win_ref), (x1_in, x1_ref), (wout_in, wout_ref))
        copies = [pltpu.make_async_copy(a, b, sems.at[k]) for k, (a, b) in enumerate(pairs)]
        for copy in copies:
            copy.start()
        copies[0].wait()
        normed, _ = norm(x_ref[...].astype(F32))
        pre = (normed * row(small_ref, GAIN) + row(small_ref, BIAS)).astype(BF)
        pre_ref[...] = pre
        sum_ref[...] = home_ref[...] + near_ref[0].astype(F32)
        copies[1].wait()
        for column in range(win.shape[0]):
            hidden = dot(pre, win_ref[column])
            gate = jax.nn.sigmoid(hidden)
            act_ref[column] = (hidden * gate).astype(BF)
            slope_ref[column] = gate * (1.0 + hidden * (1.0 - gate))
        copies[2].wait()
        copies[3].wait()

    wide = (win.shape[0], rows, 512)
    return run(
        kernel,
        [frames, x1, win, wout, small, home, near],
        [shaped((rows, width), BF), shaped(wide, BF), shaped(wide, F32), shaped(x1.shape, F32)]
        + [shaped(frames.shape, BF), shaped(win.shape, BF), shaped(wout.shape, BF), shaped(home.shape, F32)],
        "ffn1_again",
        time=0.01,
        specs=[pl.BlockSpec(memory_space=pltpu.HBM)] * 4 + [VMEM] * 3,
        scratch=[pltpu.SemaphoreType.DMA((4,))],
    )


def ffn1_backward(fast, again, upstream, far, small, conv_rows, mid_rows, grad_bias):
    pre, active, slope, x1, frames, win, wout, home = again
    rows, width = x1.shape

    def kernel(
        pre_ref, act_ref, slope_ref, x1_ref, x_ref, win_ref, wout_ref, home_ref, up_ref, far_ref, small_ref,
        conv_ref, mid_ref, bias_ref,
        *refs,
    ):
        frames_ref, outs, (chan_ref, gin_ref, gout_ref) = refs[0], refs[1:-3], refs[-3:]
        dn = home_ref[...] + far_ref[...].astype(F32)
        normed, scale = norm(x1_ref[...])
        grad, gain1, bias1 = norm_back(dn, normed, scale, row(small_ref, GAIN + 1))
        up = up_ref[...] + grad
        branch = (0.5 * up).astype(BF)
        normed, scale = norm(x_ref[...].astype(F32))
        gain0 = row(small_ref, GAIN)
        pre = pre_ref[...]
        total = jnp.zeros((rows, width), F32)
        for column in range(win_ref.shape[0]):
            gout_ref[512 * column : 512 * column + 512, :] = dot_tn(act_ref[column], branch).astype(BF)
            grad = dot_nt(branch, wout_ref[512 * column : 512 * column + 512, :])
            grad = (grad * slope_ref[column]).astype(BF)
            gin_ref[column] = dot_tn(pre, grad).astype(BF)
            total = total + dot_nt(grad, win_ref[column])
        grad, gain_grad, bias_grad = norm_back(total, normed, scale, gain0)
        frames_ref[...] = (up + grad).astype(BF)
        chan_ref[...] = jnp.zeros_like(chan_ref)
        taps = GAIN
        chan_ref[0:taps, :] = conv_ref[0:taps, :]
        for first, at in ((GAIN, 0), (BIAS, 1)):
            chan_ref[first + 2 : first + 3, :] = conv_ref[taps + at : taps + at + 1, :]
            for k in range(3):
                chan_ref[first + 3 + k : first + 4 + k, :] = mid_ref[2 * k + at : 2 * k + at + 1, :]
        chan_ref[POS_BIAS : POS_BIAS + 2, :] = bias_ref[...]
        chan_ref[GAIN : GAIN + 1, :] = gain_grad
        chan_ref[GAIN + 1 : GAIN + 2, :] = gain1
        chan_ref[BIAS : BIAS + 1, :] = bias_grad
        chan_ref[BIAS + 1 : BIAS + 2, :] = bias1
        if fast:
            a_far, a_own, b_far, b_own = outs
            turned = chan_ref[...].T.astype(BF)
            for kc, a_out, b_out in ((1, a_far, b_far), (0, a_own, b_own)):
                for one in range(2):
                    for two in range(2):
                        for i in range(4):
                            at = block_index(KZ[i], two, one, kc)
                            for column in range(4):
                                a_out[one, two, i, 16 * column : 16 * column + 16, :] = gin_ref[
                                    column, part(at, 16), :
                                ]
                            at = block_index(KZ[i], one, two, kc)
                            b_out[one, two, i] = gout_ref[part(at, 64), :]
            gin_ref[0, :, 0:128] = turned
            for kc, a_out in ((1, a_far), (0, a_own)):
                for one in range(2):
                    for two in range(2):
                        for i in range(4):
                            at = block_index(KZ[i], two, one, kc)
                            own = gin_ref[0, part(at, 16), 0:128].astype(F32)
                            own = jnp.concatenate([own[0:8], own[8:16], jnp.zeros((8, 256), F32)], axis=1)
                            a_out[one, two, i, 64:72, :] = own.astype(BF)
        else:
            outs[0][...] = gin_ref[...]
            outs[1][...] = gout_ref[...]
            outs[2][...] = chan_ref[...].T.astype(BF)

    if fast:
        outs = [shaped((2, 2, 4, 72, 512), BF)] * 2 + [shaped((2, 2, 4, 64, 512), BF)] * 2
    else:
        outs = [shaped((4, width, 512), BF), shaped((2048, width), BF), shaped((width, 128), BF)]
    return run(
        kernel,
        list(again) + [upstream, far, small, conv_rows, mid_rows, grad_bias],
        [shaped((rows, width), BF)] + outs,
        "ffn1_backward",
        time=0.01,
        scratch=[
            pltpu.VMEM((128, width), F32),
            pltpu.VMEM((4, width, 512), BF),
            pltpu.VMEM((2048, width), BF),
        ],
    )


def tables(head_index, own_length, rows, width):
    pairs = lax.axis_size("heads")
    freq = jnp.exp(
        jnp.arange(width // 2, dtype=jnp.int32).astype(F32) * (-2.0 * math.log(10000.0) / width)
    )
    steps = rows // 128
    others = jnp.arange(pairs, dtype=jnp.int32) ^ head_index
    coarse = (others[:, None] * steps + jnp.arange(steps, dtype=jnp.int32)[None, :]).reshape(-1)
    coarse_phase = (coarse * 128).astype(F32)[:, None] * freq[None, :]
    fine_phase = jnp.arange(128, dtype=jnp.int32).astype(F32)[:, None] * freq[None, :]
    phase = jnp.concatenate([coarse_phase, fine_phase])
    info = jnp.stack([head_index, own_length]).astype(jnp.int32)
    count = pairs * rows
    half = width // 2

    def kernel(info_ref, sin_ref, cos_ref, table_ref, turned_ref, own_ref, mask_ref):
        sin_b, cos_b = sin_ref[pairs * steps :, :], cos_ref[pairs * steps :, :]
        for a in range(pairs * steps):
            here = slice(128 * a, 128 * a + 128)
            sin_a, cos_a = sin_ref[a : a + 1, :], cos_ref[a : a + 1, :]
            sin = sin_a * cos_b + cos_a * sin_b
            cos = cos_a * cos_b - sin_a * sin_b
            table_ref[here, :half] = sin.astype(BF)
            table_ref[here, half:] = cos.astype(BF)
            turned_ref[:half, here] = sin.T.astype(BF)
            turned_ref[half:, here] = cos.T.astype(BF)
            if a < steps:
                own_ref[0, here, :] = cos
                own_ref[1, here, :] = sin
            at = lax.broadcasted_iota(jnp.int32, (1, 128), 1)
            at = at + ((info_ref[0] ^ (a // steps)) * rows + 128 * (a % steps))
            mask_ref[0:1, here] = jnp.where(at < info_ref[1], 0.0, -1e30)

    return run(
        kernel,
        [info, jnp.sin(phase), jnp.cos(phase)],
        [shaped((count, width), BF), shaped((width, count), BF), shaped((2, rows, half), F32), shaped((1, count), F32)],
        "tables",
        specs=[SMEM, VMEM, VMEM],
    )


def prepare(ffn1_out, dw_kernel, norm_gain, norm_bias, pos_bias, att_proj, att_out, ffn2_in, ffn2_out, conv_in, conv_out):
    head_dim = att_out.shape[1]

    dw_kernel = dw_kernel.T

    def kernel(
        out1_ref, dw_ref, gain_ref, bias_ref, posb_ref, proj_ref, att_ref, in2_ref, out2_ref, cin_ref, cout_ref,
        b_ref, t_ref, pack_ref, square_ref, pos_ref,
    ):
        b_ref[0:64, :] = out1_ref[...]
        square_ref[...] = jnp.zeros_like(square_ref)
        square_ref[GAIN:BIAS, 0:16] = gain_ref[...].astype(F32)
        square_ref[BIAS:POS_BIAS, 0:16] = bias_ref[...].astype(F32)
        square_ref[POS_BIAS : POS_BIAS + 2, 0:16] = posb_ref[...].astype(F32)
        square_ref[...] = square_ref[...].T
        square_ref[0:16, 0:GAIN] = dw_ref[...].astype(F32)
        turned = square_ref[0:16, :]
        b_ref[64:72, :] = jnp.concatenate([turned[0:8], turned[8:16], jnp.zeros((8, 256), F32)], axis=1).astype(BF)
        both = [proj_ref[h].astype(F32) for h in range(2)]
        for k in range(3):
            columns = slice(k * head_dim, k * head_dim + head_dim)
            t_ref[:, 128 * k : 128 * k + 128] = jnp.concatenate([p[:, columns] for p in both], axis=1).astype(BF)
        square_ref[...] = jnp.zeros_like(square_ref)
        square_ref[0:64, 0:64] = att_ref[0].astype(F32)
        square_ref[64:128, 0:64] = att_ref[1].astype(F32)
        t_ref[:, 384:512] = square_ref[...].T[0:64].astype(BF)
        pos_ref[...] = jnp.concatenate([p[:, 3 * head_dim :] for p in both], axis=1)
        for k in range(2):
            t_ref[32 * k : 32 * k + 32, 512:640] = pos_ref[pl.ds(k, 32, stride=2), :].astype(BF)
        for k in range(4):
            pack_ref[16 * k : 16 * k + 16, :] = in2_ref[:, 512 * k : 512 * k + 512]
        pack_ref[64:128, :] = out2_ref[...]
        for k in range(2):
            pack_ref[128 + 16 * k : 144 + 16 * k, :] = cin_ref[:, 512 * k : 512 * k + 512]
        pack_ref[160:176, :] = cout_ref[...]

    return run(
        kernel,
        [ffn1_out, dw_kernel, norm_gain, norm_bias, pos_bias, att_proj, att_out, ffn2_in, ffn2_out, conv_in, conv_out],
        [shaped((72, 512), BF), shaped((64, 640), BF), shaped((176, 512), BF)],
        "prepare",
        specs=[whole(a) for a in (ffn1_out, dw_kernel, norm_gain, norm_bias, pos_bias, att_proj, att_out)]
        + [whole(a) for a in (ffn2_in, ffn2_out, conv_in, conv_out)],
        grid=(1,),
        scratch=[pltpu.VMEM((128, 128), F32), pltpu.VMEM((64, 128), F32)],
        limit=60,
    )


def own_terms(terms):
    def spec(array):
        lead = len(array.shape) - 2
        return pl.BlockSpec((1,) * lead + array.shape[lead:], lambda *_: (0,) * (lead + 2))

    return list(terms), [spec(t) for t in terms]


def add_terms(refs):
    rows, columns = refs[0].shape[-2:]
    total = refs[0][...].reshape(rows, columns).astype(F32)
    for ref in refs[1:]:
        total = total + ref[...].reshape(rows, columns).astype(F32)
    return total


def finish_first(terms_a, terms_b):
    inputs, specs = own_terms(terms_a + terms_b)

    def kernel(*refs):
        in_ref, out_ref, dw_ref, gain_ref, bias_ref, posb_ref, square_ref = refs[12:]
        total = add_terms(refs[:6])
        for k in range(4):
            in_ref[:, 512 * k : 512 * k + 512] = total[16 * k : 16 * k + 16, :]
        square_ref[...] = jnp.zeros_like(square_ref)
        square_ref[0:8, :] = total[64:72, 0:128]
        square_ref[8:16, :] = total[64:72, 128:256]
        turned = square_ref[...].T
        dw_ref[...] = square_ref[0:16, 0:GAIN]
        gain_ref[...] = turned[GAIN:BIAS, 0:16]
        bias_ref[...] = turned[BIAS:POS_BIAS, 0:16]
        posb_ref[...] = turned[POS_BIAS : POS_BIAS + 2, 0:16]
        out_ref[...] = add_terms(refs[6:12])

    outs = [(16, 2048), (64, 512), (16, 32), (6, 16), (6, 16), (2, 16)]
    rows_in, rows_out, taps, *rest = run(
        kernel,
        inputs,
        [shaped(o, F32) for o in outs],
        "finish_first",
        specs=specs,
        grid=(1,),
        scratch=[pltpu.VMEM((128, 128), F32)],
    )
    return rows_in, rows_out, taps.T, *rest


def finish_attention(terms):
    inputs, specs = own_terms(terms)

    def kernel(*refs):
        proj_ref, out_ref, cin_ref, square_ref, pos_ref = refs[len(inputs) :]
        total = add_terms(refs[: len(inputs)])
        square_ref[...] = jnp.zeros_like(square_ref)
        square_ref[0:64, :] = total[:, 384:512]
        turned = square_ref[...].T
        for k in range(2):
            pos_ref[pl.ds(k, 32, stride=2), :] = total[32 * k : 32 * k + 32, 512:640]
        for h in range(2):
            for k in range(3):
                at = 128 * k + 64 * h
                proj_ref[h, :, 64 * k : 64 * k + 64] = total[:, at : at + 64]
            proj_ref[h, :, 192:256] = pos_ref[:, 64 * h : 64 * h + 64]
            out_ref[h] = turned[64 * h : 64 * h + 64, 0:64]
        for k in range(4):
            cin_ref[:, 256 * k : 256 * k + 256] = total[16 * k : 16 * k + 16, 640:896]

    return run(
        kernel,
        inputs,
        [shaped((2, 64, 256), F32), shaped((2, 64, 64), F32), shaped((16, 1024), F32)],
        "finish_attention",
        specs=specs,
        grid=(1,),
        scratch=[pltpu.VMEM((128, 128), F32), pltpu.VMEM((64, 128), F32)],
    )


def finish_middle(sums):
    def kernel(sum_ref, in_ref, out_ref, conv_ref):
        for k in range(4):
            in_ref[:, 512 * k : 512 * k + 512] = sum_ref[16 * k : 16 * k + 16, :].astype(F32)
        out_ref[...] = sum_ref[64:128, :].astype(F32)
        conv_ref[...] = sum_ref[128:144, :].astype(F32)

    return run(
        kernel,
        [sums],
        [shaped((16, 2048), F32), shaped((64, 512), F32), shaped((16, 512), F32)],
        "finish_middle",
    )


def small_shard(dw_kernel, norm_gain, norm_bias, pos_bias):
    stacked = jnp.concatenate([dw_kernel, norm_gain, norm_bias, pos_bias], axis=0)
    return jnp.pad(stacked.T, ((0, 0), (0, 128 - stacked.shape[0])))


def att_shard(att_proj, att_out):
    two, rows, four = att_proj.shape
    head_dim = four // 4
    parts = att_proj.reshape(two, rows, 4, head_dim).transpose(1, 2, 0, 3)
    parts = parts.reshape(rows, 4, two * head_dim)
    out_t = att_out.transpose(2, 0, 1).reshape(rows, two * head_dim)
    turned = parts[:, 3].reshape(rows // 2, 2, two * head_dim).transpose(1, 0, 2)
    turned = turned.reshape(rows, two * head_dim)
    return jnp.concatenate([parts[:, 0], parts[:, 1], parts[:, 2], out_t, turned], axis=1)


def column_chunks(array):
    rows, columns = array.shape
    return array.reshape(rows, columns // 512, 512).transpose(1, 0, 2)


def xor_order(array, index):
    bit = 1
    while bit < array.shape[0]:
        flipped = jnp.stack([array[i ^ bit] for i in range(array.shape[0])])
        array = jnp.where((index & bit) != 0, flipped, array)
        bit *= 2
    return array


def rows_of(shard):
    return lax.all_gather(shard, BOTH, axis=0, tiled=True)


def sum_rows(grad):
    return lax.psum_scatter(grad.astype(F32), BOTH, scatter_dimension=0, tiled=True)


def local(
    frames_in,
    cotangent,
    lengths,
    sample_weight,
    ffn1_in,
    ffn1_out,
    att_proj,
    att_out,
    pos_bias,
    conv_in,
    dw_kernel,
    conv_out,
    ffn2_in,
    ffn2_out,
    norm_gain,
    norm_bias,
):
    row_count, model_width = frames_in.shape
    pairs = lax.axis_size("heads")
    batches = lax.axis_size("batch")
    head_index = lax.axis_index("heads")
    batch_index = lax.axis_index("batch")
    channels = ffn1_in.shape[0]
    fast = channels == 16 and batches == 8 and pairs == 4
    kernel_len = dw_kernel.shape[0]
    head_dim = att_out.shape[1]
    width = model_width // batches

    utter_ids = jnp.arange(lengths.shape[0], dtype=jnp.int32)
    own_length = jnp.sum(jnp.where(utter_ids == batch_index, lengths, 0))
    own_weight = jnp.sum(jnp.where(utter_ids == batch_index, sample_weight, 0)).astype(F32) * 0.25
    total_valid = jnp.sum(lengths).astype(F32)
    ints = jnp.stack([own_length, head_index * row_count]).astype(jnp.int32)
    floats = jnp.stack([own_weight, total_valid])

    if fast:
        shard_b, shard_t, pack = prepare(
            ffn1_out, dw_kernel, norm_gain, norm_bias, pos_bias, att_proj, att_out, ffn2_in, ffn2_out, conv_in, conv_out
        )
        held_a, held_b = gather_depth(ffn1_in), gather_depth(shard_b)
        held_t = jnp.stack([shard_t, swap(shard_t, "heads", 2)])
        held_a, held_b, held_t = lax.optimization_barrier((held_a, held_b, held_t))
        side_a, side_b, deep_t = swap(held_a, "batch", 1), swap(held_b, "heads", 2), swap(held_t, "batch", 4)
        side_a, side_b, deep_t = lax.optimization_barrier((side_a, side_b, deep_t))
        held_a, held_b, held_t = (jnp.concatenate(p) for p in ((held_a, side_a), (held_b, side_b), (held_t, deep_t)))
        side_a, side_b, deep_t = swap(held_a, "heads", 2), swap(held_b, "batch", 1), swap(held_t, "batch", 2)
        table, table_t, own_turn, key_mask = tables(behind(head_index, held_a, held_b), own_length, row_count, model_width)
        table, table_t, own_turn, key_mask, ints, floats, side_a, side_b, deep_t = lax.optimization_barrier(
            (table, table_t, own_turn, key_mask, ints, floats, side_a, side_b, deep_t)
        )
        held_t = jnp.concatenate([held_t, deep_t])
        side_t = swap(held_t, "batch", 1)
        pack = lax.all_gather(behind(pack, held_a, held_b), BOTH, axis=0)
        win, wout, small_t, pos_b = place_first(
            (held_a, side_a, swap(held_a, "heads", 1), swap(side_a, "heads", 1)),
            (held_b, side_b, swap(held_b, "heads", 1), swap(side_b, "heads", 1)),
        )
        x1, n1 = ffn1_forward(frames_in, win, wout, small_t)
        held_t, side_t = behind(held_t, n1), behind(side_t, n1)
        sides_t = held_t, side_t
        tw, pos_w = place_attention(sides_t + tuple(swap(t, "heads", 1) for t in sides_t))
        conv_in_w = middle_w = [pack]
    else:
        table, table_t, own_turn, key_mask = tables(head_index, own_length, row_count, model_width)
        small = small_shard(dw_kernel, norm_gain, norm_bias, pos_bias)
        att_part = att_shard(att_proj, att_out)
        win, wout = column_chunks(rows_of(ffn1_in)), rows_of(ffn1_out)
        small_t = rows_of(small).T.astype(F32)
        pos_b = small_t[POS_BIAS : POS_BIAS + 2].reshape(2, batches, pairs, channels).transpose(2, 0, 1, 3)
        pos_b = pos_b.reshape(pairs, 2, 2, head_dim).transpose(0, 2, 1, 3).reshape(pairs, 2, 2 * head_dim)
        pos_b = xor_order(pos_b, head_index)
        att_all = lax.all_gather(lax.all_gather(att_part, "batch", axis=0), "heads", axis=0)
        att_all = xor_order(att_all, head_index)
        tw = att_all[..., :512].reshape(pairs, model_width, 512)
        pos_w = att_all[..., 512:].reshape(pairs, batches, 2, width // 2, 128).transpose(0, 2, 1, 3, 4)
        pos_w = pos_w.reshape(pairs, model_width, 128)
        halves_in = column_chunks(rows_of(conv_in))
        conv_in_w = [halves_in[0], halves_in[1]]
        middle_w = [
            column_chunks(rows_of(ffn2_in)),
            rows_of(ffn2_out).reshape(4, 512, model_width),
            rows_of(conv_out),
        ]

    if not fast:
        x1, n1 = ffn1_forward(frames_in, win, wout, small_t)
    across = swap(n1, "heads", 2)
    keys = [n1, swap(n1, "heads", 1), across, swap(across, "heads", 1)]
    weights, mixed, scale, kv, queries, after_att, n2 = att_forward(
        key_mask, keys, x1, small_t, tw, pos_w, pos_b, own_turn, table_t
    )
    glu, gated, conv_in_w = gate_forward(ints, n2, conv_in_w)
    rim = halo(glu)
    depth, sums = conv_forward(ints, glu, rim, small_t)
    sums = sum_over(sum_over(sums, "heads"), "batch")
    layer_out, upstream, raw, gsum, mid_rows, pre, act, dhid, branch, swish, low = middle(
        ints, floats, depth, sums, after_att, cotangent, small_t, middle_w
    )

    gsum = sum_over(gsum, "heads")
    pre = behind(pre, gsum)
    gsum = sum_over(gsum, "batch")
    mid_grads = middle_grads(fast, pre, act, dhid, branch, swish, low)
    positions = head_index * row_count + jnp.arange(row_count, dtype=jnp.int32)
    row_valid = (positions < own_length).astype(F32)[:, None]
    mean_bn = sums[0] / total_valid
    grad_first = (gsum[0] - 2.0 * mean_bn * gsum[1]) / total_valid
    grad_second = gsum[1] / total_valid
    raw = behind(raw, *mid_grads)
    depth_low = (raw + row_valid * (grad_first + 2.0 * depth * grad_second)).astype(BF)
    depth_rim = halo(depth_low)
    if fast:
        mid = lax.psum_scatter(mid_grads[0].reshape(32 * 144, 512), BOTH, scatter_dimension=0, tiled=True)
    upstream, dgated, conv_rows = conv_backward(
        ints, glu, rim, depth_low, depth_rim, small_t, gated, conv_in_w, after_att, upstream
    )
    near, far, home, grad_bias, *att_grads = att_backward(
        fast, upstream, n2, dgated, keys, mixed, scale, weights, kv, queries, tw, pos_w, own_turn, table
    )
    near = swap(near, "heads", 1)
    moving = (far.astype(F32) + near[1].astype(F32)).astype(BF)
    far = swap(moving, "heads", 2)
    grad_bias = xor_order(grad_bias, head_index).reshape(pairs, 2, 2, head_dim).transpose(0, 2, 1, 3)
    grad_bias = grad_bias.reshape(pairs, 2, batches, channels).transpose(1, 2, 0, 3).reshape(2, model_width)
    if fast:
        heard = swap(behind(att_grads[1], near), "heads", 1)
        home = behind(home, heard)
        t = Exchange(att_grads[0], behind(heard, moving), steps_attention())
        send_all([t], keep=True)
    again = ffn1_again(frames_in, x1, win, wout, small_t, home, near)
    frames_grad, *first_grads = ffn1_backward(
        fast, again, upstream, far, small_t, conv_rows, mid_rows, grad_bias
    )

    if fast:
        *first_grads, t.terms[-1] = lax.optimization_barrier((*first_grads, t.terms[-1]))
        own_ffn2_a, own_ffn2_b, own_conv_b = finish_middle(mid)
        a_far, a_own, b_far, b_own = first_grads
        a = Exchange(a_own, swap(a_far, "heads", 1), steps_first("xy"))
        b = Exchange(b_own, swap(b_far, "heads", 1), steps_first("yx"))
        t.terms[-1] = behind(t.terms[-1], mid)
        send_all((a, b, t))
        send_all((a, b, t))
        moving = send_all((a, b))
        t.terms[-1] = behind(t.terms[-1], *moving)
        send_all([t])
        send_all((a, b))
        own_proj, own_out, own_conv_a = finish_attention(t.terms)
        own_ffn1_a, own_ffn1_b, own_taps, own_gain, own_bias, own_pos = finish_first(a.terms, b.terms)
    else:

        def to_rows(chunks):
            rows = chunks.shape[1]
            return sum_rows(chunks.transpose(1, 0, 2).reshape(rows, -1))

        own_ffn2_a = to_rows(mid_grads[0])
        own_ffn2_b = sum_rows(mid_grads[1].reshape(-1, model_width))
        own_conv_b = sum_rows(mid_grads[2])
        tw_grad, pos_grad, conv_grad = att_grads
        own_conv_a = sum_rows(conv_grad)
        pos_grad = pos_grad.reshape(pairs, 2, batches, width // 2, 128).transpose(0, 2, 1, 3, 4)
        grad_att = jnp.concatenate([tw_grad, pos_grad.reshape(pairs, model_width, 128)], axis=2)
        grad_att = xor_order(grad_att, head_index).astype(F32)
        own_att = lax.psum_scatter(
            lax.psum_scatter(grad_att, "batch", scatter_dimension=1, tiled=True),
            "heads",
            scatter_dimension=0,
            tiled=True,
        )[0]
        own_ffn1_a, own_ffn1_b = to_rows(first_grads[0]), sum_rows(first_grads[1])
        own_small = sum_rows(first_grads[2])
        own_small = own_small.T
        turned = own_att[:, 512:640].reshape(2, width // 2, 128).transpose(1, 0, 2).reshape(width, 128)
        parts = jnp.stack([own_att[:, :128], own_att[:, 128:256], own_att[:, 256:384], turned], axis=1)
        own_proj = parts.reshape(width, 4, 2, head_dim).transpose(2, 0, 1, 3)
        own_proj = own_proj.reshape(2, width, 4 * head_dim)
        own_out = own_att[:, 384:512].T.reshape(2, head_dim, width)
        own_pos = own_small[POS_BIAS : POS_BIAS + 2]
        own_taps = own_small[:kernel_len]
        own_gain, own_bias = own_small[GAIN : GAIN + 6], own_small[BIAS : BIAS + 6]
    return (
        layer_out,
        frames_grad,
        own_ffn1_a,
        own_ffn1_b,
        own_proj,
        own_out,
        own_pos,
        own_conv_a,
        own_taps,
        own_conv_b,
        own_ffn2_a,
        own_ffn2_b,
        own_gain,
        own_bias,
    )


def solution(mesh):
    placed = (
        P(("batch", "heads"), None),
        P(("batch", "heads"), None),
        P(),
        P(),
        P(("batch", "heads"), None),
        P(("batch", "heads"), None),
        P("heads", "batch", None),
        P("heads", None, "batch"),
        P("heads", "batch"),
        P(("batch", "heads"), None),
        P(None, ("batch", "heads")),
        P(("batch", "heads"), None),
        P(("batch", "heads"), None),
        P(("batch", "heads"), None),
        P(None, ("batch", "heads")),
        P(None, ("batch", "heads")),
    )
    return jax.shard_map(
        local,
        mesh=mesh,
        in_specs=placed,
        out_specs=(
            P(("batch", "heads"), None),
            P(("batch", "heads"), None),
            P(("batch", "heads"), None),
            P(("batch", "heads"), None),
            P("heads", "batch", None),
            P("heads", None, "batch"),
            P("heads", "batch"),
            P(("batch", "heads"), None),
            P(None, ("batch", "heads")),
            P(("batch", "heads"), None),
            P(("batch", "heads"), None),
            P(("batch", "heads"), None),
            P(None, ("batch", "heads")),
            P(None, ("batch", "heads")),
        ),
        check_vma=False,
    )
```
